32 devices in a mesh: gx: 8 (over z, x), gy: 2 (over y), gz: 2 (over core).
Axes of the slice: x: 2, y: 2, z: 4, core: 2. Of those that a mesh axis runs over, the one named last changes fastest.
Arguments:
- basis: float32 [32768, 256], P(('gx', 'gy', 'gz'))
- target: float32 [32768, 256], P(('gx', 'gy', 'gz'))
Outputs:
- tangent: float32 [32768, 256], P(('gx', 'gy', 'gz'))
All inputs are finite; a program needn't handle non-finite values.
Results may differ from the reference program's by a relative error of at most 0.0013.
Values sent between devices are 32-bit elements; how exact they have to be, the bound alone decides.
No kernel may reach another device: no remote copies, remote signals or barrier semaphores. Data moves between devices by JAX's collectives and lax.ppermute only.
A program may use at most 64 MiB of HBM per device.

```python
import math
import jax
import jax.numpy as jnp
import numpy as np
from jax import lax

MODES = 256
ROWS = 32768


def shared_basis(key):
    normed = jnp.clip(jax.random.normal(key, (ROWS, MODES), jnp.float32), -6.0, 6.0)
    places = jnp.arange(ROWS, dtype=jnp.float32) / ROWS
    norm_const = 99.0 / (2.0 * math.log(10.0))
    scale = jnp.exp(math.log(10.0) * places) / jnp.sqrt(jnp.float32(ROWS) * norm_const)
    return (normed * scale[:, None], scale)


def draw_basis(key, part):
    values, scale = shared_basis(key)
    return values


def draw_target(key, part):
    values, scale = shared_basis(key)
    key = jax.random.fold_in(key, 7)
    first, second, third = jax.random.split(key, 3)
    diag_part = jnp.exp(jax.random.uniform(first, (MODES,), jnp.float32, math.log(0.5), math.log(2.0)))
    column_amp = jnp.exp(jax.random.uniform(second, (MODES,), jnp.float32, math.log(0.3), math.log(3.0)))
    noise = jnp.clip(jax.random.normal(third, (ROWS, MODES), jnp.float32), -6.0, 6.0)
    mixed = (values + 0.4 * jnp.roll(values, -1, axis=1)) * diag_part[None, :]
    extra = (noise + 0.6 * jnp.roll(noise, -1, axis=1)) * column_amp[None, :] * scale[:, None]
    return mixed + extra


def setup_inputs(seed: int = 0) -> dict:
    keys = jax.random.split(jax.random.key(seed), 3)
    basis = draw_basis(jax.random.fold_in(keys[2], 71), 0)
    target = draw_target(jax.random.fold_in(keys[2], 71), 0)
    return {"basis": basis, "target": target}


highest = lax.Precision.HIGHEST
half_points = [0.0950125098376374, 0.2816035507792589, 0.4580167776572274, 0.6178762444026438, 0.755404408355003, 0.8656312023878318, 0.9445750230732326, 0.9894009349916499]
half_weights = [0.1894506104550685, 0.1826034150449236, 0.1691565193950025, 0.1495959888165767, 0.1246289712555339, 0.0951585116824928, 0.0622535239386479, 0.0271524594117541]

def legendre_rule():
    points = np.array([-v for v in half_points[::-1]] + half_points)
    weights = np.array(half_weights[::-1] + half_weights)
    positions = jnp.asarray((points + 1.0) / 2.0, dtype=jnp.float32)
    node_wts = jnp.asarray(weights / 2.0, dtype=jnp.float32)
    return (positions, node_wts)

def matmul(left, right):
    return jnp.dot(left.astype(jnp.float32), right.astype(jnp.float32), precision=highest, preferred_element_type=jnp.float32)

def tmatmul(left, right):
    return lax.dot_general(left.astype(jnp.float32), right.astype(jnp.float32), (((0,), (0,)), ((), ())), precision=highest, preferred_element_type=jnp.float32)

def inverse_of(square):
    chol = jnp.linalg.cholesky(tmatmul(square, square))
    return jax.scipy.linalg.cho_solve((chol, True), square.T)

def reference(basis, target):
    positions, node_wts = legendre_rule()
    cross = tmatmul(basis, target)
    inverse = inverse_of(cross)
    lifted = matmul(target - matmul(basis, cross), inverse)
    gram = tmatmul(lifted, lifted)
    identity = jnp.eye(MODES, dtype=jnp.float32)

    def resolvent(place):
        chol = jnp.linalg.cholesky(identity + place * place * gram)
        return jax.scipy.linalg.cho_solve((chol, True), identity)
    angles = lax.optimization_barrier(jnp.sum(node_wts[:, None, None] * jax.vmap(resolvent)(positions), axis=0))
    return matmul(lifted, angles) * jnp.sqrt(jnp.float32(ROWS))
```

```python
import functools

import jax
import jax.numpy as jnp
import numpy as np
from jax import lax
from jax.experimental import pallas as pl
from jax.experimental.pallas import tpu as pltpu
from jax.sharding import PartitionSpec as P

half_points = [
    0.0950125098376374,
    0.2816035507792589,
    0.4580167776572274,
    0.6178762444026438,
    0.755404408355003,
    0.8656312023878318,
    0.9445750230732326,
    0.9894009349916499,
]
half_weights = [
    0.1894506104550685,
    0.1826034150449236,
    0.1691565193950025,
    0.1495959888165767,
    0.1246289712555339,
    0.0951585116824928,
    0.0622535239386479,
    0.0271524594117541,
]
points = (np.array([-v for v in half_points[::-1]] + half_points) + 1.0) / 2.0
weights = np.array(half_weights[::-1] + half_weights) / 2.0
NODES = 16
STEP = 32
F32 = jnp.float32
BF16 = jnp.bfloat16
highest = lax.Precision.HIGHEST


def iota(shape, dim):
    return lax.broadcasted_iota(jnp.int32, shape, dim)


def split(x):
    high = x.astype(BF16).astype(F32)
    rest = x - high
    mid = rest.astype(BF16).astype(F32)
    return high, mid, rest - mid


def dot(a, b):
    return jnp.dot(a, b, precision=highest, preferred_element_type=F32)


def tdot(a, b):
    return lax.dot_general(
        a, b, (((0,), (0,)), ((), ())), precision=highest, preferred_element_type=F32
    )


def gram_kernel(b_ref, t_ref, out_ref):
    n = b_ref.shape[1]
    b, t = b_ref[...], t_ref[...]
    bt, tt = b.T, t.T
    out_ref[0:n, :] = dot(bt, t)
    tgram = dot(tt, t)
    bgram = dot(bt, b)
    row, col = iota((n, n), 0), iota((n, n), 1)
    out_ref[n : 2 * n, :] = jnp.where(row < col, tgram, bgram)
    diag = row == col
    tdiag = jnp.sum(jnp.where(diag, tgram, 0.0), axis=0, keepdims=True)
    bdiag = jnp.sum(jnp.where(diag, bgram, 0.0), axis=0, keepdims=True)
    out_ref[2 * n :, :] = jnp.concatenate([tdiag, bdiag, jnp.zeros((14, n), F32)], 0)


def invert_blocks(v):
    lane = iota((8, 128), 1)
    row = iota((8, 128), 0)
    for q in range(4):
        pan = []
        for p in range(8):
            index = lane % NODES + p * NODES
            pan.append([jnp.take_along_axis(v[q][g], index, axis=1) for g in range(4)])
        for p in range(8):
            recip = 1.0 / pan[p][q][p : p + 1, :]
            new = [x for x in pan[p]]
            new[q] = jnp.where(row == p, 1.0, new[q])
            new = [x * recip for x in new]
            pan[p] = new
            for o in range(8):
                if o != p:
                    factor = pan[o][q][p : p + 1, :]
                    old = [x for x in pan[o]]
                    old[q] = jnp.where(row == p, 0.0, old[q])
                    pan[o] = [x - factor * y for x, y in zip(old, new)]
        for o in range(4):
            if o != q:
                acc = [x for x in v[o]]
                acc[q] = jnp.zeros((8, 128), F32)
                for p in range(8):
                    factor = v[o][q][p : p + 1, :]
                    acc = [x - factor * y for x, y in zip(acc, pan[p])]
                v[o] = acc
        mine = pan[0]
        for p in range(1, 8):
            mine = [jnp.where(lane // NODES == p, y, x) for x, y in zip(mine, pan[p])]
        v[q] = mine
    return v


def lift_kernel(pay_ref, b_ref, t_ref, out_ref, mats, turned, inverses):
    n = b_ref.shape[1]
    row, col = iota((n, n), 0), iota((n, n), 1)
    cross = pay_ref[0:n, :]
    packed = pay_ref[n : 2 * n, :]
    tdiag = pay_ref[2 * n : 2 * n + 1, :]
    bdiag = pay_ref[2 * n + 1 : 2 * n + 2, :]
    upper = jnp.where(row < col, packed, 0.0)
    lower = jnp.where(row > col, packed, 0.0)
    tgram = upper + upper.T + jnp.where(row == col, tdiag, 0.0)
    bgram = lower + lower.T + jnp.where(row == col, bdiag, 0.0)
    crosst = cross.T
    square = dot(crosst, cross)
    normal = tgram - 2.0 * square + dot(crosst, dot(bgram, cross))
    for m in range(NODES):
        shifted = square + float(points[m] ** 2) * normal
        mats[0, m * n : (m + 1) * n, :] = shifted[:, 0:128]
        mats[1, m * n : (m + 1) * n, :] = shifted[:, 128:256]

    out_ref[...] = t_ref[...] - dot(b_ref[...], cross)

    def step(kb, carry):
        start = pl.multiple_of(kb * STEP, STEP)
        tile = kb // 4
        inner = pl.multiple_of(kb % 4 * STEP, STEP)
        v = []
        for q in range(4):
            rows = [mats[tile, pl.ds(start + 8 * q + i, NODES, stride=n), :] for i in range(8)]
            turned[q] = jnp.concatenate(rows, 0).T
            block = turned[q, pl.ds(inner, STEP), :]
            v.append([block[8 * g : 8 * g + 8] for g in range(4)])
        v = invert_blocks(v)
        for q in range(4):
            h, m, l = split(jnp.concatenate(v[q], 0))
            inverses[0, q * 128 : (q + 1) * 128, :] = jnp.concatenate([h, h, m, h], 0).T
            inverses[1, q * 128 : (q + 1) * 128, :] = jnp.concatenate([l, m, m, l], 0).T

        group = iota((n, 128), 1) // STEP
        index = iota((n, 128), 1) % STEP + inner
        local = iota((STEP, n), 1) - start
        inblock = (local >= 0) & (local < STEP)
        minus = jnp.where(local == iota((STEP, n), 0), -1.0, 0.0)

        def stack(x):
            h, m, l = split(x)
            return jnp.concatenate([h, m, h, l, h, m, l, m], 0).astype(BF16)

        def update(m, carry):
            base = pl.multiple_of(m * n, n)
            here = pl.ds(pl.multiple_of(base + start, STEP), STEP)
            left = [inverses[c, pl.ds(m, STEP, stride=NODES), :] for c in range(2)]
            left = jnp.concatenate(left, 1).astype(BF16)
            panel = jnp.concatenate([mats[0, here, :], mats[1, here, :]], 1)
            panel = jnp.where(inblock, minus, panel)
            new = jnp.dot(left, stack(panel), preferred_element_type=F32)
            columns = jnp.take_along_axis(mats[tile, pl.ds(base, n), :], index, axis=1)
            h, d, l = split(columns)
            one = jnp.where(group == 2, d, h)
            two = jnp.where((group == 0) | (group == 3), l, d)
            lhs = jnp.concatenate([one, two], 1).astype(BF16)
            change = jnp.dot(lhs, stack(new), preferred_element_type=F32)
            for c in range(2):
                part = slice(c * 128, (c + 1) * 128)
                old = jnp.where(inblock[0:1, part], 0.0, mats[c, pl.ds(base, n), :])
                mats[c, pl.ds(base, n), :] = old - change[:, part]
                mats[c, here, :] = new[:, part]
            return carry

        lax.fori_loop(0, NODES, update, 0)
        return carry

    lax.fori_loop(0, n // STEP, step, 0)
    halves = []
    for c in range(2):
        half = float(weights[0]) * mats[c, 0:n, :]
        for m in range(1, NODES):
            half = half + float(weights[m]) * mats[c, m * n : (m + 1) * n, :]
        halves.append(half)
    total = jnp.concatenate(halves, 1)
    out_ref[...] = dot(out_ref[...], dot(total, crosst))


def reduced(x, mesh):
    sizes = dict(mesh.shape)
    if any(s & (s - 1) for s in sizes.values()) or sizes["gz"] != 2:
        return lax.psum(x, ("gx", "gy", "gz"))
    me = lax.axis_index("gz")
    half = x.shape[0] // 2
    mine = lax.dynamic_slice_in_dim(x, me * half, half, 0)
    other = lax.dynamic_slice_in_dim(x, (1 - me) * half, half, 0)
    mine = mine + lax.ppermute(other, "gz", [(0, 1), (1, 0)])
    for axis in ("gy", "gx"):
        bit = 1
        while bit < sizes[axis]:
            mine = mine + lax.ppermute(mine, axis, [(i, i ^ bit) for i in range(sizes[axis])])
            bit *= 2
    other = lax.ppermute(mine, "gz", [(0, 1), (1, 0)])
    return jnp.where(me == 0, jnp.concatenate([mine, other], 0), jnp.concatenate([other, mine], 0))


def on_device(basis, target, mesh):
    rows, n = basis.shape
    total_rows = rows * mesh.size
    vmem = pl.BlockSpec(memory_space=pltpu.VMEM)
    limit = pltpu.CompilerParams(vmem_limit_bytes=48 * 1024 * 1024)
    pay = pl.pallas_call(
        gram_kernel,
        out_shape=jax.ShapeDtypeStruct((2 * n + 16, n), F32),
        in_specs=[vmem, vmem],
        out_specs=vmem,
        compiler_params=limit,
    )(basis, target)
    pay = reduced(pay, mesh)
    return pl.pallas_call(
        functools.partial(lift_kernel_scaled, float(np.sqrt(total_rows))),
        out_shape=jax.ShapeDtypeStruct((rows, n), F32),
        in_specs=[vmem, vmem, vmem],
        out_specs=vmem,
        scratch_shapes=[
            pltpu.VMEM((2, NODES * n, 128), F32),
            pltpu.VMEM((4, 128, 128), F32),
            pltpu.VMEM((2, 4 * 128, 128), F32),
        ],
        compiler_params=limit,
    )(pay, basis, target)


def lift_kernel_scaled(scale, *refs):
    lift_kernel(*refs)
    out_ref = refs[3]
    out_ref[...] = out_ref[...] * (-scale)


def solution(mesh):
    return jax.shard_map(
        functools.partial(on_device, mesh=mesh),
        mesh=mesh,
        in_specs=(P(("gx", "gy", "gz"), None), P(("gx", "gy", "gz"), None)),
        out_specs=P(("gx", "gy", "gz"), None),
        check_vma=False,
    )
```

```python
import functools

import jax
import jax.numpy as jnp
import numpy as np
from jax import lax
from jax.experimental import pallas as pl
from jax.experimental.pallas import tpu as pltpu
from jax.sharding import PartitionSpec as P

half_points = [
    0.0950125098376374,
    0.2816035507792589,
    0.4580167776572274,
    0.6178762444026438,
    0.755404408355003,
    0.8656312023878318,
    0.9445750230732326,
    0.9894009349916499,
]
half_weights = [
    0.1894506104550685,
    0.1826034150449236,
    0.1691565193950025,
    0.1495959888165767,
    0.1246289712555339,
    0.0951585116824928,
    0.0622535239386479,
    0.0271524594117541,
]
points = (np.array([-v for v in half_points[::-1]] + half_points) + 1.0) / 2.0
weights = np.array(half_weights[::-1] + half_weights) / 2.0
NODES = 8
STEP = 32
F32 = jnp.float32
BF16 = jnp.bfloat16
highest = lax.Precision.HIGHEST


def iota(shape, dim):
    return lax.broadcasted_iota(jnp.int32, shape, dim)


def split(x):
    high = x.astype(BF16).astype(F32)
    rest = x - high
    mid = rest.astype(BF16).astype(F32)
    return high, mid, rest - mid


def dot(a, b):
    return jnp.dot(a, b, precision=highest, preferred_element_type=F32)


def tdot(a, b):
    return lax.dot_general(
        a, b, (((0,), (0,)), ((), ())), precision=highest, preferred_element_type=F32
    )


def gram_kernel(b_ref, t_ref, out_ref):
    n = b_ref.shape[1]
    b, t = b_ref[...], t_ref[...]
    bt, tt = b.T, t.T
    out_ref[0:n, :] = dot(bt, t)
    tgram = dot(tt, t)
    bgram = dot(bt, b)
    row, col = iota((n, n), 0), iota((n, n), 1)
    out_ref[n : 2 * n, :] = jnp.where(row < col, tgram, bgram)
    diag = row == col
    tdiag = jnp.sum(jnp.where(diag, tgram, 0.0), axis=0, keepdims=True)
    bdiag = jnp.sum(jnp.where(diag, bgram, 0.0), axis=0, keepdims=True)
    out_ref[2 * n :, :] = jnp.concatenate([tdiag, bdiag, jnp.zeros((14, n), F32)], 0)


def invert_blocks(v):
    group = iota((8, 128), 1) // NODES
    node = iota((8, 128), 1) % NODES
    row = iota((8, 128), 0)
    for g in range(4):
        q, first = g // 2, g % 2 * 8
        pan = []
        for p in range(8):
            index = node + (first + p) * NODES
            pan.append([jnp.take_along_axis(x, index, axis=1) for x in v[q]])
        for p in range(8):
            recip = 1.0 / pan[p][g][p : p + 1, :]
            new = [x for x in pan[p]]
            new[g] = jnp.where(row == p, 1.0, new[g])
            new = [x * recip for x in new]
            pan[p] = new
            for o in range(8):
                if o != p:
                    factor = pan[o][g][p : p + 1, :]
                    old = [x for x in pan[o]]
                    old[g] = jnp.where(row == p, 0.0, old[g])
                    pan[o] = [x - factor * y for x, y in zip(old, new)]
        for o in range(2):
            acc = [x for x in v[o]]
            acc[g] = jnp.zeros((8, 128), F32)
            for p in range(8):
                factor = v[o][g][p : p + 1, :]
                acc = [x - factor * y for x, y in zip(acc, pan[p])]
            if o == q:
                for p in range(8):
                    acc = [jnp.where(group == first + p, y, x) for x, y in zip(acc, pan[p])]
            v[o] = acc
    return v


def resolvent_kernel(shift_ref, weight_ref, pay_ref, out_ref, mats, turned, inverses, news):
    n = out_ref.shape[1]
    row, col = iota((n, n), 0), iota((n, n), 1)
    cross = pay_ref[0:n, :]
    packed = pay_ref[n : 2 * n, :]
    tdiag = pay_ref[2 * n : 2 * n + 1, :]
    bdiag = pay_ref[2 * n + 1 : 2 * n + 2, :]
    upper = jnp.where(row < col, packed, 0.0)
    lower = jnp.where(row > col, packed, 0.0)
    tgram = upper + upper.T + jnp.where(row == col, tdiag, 0.0)
    bgram = lower + lower.T + jnp.where(row == col, bdiag, 0.0)
    crosst = cross.T
    square = dot(crosst, cross)
    normal = tgram - 2.0 * square + dot(crosst, dot(bgram, cross))
    for m in range(NODES):
        shifted = square + shift_ref[m] * normal
        mats[0, m * n : (m + 1) * n, :] = shifted[:, 0:128]
        mats[1, m * n : (m + 1) * n, :] = shifted[:, 128:256]

    def stack(x):
        h, m, l = split(x)
        return jnp.concatenate([h, m, h, l, h, m, l, m], 0).astype(BF16)

    def step(tile, part, carry):
        inner = pl.multiple_of(part * STEP, STEP)
        start = pl.multiple_of(tile * 128 + inner, STEP)
        v = []
        for q in range(2):
            rows = [mats[tile, pl.ds(start + 16 * q + i, NODES, stride=n), :] for i in range(16)]
            turned[q] = jnp.concatenate(rows, 0).T
            block = turned[q, pl.ds(inner, STEP), :]
            v.append([block[8 * g : 8 * g + 8] for g in range(4)])
        v = invert_blocks(v)
        for q in range(2):
            h, m, l = split(jnp.concatenate(v[q], 0))
            inverses[0, q * 128 : (q + 1) * 128, :] = jnp.concatenate([h, h, m, h], 0).T
            inverses[1, q * 128 : (q + 1) * 128, :] = jnp.concatenate([l, m, m, l], 0).T

        group = iota((n, 128), 1) // STEP
        index = iota((n, 128), 1) % STEP + inner
        local = iota((STEP, n), 1) - start
        inblock = (local >= 0) & (local < STEP)
        minus = jnp.where(local == iota((STEP, n), 0), -1.0, 0.0)
        for m in range(NODES):
            left = [inverses[c, pl.ds(m, STEP, stride=NODES), :] for c in range(2)]
            left = jnp.concatenate(left, 1).astype(BF16)
            here = pl.ds(pl.multiple_of(m * n + start, STEP), STEP)
            panel = jnp.concatenate([mats[0, here, :], mats[1, here, :]], 1)
            panel = jnp.where(inblock, minus, panel)
            news[m] = jnp.dot(left, stack(panel), preferred_element_type=F32)
        for m in range(NODES):
            rows = slice(m * n, (m + 1) * n)
            columns = jnp.take_along_axis(mats[tile, rows, :], index, axis=1)
            h, d, l = split(columns)
            one = jnp.where(group == 2, d, h)
            two = jnp.where((group == 0) | (group == 3), l, d)
            lhs = jnp.concatenate([one, two], 1).astype(BF16)
            change = jnp.dot(lhs, stack(news[m]), preferred_element_type=F32)
            for c in range(2):
                half = slice(c * 128, (c + 1) * 128)
                old = mats[c, rows, :]
                if c == tile:
                    old = jnp.where(inblock[0:1, half], 0.0, old)
                mats[c, rows, :] = old - change[:, half]
        for m in range(NODES):
            here = pl.ds(pl.multiple_of(m * n + start, STEP), STEP)
            mats[0, here, :] = news[m, :, 0:128]
            mats[1, here, :] = news[m, :, 128:256]
        return carry

    for tile in range(2):
        lax.fori_loop(0, 4, functools.partial(step, tile), 0)
    for c in range(2):
        half = weight_ref[0] * mats[c, 0:n, :]
        for m in range(1, NODES):
            half = half + weight_ref[m] * mats[c, m * n : (m + 1) * n, :]
        out_ref[:, c * 128 : (c + 1) * 128] = half


def residual_kernel(pay_ref, b_ref, t_ref, out_ref):
    n = b_ref.shape[1]
    out_ref[...] = t_ref[...] - dot(b_ref[...], pay_ref[0:n, :])


def lift_kernel(scale, mine_ref, other_ref, pay_ref, z_ref, out_ref):
    n = out_ref.shape[1]
    total = (mine_ref[...] + other_ref[...]) * -scale
    out_ref[...] = dot(z_ref[...], dot(total, pay_ref[0:n, :].T))


def reduced(x, mesh):
    sizes = dict(mesh.shape)
    if any(s & (s - 1) for s in sizes.values()) or sizes["gz"] != 2:
        return lax.psum(x, ("gx", "gy", "gz"))
    me = lax.axis_index("gz")
    half = x.shape[0] // 2
    mine = lax.dynamic_slice_in_dim(x, me * half, half, 0)
    other = lax.dynamic_slice_in_dim(x, (1 - me) * half, half, 0)
    mine = mine + lax.ppermute(other, "gz", [(0, 1), (1, 0)])
    for axis in ("gy", "gx"):
        bit = 1
        while bit < sizes[axis]:
            mine = mine + lax.ppermute(mine, axis, [(i, i ^ bit) for i in range(sizes[axis])])
            bit *= 2
    other = lax.ppermute(mine, "gz", [(0, 1), (1, 0)])
    return jnp.where(me == 0, jnp.concatenate([mine, other], 0), jnp.concatenate([other, mine], 0))


def on_device(basis, target, mesh):
    rows, n = basis.shape
    total_rows = rows * mesh.size
    vmem = pl.BlockSpec(memory_space=pltpu.VMEM)
    smem = pl.BlockSpec(memory_space=pltpu.SMEM)
    limit = pltpu.CompilerParams(vmem_limit_bytes=48 * 1024 * 1024)
    pay = pl.pallas_call(
        gram_kernel,
        out_shape=jax.ShapeDtypeStruct((2 * n + 16, n), F32),
        in_specs=[vmem, vmem],
        out_specs=vmem,
        compiler_params=limit,
    )(basis, target)
    pay = reduced(pay, mesh)
    first = lax.axis_index("gz") * NODES
    shifts = lax.dynamic_slice_in_dim(jnp.asarray(points**2, F32), first, NODES)
    node_wts = lax.dynamic_slice_in_dim(jnp.asarray(weights, F32), first, NODES)
    mine = pl.pallas_call(
        resolvent_kernel,
        out_shape=jax.ShapeDtypeStruct((n, n), F32),
        in_specs=[smem, smem, vmem],
        out_specs=vmem,
        scratch_shapes=[
            pltpu.VMEM((2, NODES * n, 128), F32),
            pltpu.VMEM((2, 128, 128), F32),
            pltpu.VMEM((2, 2 * 128, 128), F32),
            pltpu.VMEM((NODES, STEP, n), F32),
        ],
        compiler_params=limit,
        cost_estimate=pl.CostEstimate(flops=10**11, bytes_accessed=10**6, transcendentals=0),
    )(shifts, node_wts, pay)
    other = lax.ppermute(mine, "gz", [(0, 1), (1, 0)])
    residual = pl.pallas_call(
        residual_kernel,
        out_shape=jax.ShapeDtypeStruct((rows, n), F32),
        in_specs=[vmem, vmem, vmem],
        out_specs=vmem,
        compiler_params=limit,
        cost_estimate=pl.CostEstimate(flops=10**9, bytes_accessed=3 * 10**6, transcendentals=0),
    )(pay, basis, target)
    return pl.pallas_call(
        functools.partial(lift_kernel, float(np.sqrt(total_rows))),
        out_shape=jax.ShapeDtypeStruct((rows, n), F32),
        in_specs=[vmem] * 4,
        out_specs=vmem,
        compiler_params=limit,
    )(mine, other, pay, residual)


def solution(mesh):
    return jax.shard_map(
        functools.partial(on_device, mesh=mesh),
        mesh=mesh,
        in_specs=(P(("gx", "gy", "gz"), None), P(("gx", "gy", "gz"), None)),
        out_specs=P(("gx", "gy", "gz"), None),
        check_vma=False,
    )
```

```python
import functools

import jax
import jax.numpy as jnp
import numpy as np
from jax import lax
from jax.experimental import pallas as pl
from jax.experimental.pallas import tpu as pltpu
from jax.sharding import PartitionSpec as P

half_points = [
    0.0950125098376374,
    0.2816035507792589,
    0.4580167776572274,
    0.6178762444026438,
    0.755404408355003,
    0.8656312023878318,
    0.9445750230732326,
    0.9894009349916499,
]
half_weights = [
    0.1894506104550685,
    0.1826034150449236,
    0.1691565193950025,
    0.1495959888165767,
    0.1246289712555339,
    0.0951585116824928,
    0.0622535239386479,
    0.0271524594117541,
]
points = (np.array([-v for v in half_points[::-1]] + half_points) + 1.0) / 2.0
weights = np.array(half_weights[::-1] + half_weights) / 2.0
NODES = 8
CHUNKS = 4
CUBE = 8
PIECE = 72
HALF = CUBE * PIECE
PAY_ROWS = 2 * HALF
STEP = 32
F32 = jnp.float32
BF16 = jnp.bfloat16
highest = lax.Precision.HIGHEST


def iota(shape, dim):
    return lax.broadcasted_iota(jnp.int32, shape, dim)


def split(x):
    high = x.astype(BF16).astype(F32)
    rest = x - high
    mid = rest.astype(BF16).astype(F32)
    return high, mid, rest - mid


def dot(a, b):
    return jnp.dot(a, b, precision=highest, preferred_element_type=F32)


def halves(x):
    high = x.astype(BF16)
    return high, (x - high.astype(F32)).astype(BF16)


def dot3(a, b):
    (ah, al), (bh, bl) = a, b
    total = jnp.dot(ah, bl, preferred_element_type=F32) + jnp.dot(al, bh, preferred_element_type=F32)
    return total + jnp.dot(ah, bh, preferred_element_type=F32)


def gram_kernel(where_ref, b_hbm, t_hbm, keep_ref, send_ref, b_ref, t_ref, pay, sems):
    rows, n = b_ref.shape
    chunk = rows // CHUNKS
    copies = []
    for c in range(CHUNKS):
        part = pl.ds(c * chunk, chunk)
        for k, (source, dest) in enumerate(((b_hbm, b_ref), (t_hbm, t_ref))):
            copy = pltpu.make_async_copy(source.at[part], dest.at[part], sems.at[k, c])
            copy.start()
            copies.append(copy)
    cross = tgram = bgram = jnp.zeros((n, n), F32)
    for c in range(CHUNKS):
        part = slice(c * chunk, (c + 1) * chunk)
        copies[2 * c].wait()
        copies[2 * c + 1].wait()
        b, t = b_ref[part, :], t_ref[part, :]
        b, bt, t, tt = halves(b), halves(b.T), halves(t), halves(t.T)
        cross += dot3(bt, t)
        tgram += dot3(tt, t)
        bgram += dot3(bt, b)
    row, col = iota((n, n), 0), iota((n, n), 1)
    packed = jnp.where(row < col, tgram, bgram)
    diag = row == col
    tdiag = jnp.sum(jnp.where(diag, tgram, 0.0), axis=0, keepdims=True)
    bdiag = jnp.sum(jnp.where(diag, bgram, 0.0), axis=0, keepdims=True)
    for c in range(2):
        half = slice(c * 128, (c + 1) * 128)
        pay[c * n : (c + 1) * n, :] = cross[:, half]
        pay[(2 + c) * n : (3 + c) * n, :] = packed[:, half]
    pay[4 * n :, :] = jnp.zeros((PAY_ROWS - 4 * n, 128), F32)
    for c in range(2):
        half = slice(c * 128, (c + 1) * 128)
        pay[4 * n + c : 4 * n + c + 1, :] = tdiag[:, half]
        pay[4 * n + 2 + c : 4 * n + 3 + c, :] = bdiag[:, half]
    core = where_ref[0]
    keep_ref[...] = pay[pl.ds(pl.multiple_of(core * HALF, 8), HALF), :]
    send_ref[...] = pay[pl.ds(pl.multiple_of((1 - core) * HALF, 8), HALF), :]


def scatter_kernel(where_ref, keep_ref, got_ref, *out_refs):
    for mask, out_ref in enumerate(out_refs):
        rows = pl.ds(pl.multiple_of((where_ref[1] ^ mask) * PIECE, 8), PIECE)
        out_ref[...] = keep_ref[rows, :] + got_ref[rows, :]


def sum_kernel(*refs):
    total = refs[0][...]
    for ref in refs[1:-1]:
        total = total + ref[...]
    refs[-1][...] = total


def gather_kernel(where_ref, *refs):
    for mask, ref in enumerate(refs[:-1]):
        rows = pl.ds(pl.multiple_of((where_ref[1] ^ mask) * PIECE, 8), PIECE)
        refs[-1][rows, :] = ref[...]


def invert_blocks(v):
    group = iota((8, 128), 1) // NODES
    node = iota((8, 128), 1) % NODES
    row = iota((8, 128), 0)
    for g in range(4):
        q, first = g // 2, g % 2 * 8
        pan = []
        for p in range(8):
            index = node + (first + p) * NODES
            pan.append([jnp.take_along_axis(x, index, axis=1) for x in v[q]])
        for p in range(8):
            recip = 1.0 / pan[p][g][p : p + 1, :]
            new = [x for x in pan[p]]
            new[g] = jnp.where(row == p, 1.0, new[g])
            new = [x * recip for x in new]
            pan[p] = new
            for o in range(8):
                if o != p:
                    factor = pan[o][g][p : p + 1, :]
                    old = [x for x in pan[o]]
                    old[g] = jnp.where(row == p, 0.0, old[g])
                    pan[o] = [x - factor * y for x, y in zip(old, new)]
        for o in range(2):
            acc = [x for x in v[o]]
            acc[g] = jnp.zeros((8, 128), F32)
            for p in range(8):
                factor = v[o][g][p : p + 1, :]
                acc = [x - factor * y for x, y in zip(acc, pan[p])]
            if o == q:
                for p in range(8):
                    acc = [jnp.where(group == first + p, y, x) for x, y in zip(acc, pan[p])]
            v[o] = acc
    return v


def resolvent_kernel(
    where_ref, shift_ref, weight_ref, mine_ref, other_ref, out_ref, cross_ref, mats, turned, inverses, news, pay
):
    n = out_ref.shape[1]
    core = where_ref[0]
    pay[pl.ds(pl.multiple_of(core * HALF, 8), HALF), :] = mine_ref[...]
    pay[pl.ds(pl.multiple_of((1 - core) * HALF, 8), HALF), :] = other_ref[...]
    row, col = iota((n, n), 0), iota((n, n), 1)

    def wide(start, rows):
        return jnp.concatenate([pay[start : start + rows, :], pay[start + rows : start + 2 * rows, :]], 1)

    cross, packed = wide(0, n), wide(2 * n, n)
    cross_ref[...] = cross
    tdiag, bdiag = wide(4 * n, 1), wide(4 * n + 2, 1)
    upper = jnp.where(row < col, packed, 0.0)
    lower = jnp.where(row > col, packed, 0.0)
    tgram = upper + upper.T + jnp.where(row == col, tdiag, 0.0)
    bgram = lower + lower.T + jnp.where(row == col, bdiag, 0.0)
    crosst = cross.T
    square = dot(crosst, cross)
    normal = tgram - 2.0 * square + dot(crosst, dot(bgram, cross))
    for m in range(NODES):
        shifted = square + shift_ref[m] * normal
        mats[0, m * n : (m + 1) * n, :] = shifted[:, 0:128]
        mats[1, m * n : (m + 1) * n, :] = shifted[:, 128:256]

    def stack(x):
        h, m, l = split(x)
        return jnp.concatenate([h, m, h, l, h, m, l, m], 0).astype(BF16)

    def step(tile, part, carry):
        inner = pl.multiple_of(part * STEP, STEP)
        start = pl.multiple_of(tile * 128 + inner, STEP)
        v = []
        for q in range(2):
            rows = [mats[tile, pl.ds(start + 16 * q + i, NODES, stride=n), :] for i in range(16)]
            turned[q] = jnp.concatenate(rows, 0).T
            block = turned[q, pl.ds(inner, STEP), :]
            v.append([block[8 * g : 8 * g + 8] for g in range(4)])
        v = invert_blocks(v)
        for q in range(2):
            h, m, l = split(jnp.concatenate(v[q], 0))
            inverses[0, q * 128 : (q + 1) * 128, :] = jnp.concatenate([h, h, m, h], 0).T
            inverses[1, q * 128 : (q + 1) * 128, :] = jnp.concatenate([l, m, m, l], 0).T

        group = iota((n, 128), 1) // STEP
        index = iota((n, 128), 1) % STEP + inner
        local = iota((STEP, n), 1) - start
        inblock = (local >= 0) & (local < STEP)
        minus = jnp.where(local == iota((STEP, n), 0), -1.0, 0.0)
        for m in range(NODES):
            left = [inverses[c, pl.ds(m, STEP, stride=NODES), :] for c in range(2)]
            left = jnp.concatenate(left, 1).astype(BF16)
            here = pl.ds(pl.multiple_of(m * n + start, STEP), STEP)
            panel = jnp.concatenate([mats[0, here, :], mats[1, here, :]], 1)
            panel = jnp.where(inblock, minus, panel)
            news[m] = jnp.dot(left, stack(panel), preferred_element_type=F32)
        for m in range(NODES):
            rows = slice(m * n, (m + 1) * n)
            columns = jnp.take_along_axis(mats[tile, rows, :], index, axis=1)
            h, d, l = split(columns)
            one = jnp.where(group == 2, d, h)
            two = jnp.where((group == 0) | (group == 3), l, d)
            lhs = jnp.concatenate([one, two], 1).astype(BF16)
            change = jnp.dot(lhs, stack(news[m]), preferred_element_type=F32)
            for c in range(2):
                half = slice(c * 128, (c + 1) * 128)
                old = mats[c, rows, :]
                if c == tile:
                    old = jnp.where(inblock[0:1, half], 0.0, old)
                mats[c, rows, :] = old - change[:, half]
        for m in range(NODES):
            here = pl.ds(pl.multiple_of(m * n + start, STEP), STEP)
            mats[0, here, :] = news[m, :, 0:128]
            mats[1, here, :] = news[m, :, 128:256]
        return carry

    for tile in range(2):
        lax.fori_loop(0, 4, functools.partial(step, tile), 0)
    for c in range(2):
        half = weight_ref[0] * mats[c, 0:n, :]
        for m in range(1, NODES):
            half = half + weight_ref[m] * mats[c, m * n : (m + 1) * n, :]
        out_ref[:, c * 128 : (c + 1) * 128] = half


def residual_kernel(cross_ref, b_ref, t_ref, out_ref):
    out_ref[...] = t_ref[...] - dot3(halves(b_ref[...]), halves(cross_ref[...]))


def lift_kernel(scale, mine_ref, other_ref, cross_ref, z_ref, out_ref):
    total = (mine_ref[...] + other_ref[...]) * -scale
    right = halves(dot(total, cross_ref[...].T))
    out_ref[...] = dot3(halves(z_ref[...]), right)


AXES = ("gx", "gy", "gz")


def exchange(x, mesh, gx=0, gy=0, gz=0):
    ny, nz = mesh.shape["gy"], mesh.shape["gz"]
    perm = []
    for i in range(mesh.size):
        x0, y0, z0 = i // (ny * nz), i // nz % ny, i % nz
        perm.append((i, ((x0 ^ gx) * ny + (y0 ^ gy)) * nz + (z0 ^ gz)))
    return lax.ppermute(x, AXES, perm)


def on_device(basis, target, mesh):
    rows, n = basis.shape
    total_rows = rows * mesh.size
    vmem = pl.BlockSpec(memory_space=pltpu.VMEM)
    smem = pl.BlockSpec(memory_space=pltpu.SMEM)
    hbm = pl.BlockSpec(memory_space=pltpu.HBM)
    limit = pltpu.CompilerParams(vmem_limit_bytes=48 * 1024 * 1024)
    core, gx, gy = lax.axis_index("gz"), lax.axis_index("gx"), lax.axis_index("gy")
    where = jnp.stack([core, (gx & 3) + 4 * (gy & 1)]).astype(jnp.int32)
    half = jax.ShapeDtypeStruct((HALF, 128), F32)
    piece = jax.ShapeDtypeStruct((PIECE, 128), F32)
    keep, send = pl.pallas_call(
        gram_kernel,
        out_shape=(half, half),
        in_specs=[smem, hbm, hbm],
        out_specs=(vmem, vmem),
        scratch_shapes=[
            pltpu.VMEM((rows, n), F32),
            pltpu.VMEM((rows, n), F32),
            pltpu.VMEM((PAY_ROWS, 128), F32),
            pltpu.SemaphoreType.DMA((2, CHUNKS)),
        ],
    )(where, basis, target)
    pieces = pl.pallas_call(
        scatter_kernel,
        out_shape=(piece,) * CUBE,
        in_specs=[smem, vmem, vmem],
        out_specs=(vmem,) * CUBE,
    )(where, keep, exchange(send, mesh, gz=1))
    masks = [(mask & 3, mask >> 2) for mask in range(CUBE)]
    got = [exchange(pieces[m], mesh, gx=masks[m][0], gy=masks[m][1]) for m in range(1, CUBE)]
    mine = pl.pallas_call(
        sum_kernel, out_shape=piece, in_specs=[vmem] * CUBE, out_specs=vmem
    )(pieces[0], *got)
    for bit in range(2, (mesh.shape["gx"] - 1).bit_length()):
        mine = mine + exchange(mine, mesh, gx=1 << bit)
    for bit in range(1, (mesh.shape["gy"] - 1).bit_length()):
        mine = mine + exchange(mine, mesh, gy=1 << bit)
    got = [exchange(mine, mesh, gx=masks[m][0], gy=masks[m][1]) for m in range(1, CUBE)]
    mine = pl.pallas_call(
        gather_kernel, out_shape=half, in_specs=[smem] + [vmem] * CUBE, out_specs=vmem
    )(where, mine, *got)
    other = exchange(mine, mesh, gz=1)
    first = core * NODES
    shifts = lax.dynamic_slice_in_dim(jnp.asarray(points**2, F32), first, NODES)
    node_wts = lax.dynamic_slice_in_dim(jnp.asarray(weights, F32), first, NODES)
    square = jax.ShapeDtypeStruct((n, n), F32)
    part, cross = pl.pallas_call(
        resolvent_kernel,
        out_shape=(square, square),
        in_specs=[smem, smem, smem, vmem, vmem],
        out_specs=(vmem, vmem),
        scratch_shapes=[
            pltpu.VMEM((2, NODES * n, 128), F32),
            pltpu.VMEM((2, 128, 128), F32),
            pltpu.VMEM((2, 2 * 128, 128), F32),
            pltpu.VMEM((NODES, STEP, n), F32),
            pltpu.VMEM((PAY_ROWS, 128), F32),
        ],
        compiler_params=limit,
        cost_estimate=pl.CostEstimate(flops=10**11, bytes_accessed=10**6, transcendentals=0),
    )(where, shifts, node_wts, mine, other)
    other = exchange(part, mesh, gz=1)
    residual = pl.pallas_call(
        residual_kernel,
        out_shape=jax.ShapeDtypeStruct((rows, n), F32),
        in_specs=[vmem, vmem, vmem],
        out_specs=vmem,
        compiler_params=limit,
        cost_estimate=pl.CostEstimate(flops=10**9, bytes_accessed=3 * 10**6, transcendentals=0),
    )(cross, basis, target)
    return pl.pallas_call(
        functools.partial(lift_kernel, float(np.sqrt(total_rows))),
        out_shape=jax.ShapeDtypeStruct((rows, n), F32),
        in_specs=[vmem] * 4,
        out_specs=vmem,
        compiler_params=limit,
    )(part, other, cross, residual)


def solution(mesh):
    return jax.shard_map(
        functools.partial(on_device, mesh=mesh),
        mesh=mesh,
        in_specs=(P(("gx", "gy", "gz"), None), P(("gx", "gy", "gz"), None)),
        out_specs=P(("gx", "gy", "gz"), None),
        check_vma=False,
    )
```

```python
import functools

import jax
import jax.numpy as jnp
import numpy as np
from jax import lax
from jax.experimental import pallas as pl
from jax.experimental.pallas import tpu as pltpu
from jax.sharding import PartitionSpec as P

half_points = [
    0.0950125098376374,
    0.2816035507792589,
    0.4580167776572274,
    0.6178762444026438,
    0.755404408355003,
    0.8656312023878318,
    0.9445750230732326,
    0.9894009349916499,
]
half_weights = [
    0.1894506104550685,
    0.1826034150449236,
    0.1691565193950025,
    0.1495959888165767,
    0.1246289712555339,
    0.0951585116824928,
    0.0622535239386479,
    0.0271524594117541,
]
points = (np.array([-v for v in half_points[::-1]] + half_points) + 1.0) / 2.0
weights = np.array(half_weights[::-1] + half_weights) / 2.0
NODES = 8
CHUNKS = 4
GRANT = 63 * 1024 * 1024
STEP = 32
F32 = jnp.float32
BF16 = jnp.bfloat16
highest = lax.Precision.HIGHEST


def iota(shape, dim):
    return lax.broadcasted_iota(jnp.int32, shape, dim)


def split(x):
    high = x.astype(BF16).astype(F32)
    rest = x - high
    mid = rest.astype(BF16).astype(F32)
    return high, mid, rest - mid


def dot(a, b):
    return jnp.dot(a, b, precision=highest, preferred_element_type=F32)


def halves(x):
    high = x.astype(BF16)
    return high, (x - high.astype(F32)).astype(BF16)


def dot3(a, b):
    (ah, al), (bh, bl) = a, b
    total = jnp.dot(ah, bl, preferred_element_type=F32) + jnp.dot(al, bh, preferred_element_type=F32)
    return total + jnp.dot(ah, bh, preferred_element_type=F32)


def gram_kernel(where_ref, b_hbm, t_hbm, keep_ref, send_ref, b_ref, t_ref, pay, sems):
    rows, n = b_ref.shape
    chunk = rows // CHUNKS
    copies = []
    for c in range(CHUNKS):
        part = pl.ds(c * chunk, chunk)
        for k, (source, dest) in enumerate(((b_hbm, b_ref), (t_hbm, t_ref))):
            copy = pltpu.make_async_copy(source.at[part], dest.at[part], sems.at[k, c])
            copy.start()
            copies.append(copy)
    cross = tgram = bgram = jnp.zeros((n, n), F32)
    for c in range(CHUNKS):
        part = slice(c * chunk, (c + 1) * chunk)
        copies[2 * c].wait()
        copies[2 * c + 1].wait()
        b, t = b_ref[part, :], t_ref[part, :]
        b, bt, t, tt = halves(b), halves(b.T), halves(t), halves(t.T)
        cross += dot3(bt, t)
        tgram += dot3(tt, t)
        bgram += dot3(bt, b)
    row, col = iota((n, n), 0), iota((n, n), 1)
    packed = jnp.where(row < col, tgram, bgram)
    diag = row == col
    tdiag = jnp.sum(jnp.where(diag, tgram, 0.0), axis=0, keepdims=True)
    bdiag = jnp.sum(jnp.where(diag, bgram, 0.0), axis=0, keepdims=True)
    for c in range(2):
        half = slice(c * 128, (c + 1) * 128)
        pay[c * n : (c + 1) * n, :] = cross[:, half]
        pay[(2 + c) * n : (3 + c) * n, :] = packed[:, half]
    pay[4 * n :, :] = jnp.zeros((pay.shape[0] - 4 * n, 128), F32)
    for c in range(2):
        half = slice(c * 128, (c + 1) * 128)
        pay[4 * n + c : 4 * n + c + 1, :] = tdiag[:, half]
        pay[4 * n + 2 + c : 4 * n + 3 + c, :] = bdiag[:, half]
    half, core = keep_ref.shape[0], where_ref[0]
    keep_ref[...] = pay[pl.ds(pl.multiple_of(core * half, 8), half), :]
    send_ref[...] = pay[pl.ds(pl.multiple_of((1 - core) * half, 8), half), :]


def invert_blocks(v):
    group = iota((8, 128), 1) // NODES
    node = iota((8, 128), 1) % NODES
    row = iota((8, 128), 0)
    for g in range(4):
        q, first = g // 2, g % 2 * 8
        pan = []
        for p in range(8):
            index = node + (first + p) * NODES
            pan.append([jnp.take_along_axis(x, index, axis=1) for x in v[q]])
        for p in range(8):
            recip = 1.0 / pan[p][g][p : p + 1, :]
            new = [x for x in pan[p]]
            new[g] = jnp.where(row == p, 1.0, new[g])
            new = [x * recip for x in new]
            pan[p] = new
            for o in range(8):
                if o != p:
                    factor = pan[o][g][p : p + 1, :]
                    old = [x for x in pan[o]]
                    old[g] = jnp.where(row == p, 0.0, old[g])
                    pan[o] = [x - factor * y for x, y in zip(old, new)]
        for o in range(2):
            acc = [x for x in v[o]]
            acc[g] = jnp.zeros((8, 128), F32)
            for p in range(8):
                factor = v[o][g][p : p + 1, :]
                acc = [x - factor * y for x, y in zip(acc, pan[p])]
            if o == q:
                for p in range(8):
                    acc = [jnp.where(group == first + p, y, x) for x, y in zip(acc, pan[p])]
            v[o] = acc
    return v


def resolvent_kernel(
    where_ref, shift_ref, weight_ref, mine_ref, other_ref, out_ref, cross_ref, mats, turned, inverses, news, pay
):
    n = out_ref.shape[1]
    half, core = mine_ref.shape[0], where_ref[0]
    pay[pl.ds(pl.multiple_of(core * half, 8), half), :] = mine_ref[...]
    pay[pl.ds(pl.multiple_of((1 - core) * half, 8), half), :] = other_ref[...]
    row, col = iota((n, n), 0), iota((n, n), 1)

    def wide(start, rows):
        return jnp.concatenate([pay[start : start + rows, :], pay[start + rows : start + 2 * rows, :]], 1)

    cross, packed = wide(0, n), wide(2 * n, n)
    cross_ref[...] = cross
    tdiag, bdiag = wide(4 * n, 1), wide(4 * n + 2, 1)
    upper = jnp.where(row < col, packed, 0.0)
    lower = jnp.where(row > col, packed, 0.0)
    tgram = upper + upper.T + jnp.where(row == col, tdiag, 0.0)
    bgram = lower + lower.T + jnp.where(row == col, bdiag, 0.0)
    crosst = cross.T
    square = dot(crosst, cross)
    normal = tgram - 2.0 * square + dot(crosst, dot(bgram, cross))
    for m in range(NODES):
        shifted = square + shift_ref[m] * normal
        mats[0, m * n : (m + 1) * n, :] = shifted[:, 0:128]
        mats[1, m * n : (m + 1) * n, :] = shifted[:, 128:256]

    def stack(x):
        h, m, l = split(x)
        return jnp.concatenate([h, m, h, l, h, m, l, m], 0).astype(BF16)

    def step(tile, part, carry):
        inner = pl.multiple_of(part * STEP, STEP)
        start = pl.multiple_of(tile * 128 + inner, STEP)
        v = []
        for q in range(2):
            rows = [mats[tile, pl.ds(start + 16 * q + i, NODES, stride=n), :] for i in range(16)]
            turned[q] = jnp.concatenate(rows, 0).T
            block = turned[q, pl.ds(inner, STEP), :]
            v.append([block[8 * g : 8 * g + 8] for g in range(4)])
        v = invert_blocks(v)
        for q in range(2):
            h, m, l = split(jnp.concatenate(v[q], 0))
            inverses[0, q * 128 : (q + 1) * 128, :] = jnp.concatenate([h, h, m, h], 0).T
            inverses[1, q * 128 : (q + 1) * 128, :] = jnp.concatenate([l, m, m, l], 0).T

        group = iota((n, 128), 1) // STEP
        index = iota((n, 128), 1) % STEP + inner
        local = iota((STEP, n), 1) - start
        inblock = (local >= 0) & (local < STEP)
        minus = jnp.where(local == iota((STEP, n), 0), -1.0, 0.0)
        for m in range(NODES):
            left = [inverses[c, pl.ds(m, STEP, stride=NODES), :] for c in range(2)]
            left = jnp.concatenate(left, 1).astype(BF16)
            here = pl.ds(pl.multiple_of(m * n + start, STEP), STEP)
            panel = jnp.concatenate([mats[0, here, :], mats[1, here, :]], 1)
            panel = jnp.where(inblock, minus, panel)
            news[m] = jnp.dot(left, stack(panel), preferred_element_type=F32)
        for m in range(NODES):
            rows = slice(m * n, (m + 1) * n)
            columns = jnp.take_along_axis(mats[tile, rows, :], index, axis=1)
            h, d, l = split(columns)
            one = jnp.where(group == 2, d, h)
            two = jnp.where((group == 0) | (group == 3), l, d)
            lhs = jnp.concatenate([one, two], 1).astype(BF16)
            change = jnp.dot(lhs, stack(news[m]), preferred_element_type=F32)
            for c in range(2):
                half = slice(c * 128, (c + 1) * 128)
                old = mats[c, rows, :]
                if c == tile:
                    old = jnp.where(inblock[0:1, half], 0.0, old)
                mats[c, rows, :] = old - change[:, half]
        for m in range(NODES):
            here = pl.ds(pl.multiple_of(m * n + start, STEP), STEP)
            mats[0, here, :] = news[m, :, 0:128]
            mats[1, here, :] = news[m, :, 128:256]
        return carry

    for tile in range(2):
        lax.fori_loop(0, 4, functools.partial(step, tile), 0)
    for c in range(2):
        half = weight_ref[0] * mats[c, 0:n, :]
        for m in range(1, NODES):
            half = half + weight_ref[m] * mats[c, m * n : (m + 1) * n, :]
        out_ref[:, c * 128 : (c + 1) * 128] = half


def residual_kernel(cross_ref, b_ref, t_ref, out_ref):
    out_ref[...] = t_ref[...] - dot3(halves(b_ref[...]), halves(cross_ref[...]))


def lift_kernel(scale, mine_ref, other_ref, cross_ref, z_ref, out_ref):
    total = (mine_ref[...] + other_ref[...]) * -scale
    right = halves(dot(total, cross_ref[...].T))
    out_ref[...] = dot3(halves(z_ref[...]), right)


def swap_cores(x):
    return lax.ppermute(x, "gz", [(0, 1), (1, 0)])


def summed(x, chips):
    pieces = lax.all_to_all(x, ("gx", "gy"), 0, 0, tiled=True)
    piece = jnp.sum(pieces.reshape(chips, -1, x.shape[1]), axis=0)
    return lax.all_to_all(jnp.tile(piece, (chips, 1)), ("gx", "gy"), 0, 0, tiled=True)


def on_device(basis, target, mesh):
    rows, n = basis.shape
    total_rows = rows * mesh.size
    chips = mesh.shape["gx"] * mesh.shape["gy"]
    pay_half = -(-(2 * n + 8) // (8 * chips)) * 8 * chips
    vmem = pl.BlockSpec(memory_space=pltpu.VMEM)
    smem = pl.BlockSpec(memory_space=pltpu.SMEM)
    hbm = pl.BlockSpec(memory_space=pltpu.HBM)
    limit = pltpu.CompilerParams(vmem_limit_bytes=48 * 1024 * 1024)
    core = lax.axis_index("gz")
    where = jnp.reshape(core, (1,)).astype(jnp.int32)
    half = jax.ShapeDtypeStruct((pay_half, 128), F32)
    keep, send = pl.pallas_call(
        gram_kernel,
        out_shape=(half, half),
        in_specs=[smem, hbm, hbm],
        out_specs=(vmem, vmem),
        scratch_shapes=[
            pltpu.VMEM((rows, n), F32),
            pltpu.VMEM((rows, n), F32),
            pltpu.VMEM((2 * pay_half, 128), F32),
            pltpu.SemaphoreType.DMA((2, CHUNKS)),
        ],
        compiler_params=pltpu.CompilerParams(vmem_limit_bytes=GRANT),
    )(where, basis, target)
    mine = summed(keep + swap_cores(send), chips)
    other = swap_cores(mine)
    first = core * NODES
    shifts = lax.dynamic_slice_in_dim(jnp.asarray(points**2, F32), first, NODES)
    node_wts = lax.dynamic_slice_in_dim(jnp.asarray(weights, F32), first, NODES)
    square = jax.ShapeDtypeStruct((n, n), F32)
    part, cross = pl.pallas_call(
        resolvent_kernel,
        out_shape=(square, square),
        in_specs=[smem, smem, smem, vmem, vmem],
        out_specs=(vmem, vmem),
        scratch_shapes=[
            pltpu.VMEM((2, NODES * n, 128), F32),
            pltpu.VMEM((2, 128, 128), F32),
            pltpu.VMEM((2, 2 * 128, 128), F32),
            pltpu.VMEM((NODES, STEP, n), F32),
            pltpu.VMEM((2 * pay_half, 128), F32),
        ],
        compiler_params=limit,
        cost_estimate=pl.CostEstimate(flops=10**11, bytes_accessed=10**6, transcendentals=0),
    )(where, shifts, node_wts, mine, other)
    other = swap_cores(part)
    residual = pl.pallas_call(
        residual_kernel,
        out_shape=jax.ShapeDtypeStruct((rows, n), F32),
        in_specs=[vmem, vmem, vmem],
        out_specs=vmem,
        compiler_params=limit,
        cost_estimate=pl.CostEstimate(flops=10**9, bytes_accessed=3 * 10**6, transcendentals=0),
    )(cross, basis, target)
    return pl.pallas_call(
        functools.partial(lift_kernel, float(np.sqrt(total_rows))),
        out_shape=jax.ShapeDtypeStruct((rows, n), F32),
        in_specs=[vmem] * 4,
        out_specs=vmem,
        compiler_params=limit,
    )(part, other, cross, residual)


def solution(mesh):
    return jax.shard_map(
        functools.partial(on_device, mesh=mesh),
        mesh=mesh,
        in_specs=(P(("gx", "gy", "gz"), None), P(("gx", "gy", "gz"), None)),
        out_specs=P(("gx", "gy", "gz"), None),
        check_vma=False,
    )
```

```python
import functools

import jax
import jax.numpy as jnp
import numpy as np
from jax import lax
from jax.experimental import pallas as pl
from jax.experimental.pallas import tpu as pltpu
from jax.sharding import PartitionSpec as P

half_points = [
    0.0950125098376374,
    0.2816035507792589,
    0.4580167776572274,
    0.6178762444026438,
    0.755404408355003,
    0.8656312023878318,
    0.9445750230732326,
    0.9894009349916499,
]
half_weights = [
    0.1894506104550685,
    0.1826034150449236,
    0.1691565193950025,
    0.1495959888165767,
    0.1246289712555339,
    0.0951585116824928,
    0.0622535239386479,
    0.0271524594117541,
]
points = (np.array([-v for v in half_points[::-1]] + half_points) + 1.0) / 2.0
weights = np.array(half_weights[::-1] + half_weights) / 2.0
NODES = 8
CHUNKS = 4
GRANT = 63 * 1024 * 1024
STEP = 32
F32 = jnp.float32
BF16 = jnp.bfloat16
highest = lax.Precision.HIGHEST


def iota(shape, dim):
    return lax.broadcasted_iota(jnp.int32, shape, dim)


def split(x):
    high = x.astype(BF16).astype(F32)
    rest = x - high
    mid = rest.astype(BF16).astype(F32)
    return high, mid, rest - mid


def dot(a, b):
    return jnp.dot(a, b, precision=highest, preferred_element_type=F32)


def halves(x):
    high = x.astype(BF16)
    return high, (x - high.astype(F32)).astype(BF16)


def dot3(a, b):
    (ah, al), (bh, bl) = a, b
    total = jnp.dot(ah, bl, preferred_element_type=F32) + jnp.dot(al, bh, preferred_element_type=F32)
    return total + jnp.dot(ah, bh, preferred_element_type=F32)


def gram_kernel(where_ref, b_hbm, t_hbm, keep_ref, send_ref, b_ref, t_ref, pay, sems):
    rows, n = b_ref.shape
    chunk = rows // CHUNKS
    copies = []
    for c in range(CHUNKS):
        part = pl.ds(c * chunk, chunk)
        for k, (source, dest) in enumerate(((b_hbm, b_ref), (t_hbm, t_ref))):
            copy = pltpu.make_async_copy(source.at[part], dest.at[part], sems.at[k, c])
            copy.start()
            copies.append(copy)
    cross = tgram = bgram = jnp.zeros((n, n), F32)
    for c in range(CHUNKS):
        part = slice(c * chunk, (c + 1) * chunk)
        copies[2 * c].wait()
        copies[2 * c + 1].wait()
        b, t = b_ref[part, :], t_ref[part, :]
        b, bt, t, tt = halves(b), halves(b.T), halves(t), halves(t.T)
        cross += dot3(bt, t)
        tgram += dot3(tt, t)
        bgram += dot3(bt, b)
    row, col = iota((n, n), 0), iota((n, n), 1)
    packed = jnp.where(row < col, tgram, bgram)
    diag = row == col
    tdiag = jnp.sum(jnp.where(diag, tgram, 0.0), axis=0, keepdims=True)
    bdiag = jnp.sum(jnp.where(diag, bgram, 0.0), axis=0, keepdims=True)
    for c in range(2):
        half = slice(c * 128, (c + 1) * 128)
        pay[c * n : (c + 1) * n, :] = cross[:, half]
        pay[(2 + c) * n : (3 + c) * n, :] = packed[:, half]
    pay[4 * n :, :] = jnp.zeros((pay.shape[0] - 4 * n, 128), F32)
    for c in range(2):
        half = slice(c * 128, (c + 1) * 128)
        pay[4 * n + c : 4 * n + c + 1, :] = tdiag[:, half]
        pay[4 * n + 2 + c : 4 * n + 3 + c, :] = bdiag[:, half]
    half, core = keep_ref.shape[0], where_ref[0]
    keep_ref[...] = pay[pl.ds(pl.multiple_of(core * half, 8), half), :]
    send_ref[...] = pay[pl.ds(pl.multiple_of((1 - core) * half, 8), half), :]


def invert_blocks(v):
    group = iota((8, 128), 1) // NODES
    node = iota((8, 128), 1) % NODES
    row = iota((8, 128), 0)
    for g in range(4):
        q, first = g // 2, g % 2 * 8
        pan = []
        for p in range(8):
            index = node + (first + p) * NODES
            pan.append([jnp.take_along_axis(x, index, axis=1) for x in v[q]])
        for p in range(8):
            recip = 1.0 / pan[p][g][p : p + 1, :]
            new = [x for x in pan[p]]
            new[g] = jnp.where(row == p, 1.0, new[g])
            new = [x * recip for x in new]
            pan[p] = new
            for o in range(8):
                if o != p:
                    factor = pan[o][g][p : p + 1, :]
                    old = [x for x in pan[o]]
                    old[g] = jnp.where(row == p, 0.0, old[g])
                    pan[o] = [x - factor * y for x, y in zip(old, new)]
        for o in range(2):
            acc = [x for x in v[o]]
            acc[g] = jnp.zeros((8, 128), F32)
            for p in range(8):
                factor = v[o][g][p : p + 1, :]
                acc = [x - factor * y for x, y in zip(acc, pan[p])]
            if o == q:
                for p in range(8):
                    acc = [jnp.where(group == first + p, y, x) for x, y in zip(acc, pan[p])]
            v[o] = acc
    return v


def resolvent_kernel(
    where_ref, shift_ref, weight_ref, mine_ref, other_ref, out_ref, cross_ref, mats, turned, inverses, news, pay
):
    n = out_ref.shape[1]
    half, core = mine_ref.shape[0], where_ref[0]
    pay[pl.ds(pl.multiple_of(core * half, 8), half), :] = mine_ref[...]
    pay[pl.ds(pl.multiple_of((1 - core) * half, 8), half), :] = other_ref[...]
    row, col = iota((n, n), 0), iota((n, n), 1)

    def wide(start, rows):
        return jnp.concatenate([pay[start : start + rows, :], pay[start + rows : start + 2 * rows, :]], 1)

    cross, packed = wide(0, n), wide(2 * n, n)
    cross_ref[...] = cross
    tdiag, bdiag = wide(4 * n, 1), wide(4 * n + 2, 1)
    upper = jnp.where(row < col, packed, 0.0)
    lower = jnp.where(row > col, packed, 0.0)
    tgram = upper + upper.T + jnp.where(row == col, tdiag, 0.0)
    bgram = lower + lower.T + jnp.where(row == col, bdiag, 0.0)
    crosst = cross.T
    square = dot(crosst, cross)
    normal = tgram - 2.0 * square + dot(crosst, dot(bgram, cross))
    for m in range(NODES):
        shifted = square + shift_ref[core * NODES + m] * normal
        mats[0, m * n : (m + 1) * n, :] = shifted[:, 0:128]
        mats[1, m * n : (m + 1) * n, :] = shifted[:, 128:256]

    def stack(x):
        h, m, l = split(x)
        return jnp.concatenate([h, m, h, l, h, m, l, m], 0).astype(BF16)

    def step(tile, part, carry):
        inner = pl.multiple_of(part * STEP, STEP)
        start = pl.multiple_of(tile * 128 + inner, STEP)
        v = []
        for q in range(2):
            rows = [mats[tile, pl.ds(start + 16 * q + i, NODES, stride=n), :] for i in range(16)]
            turned[q] = jnp.concatenate(rows, 0).T
            block = turned[q, pl.ds(inner, STEP), :]
            v.append([block[8 * g : 8 * g + 8] for g in range(4)])
        v = invert_blocks(v)
        for q in range(2):
            h, m, l = split(jnp.concatenate(v[q], 0))
            inverses[0, q * 128 : (q + 1) * 128, :] = jnp.concatenate([h, h, m, h], 0).T
            inverses[1, q * 128 : (q + 1) * 128, :] = jnp.concatenate([l, m, m, l], 0).T

        group = iota((n, 128), 1) // STEP
        index = iota((n, 128), 1) % STEP + inner
        local = iota((STEP, n), 1) - start
        inblock = (local >= 0) & (local < STEP)
        minus = jnp.where(local == iota((STEP, n), 0), -1.0, 0.0)
        for m in range(NODES):
            left = [inverses[c, pl.ds(m, STEP, stride=NODES), :] for c in range(2)]
            left = jnp.concatenate(left, 1).astype(BF16)
            here = pl.ds(pl.multiple_of(m * n + start, STEP), STEP)
            panel = jnp.concatenate([mats[0, here, :], mats[1, here, :]], 1)
            panel = jnp.where(inblock, minus, panel)
            news[m] = jnp.dot(left, stack(panel), preferred_element_type=F32)
        for m in range(NODES):
            rows = slice(m * n, (m + 1) * n)
            columns = jnp.take_along_axis(mats[tile, rows, :], index, axis=1)
            h, d, l = split(columns)
            one = jnp.where(group == 2, d, h)
            two = jnp.where((group == 0) | (group == 3), l, d)
            lhs = jnp.concatenate([one, two], 1).astype(BF16)
            change = jnp.dot(lhs, stack(news[m]), preferred_element_type=F32)
            for c in range(2):
                half = slice(c * 128, (c + 1) * 128)
                old = mats[c, rows, :]
                if c == tile:
                    old = jnp.where(inblock[0:1, half], 0.0, old)
                mats[c, rows, :] = old - change[:, half]
        for m in range(NODES):
            here = pl.ds(pl.multiple_of(m * n + start, STEP), STEP)
            mats[0, here, :] = news[m, :, 0:128]
            mats[1, here, :] = news[m, :, 128:256]
        return carry

    for tile in range(2):
        lax.fori_loop(0, 4, functools.partial(step, tile), 0)
    for c in range(2):
        half = weight_ref[core * NODES] * mats[c, 0:n, :]
        for m in range(1, NODES):
            half = half + weight_ref[core * NODES + m] * mats[c, m * n : (m + 1) * n, :]
        out_ref[:, c * 128 : (c + 1) * 128] = half


def residual_kernel(cross_ref, b_ref, t_ref, out_ref):
    out_ref[...] = t_ref[...] - dot3(halves(b_ref[...]), halves(cross_ref[...]))


def lift_kernel(scale, mine_ref, other_ref, cross_ref, z_ref, out_hbm, out_ref, sems):
    rows = z_ref.shape[0] // CHUNKS
    total = (mine_ref[...] + other_ref[...]) * -scale
    right = halves(dot(total, cross_ref[...].T))
    copies = []
    for c in range(CHUNKS):
        part = pl.ds(c * rows, rows)
        out_ref[part, :] = dot3(halves(z_ref[part, :]), right)
        copies.append(pltpu.make_async_copy(out_ref.at[part], out_hbm.at[part], sems.at[c]))
        copies[-1].start()
    for copy in copies:
        copy.wait()


def swap_cores(x):
    return lax.ppermute(x, "gz", [(0, 1), (1, 0)])


def swap_bits(x, mesh, flips):
    ny, nz = mesh.shape["gy"], mesh.shape["gz"]
    perm = []
    for i in range(mesh.size):
        gx, gy, gz = i // (ny * nz), i // nz % ny, i % nz
        perm.append((i, ((gx ^ flips[gz][0]) * ny + (gy ^ flips[gz][1])) * nz + gz))
    return lax.ppermute(x, ("gx", "gy", "gz"), perm)


def joined(side, mine, other):
    return jnp.where(side == 0, jnp.concatenate([mine, other], 0), jnp.concatenate([other, mine], 0))


def summed(x, mesh):
    core = lax.axis_index("gz")
    bit_x, bit_y = lax.axis_index("gx") & 1, lax.axis_index("gy") & 1
    sides = [jnp.where(core == 0, bit_x, bit_y), jnp.where(core == 0, bit_y, bit_x)]
    flips = [((1, 0), (0, 1)), ((0, 1), (1, 0))]
    for side, flip in zip(sides, flips):
        half = x.shape[0] // 2
        keep = lax.dynamic_slice_in_dim(x, side * half, half, 0)
        send = lax.dynamic_slice_in_dim(x, (1 - side) * half, half, 0)
        x = keep + swap_bits(send, mesh, flip)
    gx = [(1 << bit, 0) for bit in range(1, (mesh.shape["gx"] - 1).bit_length())]
    gy = [(0, 1 << bit) for bit in range(1, (mesh.shape["gy"] - 1).bit_length())]
    for flip in zip(gx + gy, (gx + gy)[::-1]):
        x = x + swap_bits(x, mesh, flip)
    for side, flip in zip(sides[::-1], flips[::-1]):
        x = joined(side, x, swap_bits(x, mesh, flip))
    return x


def on_device(basis, target, mesh):
    rows, n = basis.shape
    total_rows = rows * mesh.size
    pay_half = -(-(2 * n + 8) // 32) * 32
    vmem = pl.BlockSpec(memory_space=pltpu.VMEM)
    smem = pl.BlockSpec(memory_space=pltpu.SMEM)
    hbm = pl.BlockSpec(memory_space=pltpu.HBM)
    limit = pltpu.CompilerParams(vmem_limit_bytes=48 * 1024 * 1024)
    core = lax.axis_index("gz")
    where = jnp.reshape(core, (1,)).astype(jnp.int32)
    half = jax.ShapeDtypeStruct((pay_half, 128), F32)
    keep, send = pl.pallas_call(
        gram_kernel,
        out_shape=(half, half),
        in_specs=[smem, hbm, hbm],
        out_specs=(vmem, vmem),
        scratch_shapes=[
            pltpu.VMEM((rows, n), F32),
            pltpu.VMEM((rows, n), F32),
            pltpu.VMEM((2 * pay_half, 128), F32),
            pltpu.SemaphoreType.DMA((2, CHUNKS)),
        ],
        compiler_params=pltpu.CompilerParams(vmem_limit_bytes=GRANT),
    )(where, basis, target)
    mine = summed(keep + swap_cores(send), mesh)
    other = swap_cores(mine)
    square = jax.ShapeDtypeStruct((n, n), F32)
    part, cross = pl.pallas_call(
        resolvent_kernel,
        out_shape=(square, square),
        in_specs=[smem, smem, smem, vmem, vmem],
        out_specs=(vmem, vmem),
        scratch_shapes=[
            pltpu.VMEM((2, NODES * n, 128), F32),
            pltpu.VMEM((2, 128, 128), F32),
            pltpu.VMEM((2, 2 * 128, 128), F32),
            pltpu.VMEM((NODES, STEP, n), F32),
            pltpu.VMEM((2 * pay_half, 128), F32),
        ],
        compiler_params=limit,
        cost_estimate=pl.CostEstimate(flops=10**11, bytes_accessed=10**6, transcendentals=0),
    )(where, jnp.asarray(points**2, F32), jnp.asarray(weights, F32), mine, other)
    other = swap_cores(part)
    residual = pl.pallas_call(
        residual_kernel,
        out_shape=jax.ShapeDtypeStruct((rows, n), F32),
        in_specs=[vmem, vmem, vmem],
        out_specs=vmem,
        compiler_params=limit,
        cost_estimate=pl.CostEstimate(flops=10**9, bytes_accessed=3 * 10**6, transcendentals=0),
    )(cross, basis, target)
    return pl.pallas_call(
        functools.partial(lift_kernel, float(np.sqrt(total_rows))),
        out_shape=jax.ShapeDtypeStruct((rows, n), F32),
        in_specs=[vmem] * 4,
        out_specs=hbm,
        scratch_shapes=[pltpu.VMEM((rows, n), F32), pltpu.SemaphoreType.DMA((CHUNKS,))],
        compiler_params=limit,
    )(part, other, cross, residual)


def solution(mesh):
    return jax.shard_map(
        functools.partial(on_device, mesh=mesh),
        mesh=mesh,
        in_specs=(P(("gx", "gy", "gz"), None), P(("gx", "gy", "gz"), None)),
        out_specs=P(("gx", "gy", "gz"), None),
        check_vma=False,
    )
```

```python
import functools

import jax
import jax.numpy as jnp
import numpy as np
from jax import lax
from jax.experimental import pallas as pl
from jax.experimental.pallas import tpu as pltpu
from jax.sharding import PartitionSpec as P

half_points = [
    0.0950125098376374,
    0.2816035507792589,
    0.4580167776572274,
    0.6178762444026438,
    0.755404408355003,
    0.8656312023878318,
    0.9445750230732326,
    0.9894009349916499,
]
half_weights = [
    0.1894506104550685,
    0.1826034150449236,
    0.1691565193950025,
    0.1495959888165767,
    0.1246289712555339,
    0.0951585116824928,
    0.0622535239386479,
    0.0271524594117541,
]
points = (np.array([-v for v in half_points[::-1]] + half_points) + 1.0) / 2.0
weights = np.array(half_weights[::-1] + half_weights) / 2.0
NODES = 8
CHUNKS = 4
CUBE = 8
GRANT = 63 * 1024 * 1024
STEP = 32
F32 = jnp.float32
BF16 = jnp.bfloat16
highest = lax.Precision.HIGHEST


def iota(shape, dim):
    return lax.broadcasted_iota(jnp.int32, shape, dim)


def split(x):
    high = x.astype(BF16).astype(F32)
    rest = x - high
    mid = rest.astype(BF16).astype(F32)
    return high, mid, rest - mid


def dot(a, b):
    return jnp.dot(a, b, precision=highest, preferred_element_type=F32)


def halves(x):
    high = x.astype(BF16)
    return high, (x - high.astype(F32)).astype(BF16)


def dot3(a, b):
    (ah, al), (bh, bl) = a, b
    total = jnp.dot(ah, bl, preferred_element_type=F32) + jnp.dot(al, bh, preferred_element_type=F32)
    return total + jnp.dot(ah, bh, preferred_element_type=F32)


def gram_kernel(where_ref, b_hbm, t_hbm, keep_ref, send_ref, b_ref, t_ref, pay, sems):
    rows, n = b_ref.shape
    chunk = rows // CHUNKS
    copies = []
    for c in range(CHUNKS):
        part = pl.ds(c * chunk, chunk)
        for k, (source, dest) in enumerate(((b_hbm, b_ref), (t_hbm, t_ref))):
            copy = pltpu.make_async_copy(source.at[part], dest.at[part], sems.at[k, c])
            copy.start()
            copies.append(copy)
    cross = tgram = bgram = jnp.zeros((n, n), F32)
    for c in range(CHUNKS):
        part = slice(c * chunk, (c + 1) * chunk)
        copies[2 * c].wait()
        copies[2 * c + 1].wait()
        b, t = b_ref[part, :], t_ref[part, :]
        b, bt, t, tt = halves(b), halves(b.T), halves(t), halves(t.T)
        cross += dot3(bt, t)
        tgram += dot3(tt, t)
        bgram += dot3(bt, b)
    row, col = iota((n, n), 0), iota((n, n), 1)
    packed = jnp.where(row < col, tgram, bgram)
    diag = row == col
    tdiag = jnp.sum(jnp.where(diag, tgram, 0.0), axis=0, keepdims=True)
    bdiag = jnp.sum(jnp.where(diag, bgram, 0.0), axis=0, keepdims=True)
    for c in range(2):
        half = slice(c * 128, (c + 1) * 128)
        pay[c * n : (c + 1) * n, :] = cross[:, half]
        pay[(2 + c) * n : (3 + c) * n, :] = packed[:, half]
    pay[4 * n :, :] = jnp.zeros((pay.shape[0] - 4 * n, 128), F32)
    for c in range(2):
        half = slice(c * 128, (c + 1) * 128)
        pay[4 * n + c : 4 * n + c + 1, :] = tdiag[:, half]
        pay[4 * n + 2 + c : 4 * n + 3 + c, :] = bdiag[:, half]
    half, core = keep_ref.shape[0], where_ref[0]
    keep_ref[...] = pay[pl.ds(pl.multiple_of(core * half, 8), half), :]
    send_ref[...] = pay[pl.ds(pl.multiple_of((1 - core) * half, 8), half), :]


def invert_blocks(v):
    group = iota((8, 128), 1) // NODES
    node = iota((8, 128), 1) % NODES
    row = iota((8, 128), 0)
    for g in range(4):
        q, first = g // 2, g % 2 * 8
        pan = []
        for p in range(8):
            index = node + (first + p) * NODES
            pan.append([jnp.take_along_axis(x, index, axis=1) for x in v[q]])
        for p in range(8):
            recip = 1.0 / pan[p][g][p : p + 1, :]
            new = [x for x in pan[p]]
            new[g] = jnp.where(row == p, 1.0, new[g])
            new = [x * recip for x in new]
            pan[p] = new
            for o in range(8):
                if o != p:
                    factor = pan[o][g][p : p + 1, :]
                    old = [x for x in pan[o]]
                    old[g] = jnp.where(row == p, 0.0, old[g])
                    pan[o] = [x - factor * y for x, y in zip(old, new)]
        for o in range(2):
            acc = [x for x in v[o]]
            acc[g] = jnp.zeros((8, 128), F32)
            for p in range(8):
                factor = v[o][g][p : p + 1, :]
                acc = [x - factor * y for x, y in zip(acc, pan[p])]
            if o == q:
                for p in range(8):
                    acc = [jnp.where(group == first + p, y, x) for x, y in zip(acc, pan[p])]
            v[o] = acc
    return v


def resolvent_kernel(
    where_ref, shift_ref, weight_ref, mine_ref, other_ref, out_ref, cross_ref, mats, turned, inverses, news, pay
):
    n = out_ref.shape[1]
    half, core = mine_ref.shape[0], where_ref[0]
    pay[pl.ds(pl.multiple_of(core * half, 8), half), :] = mine_ref[...]
    pay[pl.ds(pl.multiple_of((1 - core) * half, 8), half), :] = other_ref[...]
    row, col = iota((n, n), 0), iota((n, n), 1)

    def wide(start, rows):
        return jnp.concatenate([pay[start : start + rows, :], pay[start + rows : start + 2 * rows, :]], 1)

    cross, packed = wide(0, n), wide(2 * n, n)
    cross_ref[...] = cross
    tdiag, bdiag = wide(4 * n, 1), wide(4 * n + 2, 1)
    upper = jnp.where(row < col, packed, 0.0)
    lower = jnp.where(row > col, packed, 0.0)
    tgram = upper + upper.T + jnp.where(row == col, tdiag, 0.0)
    bgram = lower + lower.T + jnp.where(row == col, bdiag, 0.0)
    crosst = cross.T
    square = dot(crosst, cross)
    normal = tgram - 2.0 * square + dot(crosst, dot(bgram, cross))
    for m in range(NODES):
        shifted = square + shift_ref[core * NODES + m] * normal
        mats[0, m * n : (m + 1) * n, :] = shifted[:, 0:128]
        mats[1, m * n : (m + 1) * n, :] = shifted[:, 128:256]

    def stack(x):
        h, m, l = split(x)
        return jnp.concatenate([h, m, h, l, h, m, l, m], 0).astype(BF16)

    def step(tile, part, carry):
        inner = pl.multiple_of(part * STEP, STEP)
        start = pl.multiple_of(tile * 128 + inner, STEP)
        v = []
        for q in range(2):
            rows = [mats[tile, pl.ds(start + 16 * q + i, NODES, stride=n), :] for i in range(16)]
            turned[q] = jnp.concatenate(rows, 0).T
            block = turned[q, pl.ds(inner, STEP), :]
            v.append([block[8 * g : 8 * g + 8] for g in range(4)])
        v = invert_blocks(v)
        for q in range(2):
            h, m, l = split(jnp.concatenate(v[q], 0))
            inverses[0, q * 128 : (q + 1) * 128, :] = jnp.concatenate([h, h, m, h], 0).T
            inverses[1, q * 128 : (q + 1) * 128, :] = jnp.concatenate([l, m, m, l], 0).T

        group = iota((n, 128), 1) // STEP
        index = iota((n, 128), 1) % STEP + inner
        local = iota((STEP, n), 1) - start
        inblock = (local >= 0) & (local < STEP)
        minus = jnp.where(local == iota((STEP, n), 0), -1.0, 0.0)
        for m in range(NODES):
            left = [inverses[c, pl.ds(m, STEP, stride=NODES), :] for c in range(2)]
            left = jnp.concatenate(left, 1).astype(BF16)
            here = pl.ds(pl.multiple_of(m * n + start, STEP), STEP)
            panel = jnp.concatenate([mats[0, here, :], mats[1, here, :]], 1)
            panel = jnp.where(inblock, minus, panel)
            news[m] = jnp.dot(left, stack(panel), preferred_element_type=F32)
        for m in range(NODES):
            rows = slice(m * n, (m + 1) * n)
            columns = jnp.take_along_axis(mats[tile, rows, :], index, axis=1)
            h, d, l = split(columns)
            one = jnp.where(group == 2, d, h)
            two = jnp.where((group == 0) | (group == 3), l, d)
            lhs = jnp.concatenate([one, two], 1).astype(BF16)
            change = jnp.dot(lhs, stack(news[m]), preferred_element_type=F32)
            for c in range(2):
                half = slice(c * 128, (c + 1) * 128)
                old = mats[c, rows, :]
                if c == tile:
                    old = jnp.where(inblock[0:1, half], 0.0, old)
                mats[c, rows, :] = old - change[:, half]
        for m in range(NODES):
            here = pl.ds(pl.multiple_of(m * n + start, STEP), STEP)
            mats[0, here, :] = news[m, :, 0:128]
            mats[1, here, :] = news[m, :, 128:256]
        return carry

    for tile in range(2):
        lax.fori_loop(0, 4, functools.partial(step, tile), 0)
    for c in range(2):
        half = weight_ref[core * NODES] * mats[c, 0:n, :]
        for m in range(1, NODES):
            half = half + weight_ref[core * NODES + m] * mats[c, m * n : (m + 1) * n, :]
        out_ref[:, c * 128 : (c + 1) * 128] = half


def residual_kernel(cross_ref, b_ref, t_ref, out_ref):
    out_ref[...] = t_ref[...] - dot3(halves(b_ref[...]), halves(cross_ref[...]))


def lift_kernel(scale, mine_ref, other_ref, cross_ref, z_ref, out_hbm, out_ref, sems):
    rows = z_ref.shape[0] // CHUNKS
    total = (mine_ref[...] + other_ref[...]) * -scale
    right = halves(dot(total, cross_ref[...].T))
    copies = []
    for c in range(CHUNKS):
        part = pl.ds(c * rows, rows)
        out_ref[part, :] = dot3(halves(z_ref[part, :]), right)
        copies.append(pltpu.make_async_copy(out_ref.at[part], out_hbm.at[part], sems.at[c]))
        copies[-1].start()
    for copy in copies:
        copy.wait()


def swap_cores(x):
    return lax.ppermute(x, "gz", [(0, 1), (1, 0)])


def swap_bits(x, mesh, gx, gy):
    ny, nz = mesh.shape["gy"], mesh.shape["gz"]
    perm = []
    for i in range(mesh.size):
        x0, y0, z0 = i // (ny * nz), i // nz % ny, i % nz
        perm.append((i, ((x0 ^ gx) * ny + (y0 ^ gy)) * nz + z0))
    return lax.ppermute(x, ("gx", "gy", "gz"), perm)


def summed(x, mesh):
    nx, ny = mesh.shape["gx"], mesh.shape["gy"]
    low = [(a, b) for a in range(4) for b in range(2)]
    groups = [
        [(gx + a) * ny + gy + b for a, b in low] for gx in range(0, nx, 4) for gy in range(0, ny, 2)
    ]

    def cube(pieces):
        return lax.all_to_all(
            pieces, ("gx", "gy"), 0, 0, axis_index_groups=groups, tiled=True
        )

    x = jnp.sum(cube(x).reshape(CUBE, -1, x.shape[1]), axis=0)
    for bit in range(2, (nx - 1).bit_length()):
        x = x + swap_bits(x, mesh, 1 << bit, 0)
    for bit in range(1, (ny - 1).bit_length()):
        x = x + swap_bits(x, mesh, 0, 1 << bit)
    return cube(jnp.tile(x, (CUBE, 1)))


def on_device(basis, target, mesh):
    rows, n = basis.shape
    total_rows = rows * mesh.size
    pay_half = -(-(2 * n + 8) // (8 * CUBE)) * 8 * CUBE
    vmem = pl.BlockSpec(memory_space=pltpu.VMEM)
    smem = pl.BlockSpec(memory_space=pltpu.SMEM)
    hbm = pl.BlockSpec(memory_space=pltpu.HBM)
    limit = pltpu.CompilerParams(vmem_limit_bytes=48 * 1024 * 1024)
    core = lax.axis_index("gz")
    where = jnp.reshape(core, (1,)).astype(jnp.int32)
    half = jax.ShapeDtypeStruct((pay_half, 128), F32)
    keep, send = pl.pallas_call(
        gram_kernel,
        out_shape=(half, half),
        in_specs=[smem, hbm, hbm],
        out_specs=(vmem, vmem),
        scratch_shapes=[
            pltpu.VMEM((rows, n), F32),
            pltpu.VMEM((rows, n), F32),
            pltpu.VMEM((2 * pay_half, 128), F32),
            pltpu.SemaphoreType.DMA((2, CHUNKS)),
        ],
        compiler_params=pltpu.CompilerParams(vmem_limit_bytes=GRANT),
    )(where, basis, target)
    mine = summed(keep + swap_cores(send), mesh)
    other = swap_cores(mine)
    square = jax.ShapeDtypeStruct((n, n), F32)
    part, cross = pl.pallas_call(
        resolvent_kernel,
        out_shape=(square, square),
        in_specs=[smem, smem, smem, vmem, vmem],
        out_specs=(vmem, vmem),
        scratch_shapes=[
            pltpu.VMEM((2, NODES * n, 128), F32),
            pltpu.VMEM((2, 128, 128), F32),
            pltpu.VMEM((2, 2 * 128, 128), F32),
            pltpu.VMEM((NODES, STEP, n), F32),
            pltpu.VMEM((2 * pay_half, 128), F32),
        ],
        compiler_params=limit,
        cost_estimate=pl.CostEstimate(flops=10**11, bytes_accessed=10**6, transcendentals=0),
    )(where, jnp.asarray(points**2, F32), jnp.asarray(weights, F32), mine, other)
    other = swap_cores(part)
    residual = pl.pallas_call(
        residual_kernel,
        out_shape=jax.ShapeDtypeStruct((rows, n), F32),
        in_specs=[vmem, vmem, vmem],
        out_specs=vmem,
        compiler_params=limit,
        cost_estimate=pl.CostEstimate(flops=10**9, bytes_accessed=3 * 10**6, transcendentals=0),
    )(cross, basis, target)
    return pl.pallas_call(
        functools.partial(lift_kernel, float(np.sqrt(total_rows))),
        out_shape=jax.ShapeDtypeStruct((rows, n), F32),
        in_specs=[vmem] * 4,
        out_specs=hbm,
        scratch_shapes=[pltpu.VMEM((rows, n), F32), pltpu.SemaphoreType.DMA((CHUNKS,))],
        compiler_params=limit,
    )(part, other, cross, residual)


def solution(mesh):
    return jax.shard_map(
        functools.partial(on_device, mesh=mesh),
        mesh=mesh,
        in_specs=(P(("gx", "gy", "gz"), None), P(("gx", "gy", "gz"), None)),
        out_specs=P(("gx", "gy", "gz"), None),
        check_vma=False,
    )
```

```python
import functools

import jax
import jax.numpy as jnp
import numpy as np
from jax import lax
from jax.experimental import pallas as pl
from jax.experimental.pallas import tpu as pltpu
from jax.sharding import PartitionSpec as P

half_points = [
    0.0950125098376374,
    0.2816035507792589,
    0.4580167776572274,
    0.6178762444026438,
    0.755404408355003,
    0.8656312023878318,
    0.9445750230732326,
    0.9894009349916499,
]
half_weights = [
    0.1894506104550685,
    0.1826034150449236,
    0.1691565193950025,
    0.1495959888165767,
    0.1246289712555339,
    0.0951585116824928,
    0.0622535239386479,
    0.0271524594117541,
]
points = (np.array([-v for v in half_points[::-1]] + half_points) + 1.0) / 2.0
weights = np.array(half_weights[::-1] + half_weights) / 2.0
NODES = 8
CHUNKS = 4
CUBE = 8
GRANT = 53 * 1024 * 1024
STEP = 32
F32 = jnp.float32
BF16 = jnp.bfloat16
highest = lax.Precision.HIGHEST


def iota(shape, dim):
    return lax.broadcasted_iota(jnp.int32, shape, dim)


def split(x):
    high = x.astype(BF16).astype(F32)
    rest = x - high
    mid = rest.astype(BF16).astype(F32)
    return high, mid, rest - mid


def dot(a, b):
    return jnp.dot(a, b, precision=highest, preferred_element_type=F32)


def halves(x):
    high = x.astype(BF16)
    return high, (x - high.astype(F32)).astype(BF16)


def dot3(a, b):
    (ah, al), (bh, bl) = a, b
    total = jnp.dot(ah, bl, preferred_element_type=F32) + jnp.dot(al, bh, preferred_element_type=F32)
    return total + jnp.dot(ah, bh, preferred_element_type=F32)


def gram_kernel(where_ref, b_hbm, t_hbm, keep_ref, send_ref, b_ref, t_ref, pay, sems):
    rows, n = b_ref.shape
    chunk = rows // CHUNKS
    copies = []
    for c in range(CHUNKS):
        part = pl.ds(c * chunk, chunk)
        for k, (source, dest) in enumerate(((b_hbm, b_ref), (t_hbm, t_ref))):
            copy = pltpu.make_async_copy(source.at[part], dest.at[part], sems.at[k, c])
            copy.start()
            copies.append(copy)
    cross = tgram = bgram = jnp.zeros((n, n), F32)
    for c in range(CHUNKS):
        part = slice(c * chunk, (c + 1) * chunk)
        copies[2 * c].wait()
        copies[2 * c + 1].wait()
        b, t = b_ref[part, :], t_ref[part, :]
        b, bt, t, tt = halves(b), halves(b.T), halves(t), halves(t.T)
        cross += dot3(bt, t)
        tgram += dot3(tt, t)
        bgram += dot3(bt, b)
    row, col = iota((n, n), 0), iota((n, n), 1)
    packed = jnp.where(row < col, tgram, bgram)
    diag = row == col
    tdiag = jnp.sum(jnp.where(diag, tgram, 0.0), axis=0, keepdims=True)
    bdiag = jnp.sum(jnp.where(diag, bgram, 0.0), axis=0, keepdims=True)
    for c in range(2):
        half = slice(c * 128, (c + 1) * 128)
        pay[c * n : (c + 1) * n, :] = cross[:, half]
        pay[(2 + c) * n : (3 + c) * n, :] = packed[:, half]
    pay[4 * n :, :] = jnp.zeros((pay.shape[0] - 4 * n, 128), F32)
    for c in range(2):
        half = slice(c * 128, (c + 1) * 128)
        pay[4 * n + c : 4 * n + c + 1, :] = tdiag[:, half]
        pay[4 * n + 2 + c : 4 * n + 3 + c, :] = bdiag[:, half]
    half, core = keep_ref.shape[0], where_ref[0]
    keep_ref[...] = pay[pl.ds(pl.multiple_of(core * half, 8), half), :]
    send_ref[...] = pay[pl.ds(pl.multiple_of((1 - core) * half, 8), half), :]


def invert_blocks(v):
    group = iota((8, 128), 1) // NODES
    node = iota((8, 128), 1) % NODES
    row = iota((8, 128), 0)
    for g in range(4):
        q, first = g // 2, g % 2 * 8
        pan = []
        for p in range(8):
            index = node + (first + p) * NODES
            pan.append([jnp.take_along_axis(x, index, axis=1) for x in v[q]])
        for p in range(8):
            pivot = pan[p][g][p : p + 1, :]
            recip = pl.reciprocal(pivot, approx=True)
            recip = recip * (2.0 - pivot * recip)
            new = [x for x in pan[p]]
            new[g] = jnp.where(row == p, 1.0, new[g])
            new = [x * recip for x in new]
            pan[p] = new
            for o in range(8):
                if o != p:
                    factor = pan[o][g][p : p + 1, :]
                    old = [x for x in pan[o]]
                    old[g] = jnp.where(row == p, 0.0, old[g])
                    pan[o] = [x - factor * y for x, y in zip(old, new)]
        for o in range(2):
            acc = [x for x in v[o]]
            acc[g] = jnp.zeros((8, 128), F32)
            for p in range(8):
                factor = v[o][g][p : p + 1, :]
                acc = [x - factor * y for x, y in zip(acc, pan[p])]
            if o == q:
                for p in range(8):
                    acc = [jnp.where(group == first + p, y, x) for x, y in zip(acc, pan[p])]
            v[o] = acc
    return v


def resolvent_kernel(
    where_ref, shift_ref, weight_ref, mine_ref, other_ref, out_ref, cross_ref, mats, turned, inverses, news, pay
):
    n = out_ref.shape[1]
    half, core = mine_ref.shape[0], where_ref[0]
    pay[pl.ds(pl.multiple_of(core * half, 8), half), :] = mine_ref[...]
    pay[pl.ds(pl.multiple_of((1 - core) * half, 8), half), :] = other_ref[...]
    row, col = iota((n, n), 0), iota((n, n), 1)

    def wide(start, rows):
        return jnp.concatenate([pay[start : start + rows, :], pay[start + rows : start + 2 * rows, :]], 1)

    cross, packed = wide(0, n), wide(2 * n, n)
    cross_ref[...] = cross
    tdiag, bdiag = wide(4 * n, 1), wide(4 * n + 2, 1)
    upper = jnp.where(row < col, packed, 0.0)
    lower = jnp.where(row > col, packed, 0.0)
    tgram = upper + upper.T + jnp.where(row == col, tdiag, 0.0)
    bgram = lower + lower.T + jnp.where(row == col, bdiag, 0.0)
    crosst = cross.T
    square = dot(crosst, cross)
    normal = tgram - 2.0 * square + dot(crosst, dot(bgram, cross))
    for m in range(NODES):
        shifted = square + shift_ref[core * NODES + m] * normal
        mats[0, m * n : (m + 1) * n, :] = shifted[:, 0:128]
        mats[1, m * n : (m + 1) * n, :] = shifted[:, 128:256]

    def stack(x):
        h, m, l = split(x)
        return jnp.concatenate([h, m, h, l, h, m, l, m], 0).astype(BF16)

    def step(tile, part, carry):
        inner = pl.multiple_of(part * STEP, STEP)
        start = pl.multiple_of(tile * 128 + inner, STEP)
        v = []
        for q in range(2):
            rows = [mats[tile, pl.ds(start + 16 * q + i, NODES, stride=n), :] for i in range(16)]
            turned[q] = jnp.concatenate(rows, 0).T
            block = turned[q, pl.ds(inner, STEP), :]
            v.append([block[8 * g : 8 * g + 8] for g in range(4)])
        v = invert_blocks(v)
        for q in range(2):
            h, m, l = split(jnp.concatenate(v[q], 0))
            inverses[0, q * 128 : (q + 1) * 128, :] = jnp.concatenate([h, h, m, h], 0).T
            inverses[1, q * 128 : (q + 1) * 128, :] = jnp.concatenate([l, m, m, l], 0).T

        local = iota((STEP, n), 1) - start
        inblock = (local >= 0) & (local < STEP)
        minus = jnp.where(local == iota((STEP, n), 0), -1.0, 0.0)
        for m in range(NODES):
            left = [inverses[c, pl.ds(m, STEP, stride=NODES), :] for c in range(2)]
            left = jnp.concatenate(left, 1).astype(BF16)
            here = pl.ds(pl.multiple_of(m * n + start, STEP), STEP)
            panel = jnp.concatenate([mats[0, here, :], mats[1, here, :]], 1)
            panel = jnp.where(inblock, minus, panel)
            news[m] = jnp.dot(left, stack(panel), preferred_element_type=F32)
        for m in range(NODES):
            rows = slice(m * n, (m + 1) * n)
            here = pl.ds(pl.multiple_of(m * n + start, STEP), STEP)
            h, d, l = split(jnp.concatenate([mats[0, here, :], mats[1, here, :]], 1))
            lhs = jnp.concatenate([h, h, d, h, l, d, d, l], 0).astype(BF16)
            change = lax.dot_general(
                lhs, stack(news[m]), (((0,), (0,)), ((), ())), preferred_element_type=F32
            )
            for c in range(2):
                half = slice(c * 128, (c + 1) * 128)
                old = mats[c, rows, :]
                if c == tile:
                    old = jnp.where(inblock[0:1, half], 0.0, old)
                mats[c, rows, :] = old - change[:, half]
        for m in range(NODES):
            here = pl.ds(pl.multiple_of(m * n + start, STEP), STEP)
            mats[0, here, :] = news[m, :, 0:128]
            mats[1, here, :] = news[m, :, 128:256]
        return carry

    for tile in range(2):
        lax.fori_loop(0, 4, functools.partial(step, tile), 0)
    for c in range(2):
        half = weight_ref[core * NODES] * mats[c, 0:n, :]
        for m in range(1, NODES):
            half = half + weight_ref[core * NODES + m] * mats[c, m * n : (m + 1) * n, :]
        out_ref[:, c * 128 : (c + 1) * 128] = half


def residual_kernel(cross_ref, b_ref, t_ref, high_ref, low_ref):
    z = t_ref[...] - dot3(halves(b_ref[...]), halves(cross_ref[...]))
    high_ref[...], low_ref[...] = halves(z)


def lift_kernel(scale, mine_ref, other_ref, cross_ref, high_ref, low_ref, out_hbm, out_ref, sems):
    rows = high_ref.shape[0] // CHUNKS
    total = (mine_ref[...] + other_ref[...]) * -scale
    right = halves(dot3(halves(total), halves(cross_ref[...].T)))
    copies = []
    for c in range(CHUNKS):
        part = pl.ds(c * rows, rows)
        out_ref[part, :] = dot3((high_ref[part, :], low_ref[part, :]), right)
        copies.append(pltpu.make_async_copy(out_ref.at[part], out_hbm.at[part], sems.at[c]))
        copies[-1].start()
    for copy in copies:
        copy.wait()


def swap_cores(x):
    return lax.ppermute(x, "gz", [(0, 1), (1, 0)])


def swap_bits(x, mesh, gx, gy):
    ny, nz = mesh.shape["gy"], mesh.shape["gz"]
    perm = []
    for i in range(mesh.size):
        x0, y0, z0 = i // (ny * nz), i // nz % ny, i % nz
        perm.append((i, ((x0 ^ gx) * ny + (y0 ^ gy)) * nz + z0))
    return lax.ppermute(x, ("gx", "gy", "gz"), perm)


def summed(x, mesh):
    nx, ny = mesh.shape["gx"], mesh.shape["gy"]
    low = [(a, b) for a in range(4) for b in range(2)]
    groups = [
        [(gx + a) * ny + gy + b for a, b in low] for gx in range(0, nx, 4) for gy in range(0, ny, 2)
    ]

    def cube(pieces):
        return lax.all_to_all(
            pieces, ("gx", "gy"), 0, 0, axis_index_groups=groups, tiled=True
        )

    x = jnp.sum(cube(x).reshape(CUBE, -1, x.shape[1]), axis=0)
    for bit in range(2, (nx - 1).bit_length()):
        x = x + swap_bits(x, mesh, 1 << bit, 0)
    for bit in range(1, (ny - 1).bit_length()):
        x = x + swap_bits(x, mesh, 0, 1 << bit)
    return cube(jnp.tile(x, (CUBE, 1)))


def on_device(basis, target, mesh):
    rows, n = basis.shape
    total_rows = rows * mesh.size
    pay_half = -(-(2 * n + 8) // (8 * CUBE)) * 8 * CUBE
    vmem = pl.BlockSpec(memory_space=pltpu.VMEM)
    smem = pl.BlockSpec(memory_space=pltpu.SMEM)
    hbm = pl.BlockSpec(memory_space=pltpu.HBM)
    limit = pltpu.CompilerParams(vmem_limit_bytes=48 * 1024 * 1024)
    core = lax.axis_index("gz")
    where = jnp.reshape(core, (1,)).astype(jnp.int32)
    half = jax.ShapeDtypeStruct((pay_half, 128), F32)
    keep, send = pl.pallas_call(
        gram_kernel,
        out_shape=(half, half),
        in_specs=[smem, hbm, hbm],
        out_specs=(vmem, vmem),
        scratch_shapes=[
            pltpu.VMEM((rows, n), F32),
            pltpu.VMEM((rows, n), F32),
            pltpu.VMEM((2 * pay_half, 128), F32),
            pltpu.SemaphoreType.DMA((2, CHUNKS)),
        ],
        compiler_params=pltpu.CompilerParams(vmem_limit_bytes=GRANT),
    )(where, basis, target)
    mine = summed(keep + swap_cores(send), mesh)
    other = swap_cores(mine)
    square = jax.ShapeDtypeStruct((n, n), F32)
    part, cross = pl.pallas_call(
        resolvent_kernel,
        out_shape=(square, square),
        in_specs=[smem, smem, smem, vmem, vmem],
        out_specs=(vmem, vmem),
        scratch_shapes=[
            pltpu.VMEM((2, NODES * n, 128), F32),
            pltpu.VMEM((2, 128, 128), F32),
            pltpu.VMEM((2, 2 * 128, 128), F32),
            pltpu.VMEM((NODES, STEP, n), F32),
            pltpu.VMEM((2 * pay_half, 128), F32),
        ],
        compiler_params=limit,
        cost_estimate=pl.CostEstimate(flops=10**11, bytes_accessed=10**6, transcendentals=0),
    )(where, jnp.asarray(points**2, F32), jnp.asarray(weights, F32), mine, other)
    other = swap_cores(part)
    high, low = pl.pallas_call(
        residual_kernel,
        out_shape=(jax.ShapeDtypeStruct((rows, n), BF16),) * 2,
        in_specs=[vmem, vmem, vmem],
        out_specs=(vmem, vmem),
        compiler_params=limit,
        cost_estimate=pl.CostEstimate(flops=10**9, bytes_accessed=3 * 10**6, transcendentals=0),
    )(cross, basis, target)
    return pl.pallas_call(
        functools.partial(lift_kernel, float(np.sqrt(total_rows))),
        out_shape=jax.ShapeDtypeStruct((rows, n), F32),
        in_specs=[vmem] * 5,
        out_specs=hbm,
        scratch_shapes=[pltpu.VMEM((rows, n), F32), pltpu.SemaphoreType.DMA((CHUNKS,))],
        compiler_params=limit,
    )(part, other, cross, high, low)


def solution(mesh):
    return jax.shard_map(
        functools.partial(on_device, mesh=mesh),
        mesh=mesh,
        in_specs=(P(("gx", "gy", "gz"), None), P(("gx", "gy", "gz"), None)),
        out_specs=P(("gx", "gy", "gz"), None),
        check_vma=False,
    )
```

```python
import functools

import jax
import jax.numpy as jnp
import numpy as np
from jax import lax
from jax.experimental import pallas as pl
from jax.experimental.pallas import tpu as pltpu
from jax.sharding import PartitionSpec as P

half_points = [
    0.0950125098376374,
    0.2816035507792589,
    0.4580167776572274,
    0.6178762444026438,
    0.755404408355003,
    0.8656312023878318,
    0.9445750230732326,
    0.9894009349916499,
]
half_weights = [
    0.1894506104550685,
    0.1826034150449236,
    0.1691565193950025,
    0.1495959888165767,
    0.1246289712555339,
    0.0951585116824928,
    0.0622535239386479,
    0.0271524594117541,
]
points = (np.array([-v for v in half_points[::-1]] + half_points) + 1.0) / 2.0
weights = np.array(half_weights[::-1] + half_weights) / 2.0
NODES = 8
CHUNKS = 4
CUBE = 8
GRANT = 53 * 1024 * 1024
STEP = 32
F32 = jnp.float32
BF16 = jnp.bfloat16
highest = lax.Precision.HIGHEST


def iota(shape, dim):
    return lax.broadcasted_iota(jnp.int32, shape, dim)


def split(x):
    high = x.astype(BF16).astype(F32)
    rest = x - high
    mid = rest.astype(BF16).astype(F32)
    return high, mid, rest - mid


def dot(a, b):
    return jnp.dot(a, b, precision=highest, preferred_element_type=F32)


def halves(x):
    high = x.astype(BF16)
    return high, (x - high.astype(F32)).astype(BF16)


def dot3(a, b):
    (ah, al), (bh, bl) = a, b
    total = jnp.dot(ah, bl, preferred_element_type=F32) + jnp.dot(al, bh, preferred_element_type=F32)
    return total + jnp.dot(ah, bh, preferred_element_type=F32)


def gram_kernel(where_ref, b_hbm, t_hbm, keep_ref, send_ref, b_ref, t_ref, pay, sems):
    rows, n = b_ref.shape
    chunk = rows // CHUNKS
    copies = []
    for c in range(CHUNKS):
        part = pl.ds(c * chunk, chunk)
        for k, (source, dest) in enumerate(((b_hbm, b_ref), (t_hbm, t_ref))):
            copy = pltpu.make_async_copy(source.at[part], dest.at[part], sems.at[k, c])
            copy.start()
            copies.append(copy)
    cross = tgram = bgram = jnp.zeros((n, n), F32)
    for c in range(CHUNKS):
        part = slice(c * chunk, (c + 1) * chunk)
        copies[2 * c].wait()
        copies[2 * c + 1].wait()
        b, t = b_ref[part, :], t_ref[part, :]
        b, bt, t, tt = halves(b), halves(b.T), halves(t), halves(t.T)
        cross += dot3(bt, t)
        tgram += dot3(tt, t)
        bgram += dot3(bt, b)
    row, col = iota((n, n), 0), iota((n, n), 1)
    packed = jnp.where(row < col, tgram, bgram)
    diag = row == col
    tdiag = jnp.sum(jnp.where(diag, tgram, 0.0), axis=0, keepdims=True)
    bdiag = jnp.sum(jnp.where(diag, bgram, 0.0), axis=0, keepdims=True)
    for c in range(2):
        half = slice(c * 128, (c + 1) * 128)
        pay[c * n : (c + 1) * n, :] = cross[:, half]
        pay[(2 + c) * n : (3 + c) * n, :] = packed[:, half]
    pay[4 * n :, :] = jnp.zeros((pay.shape[0] - 4 * n, 128), F32)
    for c in range(2):
        half = slice(c * 128, (c + 1) * 128)
        pay[4 * n + c : 4 * n + c + 1, :] = tdiag[:, half]
        pay[4 * n + 2 + c : 4 * n + 3 + c, :] = bdiag[:, half]
    half, core = keep_ref.shape[0], where_ref[0]
    keep_ref[...] = pay[pl.ds(pl.multiple_of(core * half, 8), half), :]
    send_ref[...] = pay[pl.ds(pl.multiple_of((1 - core) * half, 8), half), :]


def invert_blocks(v, between):
    group = iota((8, 128), 1) // NODES
    node = iota((8, 128), 1) % NODES
    row = iota((8, 128), 0)
    for g in range(4):
        q, first = g // 2, g % 2 * 8
        pan = []
        for p in range(8):
            index = node + (first + p) * NODES
            pan.append([jnp.take_along_axis(x, index, axis=1) for x in v[q]])
        for p in range(8):
            pivot = pan[p][g][p : p + 1, :]
            recip = pl.reciprocal(pivot, approx=True)
            recip = recip * (2.0 - pivot * recip)
            new = [x for x in pan[p]]
            new[g] = jnp.where(row == p, 1.0, new[g])
            new = [x * recip for x in new]
            pan[p] = new
            for o in range(8):
                if o != p:
                    factor = pan[o][g][p : p + 1, :]
                    old = [x for x in pan[o]]
                    old[g] = jnp.where(row == p, 0.0, old[g])
                    pan[o] = [x - factor * y for x, y in zip(old, new)]
        for o in range(2):
            acc = [x for x in v[o]]
            acc[g] = jnp.zeros((8, 128), F32)
            for p in range(8):
                factor = v[o][g][p : p + 1, :]
                acc = [x - factor * y for x, y in zip(acc, pan[p])]
            if o == q:
                for p in range(8):
                    acc = [jnp.where(group == first + p, y, x) for x, y in zip(acc, pan[p])]
            v[o] = acc
        between[g]()
    return v


def resolvent_kernel(
    where_ref, shift_ref, weight_ref, mine_ref, other_ref, out_ref, cross_ref, pay, blocks, turned, inverses, news, *mats
):
    n = out_ref.shape[1]
    last = n // STEP - 1
    half, core = mine_ref.shape[0], where_ref[0]
    pay[pl.ds(pl.multiple_of(core * half, 8), half), :] = mine_ref[...]
    pay[pl.ds(pl.multiple_of((1 - core) * half, 8), half), :] = other_ref[...]
    row, col = iota((n, n), 0), iota((n, n), 1)

    def wide(start, rows):
        return jnp.concatenate([pay[start : start + rows, :], pay[start + rows : start + 2 * rows, :]], 1)

    cross, packed = wide(0, n), wide(2 * n, n)
    cross_ref[...] = cross
    tdiag, bdiag = wide(4 * n, 1), wide(4 * n + 2, 1)
    upper = jnp.where(row < col, packed, 0.0)
    lower = jnp.where(row > col, packed, 0.0)
    tgram = upper + upper.T + jnp.where(row == col, tdiag, 0.0)
    bgram = lower + lower.T + jnp.where(row == col, bdiag, 0.0)
    crosst = cross.T
    square = dot(crosst, cross)
    normal = tgram - 2.0 * square + dot(crosst, dot(bgram, cross))
    for m in range(NODES):
        shifted = square + shift_ref[core * NODES + m] * normal
        mats[m][0] = shifted[:, 0:128]
        mats[m][1] = shifted[:, 128:256]
        blocks[m * STEP : (m + 1) * STEP, :] = shifted[0:STEP, 0:128]

    def stack(x):
        h, m, l = split(x)
        return jnp.concatenate([h, m, h, l, h, m, l, m], 0).astype(BF16)

    def spread(x, first):
        lane = iota(x.shape, 1)
        group = lane // STEP
        h, d, l = split(jnp.take_along_axis(x, lane % STEP + first, axis=1))
        one = jnp.where(group == 2, d, h)
        two = jnp.where((group == 0) | (group == 3), l, d)
        return jnp.concatenate([one, two], 1).astype(BF16)

    def place(kb):
        return kb // 4, pl.multiple_of(kb % 4 * STEP, STEP), pl.ds(pl.multiple_of(kb * STEP, STEP), STEP)

    def columns_of(kb):
        local = iota((STEP, n), 1) - kb * STEP
        return local, (local >= 0) & (local < STEP)

    def update(kb, m):
        tile, first, here = place(kb)
        local, inblock = columns_of(kb)
        new = jnp.concatenate([news[m, 0], news[m, 1]], 1)
        change = jnp.dot(spread(mats[m][tile], first), stack(new), preferred_element_type=F32)
        for c in range(2):
            part = slice(c * 128, (c + 1) * 128)
            mats[m][c] = jnp.where(inblock[0:1, part], 0.0, mats[m][c]) - change[:, part]
        for c in range(2):
            mats[m][c, here, :] = news[m, c]

    def pivots(kb, work):
        tile, first, here = place(kb)
        v = []
        for q in range(2):
            rows = [blocks[pl.ds(16 * q + i, NODES, stride=STEP), :] for i in range(16)]
            turned[q] = jnp.concatenate(rows, 0).T
            block = turned[q, pl.ds(first, STEP), :]
            v.append([block[8 * g : 8 * g + 8] for g in range(4)])
        v = invert_blocks(v, work)
        for q in range(2):
            inverses[q * 128 : (q + 1) * 128, 0:STEP] = jnp.concatenate(v[q], 0).T
        local, inblock = columns_of(kb)
        minus = jnp.where(local == iota((STEP, n), 0), -1.0, 0.0)
        for m in range(NODES):
            left = spread(inverses[pl.ds(m, STEP, stride=NODES), :], 0)
            panel = jnp.concatenate([mats[m][0, here, :], mats[m][1, here, :]], 1)
            panel = jnp.where(inblock, minus, panel)
            new = jnp.dot(left, stack(panel), preferred_element_type=F32)
            news[m, 0] = new[:, 0:128]
            news[m, 1] = new[:, 128:256]
        tile1, _, here1 = place(jnp.minimum(kb + 1, last))
        for m in range(NODES):
            left = spread(mats[m][tile, here1, :], first)
            change = jnp.dot(left, stack(news[m, tile1]), preferred_element_type=F32)
            blocks[m * STEP : (m + 1) * STEP, :] = mats[m][tile1, here1, :] - change

    def step(kb, carry):
        def updates(g):
            for m in range(2 * g, 2 * g + 2):
                update(kb - 1, m)

        pivots(kb, [functools.partial(updates, g) for g in range(4)])
        return carry

    pivots(jnp.int32(0), [lambda: None] * 4)
    lax.fori_loop(1, last + 1, step, 0)
    for m in range(NODES):
        update(jnp.int32(last), m)
    for c in range(2):
        total = weight_ref[core * NODES] * mats[0][c]
        for m in range(1, NODES):
            total = total + weight_ref[core * NODES + m] * mats[m][c]
        out_ref[:, c * 128 : (c + 1) * 128] = total


def residual_kernel(cross_ref, b_ref, t_ref, high_ref, low_ref):
    z = t_ref[...] - dot3(halves(b_ref[...]), halves(cross_ref[...]))
    high_ref[...], low_ref[...] = halves(z)


def lift_kernel(scale, mine_ref, other_ref, cross_ref, high_ref, low_ref, out_hbm, out_ref, sems):
    rows = high_ref.shape[0] // CHUNKS
    total = (mine_ref[...] + other_ref[...]) * -scale
    right = halves(dot3(halves(total), halves(cross_ref[...].T)))
    copies = []
    for c in range(CHUNKS):
        part = pl.ds(c * rows, rows)
        out_ref[part, :] = dot3((high_ref[part, :], low_ref[part, :]), right)
        copies.append(pltpu.make_async_copy(out_ref.at[part], out_hbm.at[part], sems.at[c]))
        copies[-1].start()
    for copy in copies:
        copy.wait()


def swap_cores(x):
    return lax.ppermute(x, "gz", [(0, 1), (1, 0)])


def swap_bits(x, mesh, gx, gy):
    ny, nz = mesh.shape["gy"], mesh.shape["gz"]
    perm = []
    for i in range(mesh.size):
        x0, y0, z0 = i // (ny * nz), i // nz % ny, i % nz
        perm.append((i, ((x0 ^ gx) * ny + (y0 ^ gy)) * nz + z0))
    return lax.ppermute(x, ("gx", "gy", "gz"), perm)


def summed(x, mesh):
    nx, ny = mesh.shape["gx"], mesh.shape["gy"]
    low = [(a, b) for a in range(4) for b in range(2)]
    groups = [
        [(gx + a) * ny + gy + b for a, b in low] for gx in range(0, nx, 4) for gy in range(0, ny, 2)
    ]

    def cube(pieces):
        return lax.all_to_all(
            pieces, ("gx", "gy"), 0, 0, axis_index_groups=groups, tiled=True
        )

    x = jnp.sum(cube(x).reshape(CUBE, -1, x.shape[1]), axis=0)
    for bit in range(2, (nx - 1).bit_length()):
        x = x + swap_bits(x, mesh, 1 << bit, 0)
    for bit in range(1, (ny - 1).bit_length()):
        x = x + swap_bits(x, mesh, 0, 1 << bit)
    return cube(jnp.tile(x, (CUBE, 1)))


def on_device(basis, target, mesh):
    rows, n = basis.shape
    total_rows = rows * mesh.size
    pay_half = -(-(2 * n + 8) // (8 * CUBE)) * 8 * CUBE
    vmem = pl.BlockSpec(memory_space=pltpu.VMEM)
    smem = pl.BlockSpec(memory_space=pltpu.SMEM)
    hbm = pl.BlockSpec(memory_space=pltpu.HBM)
    limit = pltpu.CompilerParams(vmem_limit_bytes=48 * 1024 * 1024)
    core = lax.axis_index("gz")
    where = jnp.reshape(core, (1,)).astype(jnp.int32)
    half = jax.ShapeDtypeStruct((pay_half, 128), F32)
    keep, send = pl.pallas_call(
        gram_kernel,
        out_shape=(half, half),
        in_specs=[smem, hbm, hbm],
        out_specs=(vmem, vmem),
        scratch_shapes=[
            pltpu.VMEM((rows, n), F32),
            pltpu.VMEM((rows, n), F32),
            pltpu.VMEM((2 * pay_half, 128), F32),
            pltpu.SemaphoreType.DMA((2, CHUNKS)),
        ],
        compiler_params=pltpu.CompilerParams(vmem_limit_bytes=GRANT),
    )(where, basis, target)
    mine = summed(keep + swap_cores(send), mesh)
    other = swap_cores(mine)
    square = jax.ShapeDtypeStruct((n, n), F32)
    part, cross = pl.pallas_call(
        resolvent_kernel,
        out_shape=(square, square),
        in_specs=[smem, smem, smem, vmem, vmem],
        out_specs=(vmem, vmem),
        scratch_shapes=[
            pltpu.VMEM((2 * pay_half, 128), F32),
            pltpu.VMEM((NODES * STEP, 128), F32),
            pltpu.VMEM((2, 128, 128), F32),
            pltpu.VMEM((2 * 128, 128), F32),
            pltpu.VMEM((NODES, 2, STEP, 128), F32),
        ]
        + [pltpu.VMEM((2, n, 128), F32)] * NODES,
        compiler_params=limit,
        cost_estimate=pl.CostEstimate(flops=10**11, bytes_accessed=10**6, transcendentals=0),
    )(where, jnp.asarray(points**2, F32), jnp.asarray(weights, F32), mine, other)
    other = swap_cores(part)
    high, low = pl.pallas_call(
        residual_kernel,
        out_shape=(jax.ShapeDtypeStruct((rows, n), BF16),) * 2,
        in_specs=[vmem, vmem, vmem],
        out_specs=(vmem, vmem),
        compiler_params=limit,
        cost_estimate=pl.CostEstimate(flops=10**9, bytes_accessed=3 * 10**6, transcendentals=0),
    )(cross, basis, target)
    return pl.pallas_call(
        functools.partial(lift_kernel, float(np.sqrt(total_rows))),
        out_shape=jax.ShapeDtypeStruct((rows, n), F32),
        in_specs=[vmem] * 5,
        out_specs=hbm,
        scratch_shapes=[pltpu.VMEM((rows, n), F32), pltpu.SemaphoreType.DMA((CHUNKS,))],
        compiler_params=limit,
    )(part, other, cross, high, low)


def solution(mesh):
    return jax.shard_map(
        functools.partial(on_device, mesh=mesh),
        mesh=mesh,
        in_specs=(P(("gx", "gy", "gz"), None), P(("gx", "gy", "gz"), None)),
        out_specs=P(("gx", "gy", "gz"), None),
        check_vma=False,
    )
```

```python
import functools

import jax
import jax.numpy as jnp
import numpy as np
from jax import lax
from jax.experimental import pallas as pl
from jax.experimental.pallas import tpu as pltpu
from jax.sharding import PartitionSpec as P

half_points = [
    0.0950125098376374,
    0.2816035507792589,
    0.4580167776572274,
    0.6178762444026438,
    0.755404408355003,
    0.8656312023878318,
    0.9445750230732326,
    0.9894009349916499,
]
half_weights = [
    0.1894506104550685,
    0.1826034150449236,
    0.1691565193950025,
    0.1495959888165767,
    0.1246289712555339,
    0.0951585116824928,
    0.0622535239386479,
    0.0271524594117541,
]
points = (np.array([-v for v in half_points[::-1]] + half_points) + 1.0) / 2.0
weights = np.array(half_weights[::-1] + half_weights) / 2.0
NODES = 8
CHUNKS = 4
CUBE = 8
GRANT = 53 * 1024 * 1024
STEP = 32
F32 = jnp.float32
BF16 = jnp.bfloat16
highest = lax.Precision.HIGHEST


def iota(shape, dim):
    return lax.broadcasted_iota(jnp.int32, shape, dim)


def split(x):
    high = x.astype(BF16).astype(F32)
    rest = x - high
    mid = rest.astype(BF16).astype(F32)
    return high, mid, rest - mid


def dot(a, b):
    return jnp.dot(a, b, precision=highest, preferred_element_type=F32)


def halves(x):
    high = x.astype(BF16)
    return high, (x - high.astype(F32)).astype(BF16)


def dot3(a, b):
    (ah, al), (bh, bl) = a, b
    total = jnp.dot(ah, bl, preferred_element_type=F32) + jnp.dot(al, bh, preferred_element_type=F32)
    return total + jnp.dot(ah, bh, preferred_element_type=F32)


def gram_kernel(where_ref, b_hbm, t_hbm, keep_ref, send_ref, b_ref, t_ref, pay, sems):
    rows, n = b_ref.shape
    chunk = rows // CHUNKS
    copies = []
    for c in range(CHUNKS):
        part = pl.ds(c * chunk, chunk)
        for k, (source, dest) in enumerate(((b_hbm, b_ref), (t_hbm, t_ref))):
            copy = pltpu.make_async_copy(source.at[part], dest.at[part], sems.at[k, c])
            copy.start()
            copies.append(copy)
    cross = tgram = bgram = jnp.zeros((n, n), F32)
    for c in range(CHUNKS):
        part = slice(c * chunk, (c + 1) * chunk)
        copies[2 * c].wait()
        copies[2 * c + 1].wait()
        b, t = b_ref[part, :], t_ref[part, :]
        b, bt, t, tt = halves(b), halves(b.T), halves(t), halves(t.T)
        cross += dot3(bt, t)
        tgram += dot3(tt, t)
        bgram += dot3(bt, b)
    row, col = iota((n, n), 0), iota((n, n), 1)
    packed = jnp.where(row < col, tgram, bgram)
    diag = row == col
    tdiag = jnp.sum(jnp.where(diag, tgram, 0.0), axis=0, keepdims=True)
    bdiag = jnp.sum(jnp.where(diag, bgram, 0.0), axis=0, keepdims=True)
    for c in range(2):
        half = slice(c * 128, (c + 1) * 128)
        pay[c * n : (c + 1) * n, :] = cross[:, half]
        pay[(2 + c) * n : (3 + c) * n, :] = packed[:, half]
    pay[4 * n :, :] = jnp.zeros((pay.shape[0] - 4 * n, 128), F32)
    for c in range(2):
        half = slice(c * 128, (c + 1) * 128)
        pay[4 * n + c : 4 * n + c + 1, :] = tdiag[:, half]
        pay[4 * n + 2 + c : 4 * n + 3 + c, :] = bdiag[:, half]
    half, core = keep_ref.shape[0], where_ref[0]
    keep_ref[...] = pay[pl.ds(pl.multiple_of(core * half, 8), half), :]
    send_ref[...] = pay[pl.ds(pl.multiple_of((1 - core) * half, 8), half), :]


def invert_blocks(v, between):
    group = iota((8, 128), 1) // NODES
    node = iota((8, 128), 1) % NODES
    row = iota((8, 128), 0)
    for g in range(4):
        q, first = g // 2, g % 2 * 8
        pan = []
        for p in range(8):
            index = node + (first + p) * NODES
            pan.append([jnp.take_along_axis(x, index, axis=1) for x in v[q]])
        for p in range(8):
            pivot = pan[p][g][p : p + 1, :]
            recip = pl.reciprocal(pivot, approx=True)
            recip = recip * (2.0 - pivot * recip)
            new = [x for x in pan[p]]
            new[g] = jnp.where(row == p, 1.0, new[g])
            new = [x * recip for x in new]
            pan[p] = new
            for o in range(8):
                if o != p:
                    factor = pan[o][g][p : p + 1, :]
                    old = [x for x in pan[o]]
                    old[g] = jnp.where(row == p, 0.0, old[g])
                    pan[o] = [x - factor * y for x, y in zip(old, new)]
            if p % 2:
                between[(8 * g + p) // 2]()
        for o in range(2):
            acc = [x for x in v[o]]
            acc[g] = jnp.zeros((8, 128), F32)
            for p in range(8):
                factor = v[o][g][p : p + 1, :]
                acc = [x - factor * y for x, y in zip(acc, pan[p])]
            if o == q:
                for p in range(8):
                    acc = [jnp.where(group == first + p, y, x) for x, y in zip(acc, pan[p])]
            v[o] = acc
    return v


def resolvent_kernel(
    where_ref, shift_ref, weight_ref, mine_ref, other_ref, out_ref, cross_ref, pay, blocks, turned, inverses, news, stacks, *mats
):
    n = out_ref.shape[1]
    last = n // STEP - 1
    half, core = mine_ref.shape[0], where_ref[0]
    pay[pl.ds(pl.multiple_of(core * half, 8), half), :] = mine_ref[...]
    pay[pl.ds(pl.multiple_of((1 - core) * half, 8), half), :] = other_ref[...]
    row, col = iota((n, n), 0), iota((n, n), 1)

    def wide(start, rows):
        return jnp.concatenate([pay[start : start + rows, :], pay[start + rows : start + 2 * rows, :]], 1)

    cross, packed = wide(0, n), wide(2 * n, n)
    cross_ref[...] = cross
    tdiag, bdiag = wide(4 * n, 1), wide(4 * n + 2, 1)
    upper = jnp.where(row < col, packed, 0.0)
    lower = jnp.where(row > col, packed, 0.0)
    tgram = upper + upper.T + jnp.where(row == col, tdiag, 0.0)
    bgram = lower + lower.T + jnp.where(row == col, bdiag, 0.0)
    crosst = cross.T
    square = dot(crosst, cross)
    normal = tgram - 2.0 * square + dot(crosst, dot(bgram, cross))
    for m in range(NODES):
        shifted = square + shift_ref[core * NODES + m] * normal
        mats[m][0] = shifted[:, 0:128]
        mats[m][1] = shifted[:, 128:256]
        blocks[m * STEP : (m + 1) * STEP, :] = shifted[0:STEP, 0:128]

    def stack(x):
        h, m, l = split(x)
        return jnp.concatenate([h, m, h, l, h, m, l, m], 0).astype(BF16)

    def spread(x, first):
        lane = iota(x.shape, 1)
        group = lane // STEP
        h, d, l = split(jnp.take_along_axis(x, lane % STEP + first, axis=1))
        one = jnp.where(group == 2, d, h)
        two = jnp.where((group == 0) | (group == 3), l, d)
        return jnp.concatenate([one, two], 1).astype(BF16)

    def place(kb):
        return kb // 4, pl.multiple_of(kb % 4 * STEP, STEP), pl.ds(pl.multiple_of(kb * STEP, STEP), STEP)

    def columns_of(kb):
        local = iota((STEP, n), 1) - kb * STEP
        return local, (local >= 0) & (local < STEP)

    def update(kb, m, side):
        tile, first, here = place(kb)
        local, inblock = columns_of(kb)
        rows = slice(side * 128, (side + 1) * 128)
        right = jnp.concatenate([stacks[m, 0], stacks[m, 1]], 1)
        change = jnp.dot(spread(mats[m][tile, rows, :], first), right, preferred_element_type=F32)
        for c in range(2):
            part = slice(c * 128, (c + 1) * 128)
            old = jnp.where(inblock[0:1, part], 0.0, mats[m][c, rows, :])
            mats[m][c, rows, :] = old - change[:, part]
        if side == 1:
            for c in range(2):
                mats[m][c, here, :] = news[m, c]

    def pivots(kb, work):
        tile, first, here = place(kb)
        v = []
        for q in range(2):
            rows = [blocks[pl.ds(16 * q + i, NODES, stride=STEP), :] for i in range(16)]
            turned[q] = jnp.concatenate(rows, 0).T
            block = turned[q, pl.ds(first, STEP), :]
            v.append([block[8 * g : 8 * g + 8] for g in range(4)])
        v = invert_blocks(v, work)
        for q in range(2):
            inverses[q * 128 : (q + 1) * 128, 0:STEP] = jnp.concatenate(v[q], 0).T
        local, inblock = columns_of(kb)
        minus = jnp.where(local == iota((STEP, n), 0), -1.0, 0.0)
        for m in range(NODES):
            left = spread(inverses[pl.ds(m, STEP, stride=NODES), :], 0)
            panel = jnp.concatenate([mats[m][0, here, :], mats[m][1, here, :]], 1)
            panel = jnp.where(inblock, minus, panel)
            new = jnp.dot(left, stack(panel), preferred_element_type=F32)
            for c in range(2):
                part = new[:, c * 128 : (c + 1) * 128]
                news[m, c] = part
                stacks[m, c] = stack(part)
        tile1, _, here1 = place(jnp.minimum(kb + 1, last))
        for m in range(NODES):
            left = spread(mats[m][tile, here1, :], first)
            change = jnp.dot(left, stacks[m, tile1], preferred_element_type=F32)
            blocks[m * STEP : (m + 1) * STEP, :] = mats[m][tile1, here1, :] - change

    def step(kb, carry):
        work = [functools.partial(update, kb - 1, m, side) for m in range(NODES) for side in range(2)]
        pivots(kb, work)
        return carry

    pivots(jnp.int32(0), [lambda: None] * 16)
    lax.fori_loop(1, last + 1, step, 0)
    for m in range(NODES):
        for side in range(2):
            update(jnp.int32(last), m, side)
    for c in range(2):
        total = weight_ref[core * NODES] * mats[0][c]
        for m in range(1, NODES):
            total = total + weight_ref[core * NODES + m] * mats[m][c]
        out_ref[:, c * 128 : (c + 1) * 128] = total


def residual_kernel(cross_ref, b_ref, t_ref, high_ref, low_ref):
    z = t_ref[...] - dot3(halves(b_ref[...]), halves(cross_ref[...]))
    high_ref[...], low_ref[...] = halves(z)


def lift_kernel(scale, mine_ref, other_ref, cross_ref, high_ref, low_ref, out_hbm, out_ref, sems):
    rows = high_ref.shape[0] // CHUNKS
    total = (mine_ref[...] + other_ref[...]) * -scale
    right = halves(dot3(halves(total), halves(cross_ref[...].T)))
    copies = []
    for c in range(CHUNKS):
        part = pl.ds(c * rows, rows)
        out_ref[part, :] = dot3((high_ref[part, :], low_ref[part, :]), right)
        copies.append(pltpu.make_async_copy(out_ref.at[part], out_hbm.at[part], sems.at[c]))
        copies[-1].start()
    for copy in copies:
        copy.wait()


def swap_cores(x):
    return lax.ppermute(x, "gz", [(0, 1), (1, 0)])


def swap_bits(x, mesh, gx, gy):
    ny, nz = mesh.shape["gy"], mesh.shape["gz"]
    perm = []
    for i in range(mesh.size):
        x0, y0, z0 = i // (ny * nz), i // nz % ny, i % nz
        perm.append((i, ((x0 ^ gx) * ny + (y0 ^ gy)) * nz + z0))
    return lax.ppermute(x, ("gx", "gy", "gz"), perm)


def summed(x, mesh):
    nx, ny = mesh.shape["gx"], mesh.shape["gy"]
    low = [(a, b) for a in range(4) for b in range(2)]
    groups = [
        [(gx + a) * ny + gy + b for a, b in low] for gx in range(0, nx, 4) for gy in range(0, ny, 2)
    ]

    def cube(pieces):
        return lax.all_to_all(
            pieces, ("gx", "gy"), 0, 0, axis_index_groups=groups, tiled=True
        )

    x = jnp.sum(cube(x).reshape(CUBE, -1, x.shape[1]), axis=0)
    for bit in range(2, (nx - 1).bit_length()):
        x = x + swap_bits(x, mesh, 1 << bit, 0)
    for bit in range(1, (ny - 1).bit_length()):
        x = x + swap_bits(x, mesh, 0, 1 << bit)
    return cube(jnp.tile(x, (CUBE, 1)))


def on_device(basis, target, mesh):
    rows, n = basis.shape
    total_rows = rows * mesh.size
    pay_half = -(-(2 * n + 8) // (8 * CUBE)) * 8 * CUBE
    vmem = pl.BlockSpec(memory_space=pltpu.VMEM)
    smem = pl.BlockSpec(memory_space=pltpu.SMEM)
    hbm = pl.BlockSpec(memory_space=pltpu.HBM)
    limit = pltpu.CompilerParams(vmem_limit_bytes=48 * 1024 * 1024)
    core = lax.axis_index("gz")
    where = jnp.reshape(core, (1,)).astype(jnp.int32)
    half = jax.ShapeDtypeStruct((pay_half, 128), F32)
    keep, send = pl.pallas_call(
        gram_kernel,
        out_shape=(half, half),
        in_specs=[smem, hbm, hbm],
        out_specs=(vmem, vmem),
        scratch_shapes=[
            pltpu.VMEM((rows, n), F32),
            pltpu.VMEM((rows, n), F32),
            pltpu.VMEM((2 * pay_half, 128), F32),
            pltpu.SemaphoreType.DMA((2, CHUNKS)),
        ],
        compiler_params=pltpu.CompilerParams(vmem_limit_bytes=GRANT),
    )(where, basis, target)
    mine = summed(keep + swap_cores(send), mesh)
    other = swap_cores(mine)
    square = jax.ShapeDtypeStruct((n, n), F32)
    part, cross = pl.pallas_call(
        resolvent_kernel,
        out_shape=(square, square),
        in_specs=[smem, smem, smem, vmem, vmem],
        out_specs=(vmem, vmem),
        scratch_shapes=[
            pltpu.VMEM((2 * pay_half, 128), F32),
            pltpu.VMEM((NODES * STEP, 128), F32),
            pltpu.VMEM((2, 128, 128), F32),
            pltpu.VMEM((2 * 128, 128), F32),
            pltpu.VMEM((NODES, 2, STEP, 128), F32),
            pltpu.VMEM((NODES, 2, 8 * STEP, 128), BF16),
        ]
        + [pltpu.VMEM((2, n, 128), F32)] * NODES,
        compiler_params=limit,
        cost_estimate=pl.CostEstimate(flops=10**11, bytes_accessed=10**6, transcendentals=0),
    )(where, jnp.asarray(points**2, F32), jnp.asarray(weights, F32), mine, other)
    other = swap_cores(part)
    high, low = pl.pallas_call(
        residual_kernel,
        out_shape=(jax.ShapeDtypeStruct((rows, n), BF16),) * 2,
        in_specs=[vmem, vmem, vmem],
        out_specs=(vmem, vmem),
        compiler_params=limit,
        cost_estimate=pl.CostEstimate(flops=10**9, bytes_accessed=3 * 10**6, transcendentals=0),
    )(cross, basis, target)
    return pl.pallas_call(
        functools.partial(lift_kernel, float(np.sqrt(total_rows))),
        out_shape=jax.ShapeDtypeStruct((rows, n), F32),
        in_specs=[vmem] * 5,
        out_specs=hbm,
        scratch_shapes=[pltpu.VMEM((rows, n), F32), pltpu.SemaphoreType.DMA((CHUNKS,))],
        compiler_params=limit,
    )(part, other, cross, high, low)


def solution(mesh):
    return jax.shard_map(
        functools.partial(on_device, mesh=mesh),
        mesh=mesh,
        in_specs=(P(("gx", "gy", "gz"), None), P(("gx", "gy", "gz"), None)),
        out_specs=P(("gx", "gy", "gz"), None),
        check_vma=False,
    )
```

```python
import functools

import jax
import jax.numpy as jnp
import numpy as np
from jax import lax
from jax.experimental import pallas as pl
from jax.experimental.pallas import tpu as pltpu
from jax.sharding import PartitionSpec as P

half_points = [
    0.0950125098376374,
    0.2816035507792589,
    0.4580167776572274,
    0.6178762444026438,
    0.755404408355003,
    0.8656312023878318,
    0.9445750230732326,
    0.9894009349916499,
]
half_weights = [
    0.1894506104550685,
    0.1826034150449236,
    0.1691565193950025,
    0.1495959888165767,
    0.1246289712555339,
    0.0951585116824928,
    0.0622535239386479,
    0.0271524594117541,
]
points = (np.array([-v for v in half_points[::-1]] + half_points) + 1.0) / 2.0
weights = np.array(half_weights[::-1] + half_weights) / 2.0
NODES = 8
CHUNKS = 4
CUBE = 8
GRANT = 53 * 1024 * 1024
STEP = 32
F32 = jnp.float32
BF16 = jnp.bfloat16
highest = lax.Precision.HIGHEST


def iota(shape, dim):
    return lax.broadcasted_iota(jnp.int32, shape, dim)


def split(x):
    high = x.astype(BF16).astype(F32)
    rest = x - high
    mid = rest.astype(BF16).astype(F32)
    return high, mid, rest - mid


def dot(a, b):
    return jnp.dot(a, b, precision=highest, preferred_element_type=F32)


def halves(x):
    high = x.astype(BF16)
    return high, (x - high.astype(F32)).astype(BF16)


def dot3(a, b):
    (ah, al), (bh, bl) = a, b
    total = jnp.dot(ah, bl, preferred_element_type=F32) + jnp.dot(al, bh, preferred_element_type=F32)
    return total + jnp.dot(ah, bh, preferred_element_type=F32)


def gram_kernel(where_ref, b_hbm, t_hbm, keep_ref, send_ref, b_ref, t_ref, pay, sems):
    rows, n = b_ref.shape
    chunk = rows // CHUNKS
    copies = []
    for c in range(CHUNKS):
        part = pl.ds(c * chunk, chunk)
        for k, (source, dest) in enumerate(((b_hbm, b_ref), (t_hbm, t_ref))):
            copy = pltpu.make_async_copy(source.at[part], dest.at[part], sems.at[k, c])
            copy.start()
            copies.append(copy)
    cross = tgram = bgram = jnp.zeros((n, n), F32)
    for c in range(CHUNKS):
        part = slice(c * chunk, (c + 1) * chunk)
        copies[2 * c].wait()
        copies[2 * c + 1].wait()
        b, t = b_ref[part, :], t_ref[part, :]
        b, bt, t, tt = halves(b), halves(b.T), halves(t), halves(t.T)
        cross += dot3(bt, t)
        tgram += dot3(tt, t)
        bgram += dot3(bt, b)
    row, col = iota((n, n), 0), iota((n, n), 1)
    packed = jnp.where(row < col, tgram, bgram)
    diag = row == col
    tdiag = jnp.sum(jnp.where(diag, tgram, 0.0), axis=0, keepdims=True)
    bdiag = jnp.sum(jnp.where(diag, bgram, 0.0), axis=0, keepdims=True)
    for c in range(2):
        half = slice(c * 128, (c + 1) * 128)
        pay[c * n : (c + 1) * n, :] = cross[:, half]
        pay[(2 + c) * n : (3 + c) * n, :] = packed[:, half]
    pay[4 * n :, :] = jnp.zeros((pay.shape[0] - 4 * n, 128), F32)
    for c in range(2):
        half = slice(c * 128, (c + 1) * 128)
        pay[4 * n + c : 4 * n + c + 1, :] = tdiag[:, half]
        pay[4 * n + 2 + c : 4 * n + 3 + c, :] = bdiag[:, half]
    half, core = keep_ref.shape[0], where_ref[0]
    keep_ref[...] = pay[pl.ds(pl.multiple_of(core * half, 8), half), :]
    send_ref[...] = pay[pl.ds(pl.multiple_of((1 - core) * half, 8), half), :]


def invert_blocks(v):
    group = iota((8, 128), 1) // NODES
    node = iota((8, 128), 1) % NODES
    row = iota((8, 128), 0)
    for g in range(4):
        q, first = g // 2, g % 2 * 8
        pan = []
        for p in range(8):
            index = node + (first + p) * NODES
            pan.append([jnp.take_along_axis(x, index, axis=1) for x in v[q]])
        for p in range(8):
            pivot = pan[p][g][p : p + 1, :]
            recip = pl.reciprocal(pivot, approx=True)
            recip = recip * (2.0 - pivot * recip)
            new = [x for x in pan[p]]
            new[g] = jnp.where(row == p, 1.0, new[g])
            new = [x * recip for x in new]
            pan[p] = new
            for o in range(8):
                if o != p:
                    factor = pan[o][g][p : p + 1, :]
                    old = [x for x in pan[o]]
                    old[g] = jnp.where(row == p, 0.0, old[g])
                    pan[o] = [x - factor * y for x, y in zip(old, new)]
        for o in range(2):
            acc = [x for x in v[o]]
            acc[g] = jnp.zeros((8, 128), F32)
            for p in range(8):
                factor = v[o][g][p : p + 1, :]
                acc = [x - factor * y for x, y in zip(acc, pan[p])]
            if o == q:
                for p in range(8):
                    acc = [jnp.where(group == first + p, y, x) for x, y in zip(acc, pan[p])]
            v[o] = acc
    return v


def resolvent_kernel(
    where_ref, shift_ref, weight_ref, mine_ref, other_ref, out_ref, cross_ref, mats, turned, inverses, news, pay
):
    n = out_ref.shape[1]
    half, core = mine_ref.shape[0], where_ref[0]
    pay[pl.ds(pl.multiple_of(core * half, 8), half), :] = mine_ref[...]
    pay[pl.ds(pl.multiple_of((1 - core) * half, 8), half), :] = other_ref[...]
    row, col = iota((n, n), 0), iota((n, n), 1)

    def wide(start, rows):
        return jnp.concatenate([pay[start : start + rows, :], pay[start + rows : start + 2 * rows, :]], 1)

    cross, packed = wide(0, n), wide(2 * n, n)
    cross_ref[...] = cross
    tdiag, bdiag = wide(4 * n, 1), wide(4 * n + 2, 1)
    upper = jnp.where(row < col, packed, 0.0)
    lower = jnp.where(row > col, packed, 0.0)
    tgram = upper + upper.T + jnp.where(row == col, tdiag, 0.0)
    bgram = lower + lower.T + jnp.where(row == col, bdiag, 0.0)
    crosst = cross.T
    square = dot(crosst, cross)
    normal = tgram - 2.0 * square + dot(crosst, dot(bgram, cross))
    for m in range(NODES):
        shifted = square + shift_ref[core * NODES + m] * normal
        mats[0, m * n : (m + 1) * n, :] = shifted[:, 0:128]
        mats[1, m * n : (m + 1) * n, :] = shifted[:, 128:256]

    def stack(x):
        h, m, l = split(x)
        return jnp.concatenate([h, m, h, l, h, m], 0).astype(BF16)

    def spread(x, first):
        lane = iota(x.shape, 1)
        group = lane // STEP
        h, d, l = split(jnp.take_along_axis(x, lane % STEP + first, axis=1))
        one = jnp.where(group == 2, d, h).astype(BF16)
        two = jnp.where(group == 0, l, d).astype(BF16)
        return jnp.concatenate([one, two[:, : 2 * STEP]], 1)

    def step(tile, part, carry):
        inner = pl.multiple_of(part * STEP, STEP)
        start = pl.multiple_of(tile * 128 + inner, STEP)
        v = []
        for q in range(2):
            rows = [mats[tile, pl.ds(start + 16 * q + i, NODES, stride=n), :] for i in range(16)]
            turned[q] = jnp.concatenate(rows, 0).T
            block = turned[q, pl.ds(inner, STEP), :]
            v.append([block[8 * g : 8 * g + 8] for g in range(4)])
        v = invert_blocks(v)
        for q in range(2):
            inverses[q * 128 : (q + 1) * 128, 0:STEP] = jnp.concatenate(v[q], 0).T

        local = iota((STEP, n), 1) - start
        inblock = (local >= 0) & (local < STEP)
        minus = jnp.where(local == iota((STEP, n), 0), -1.0, 0.0)
        for m in range(NODES):
            left = spread(inverses[pl.ds(m, STEP, stride=NODES), :], 0)
            here = pl.ds(pl.multiple_of(m * n + start, STEP), STEP)
            panel = jnp.concatenate([mats[0, here, :], mats[1, here, :]], 1)
            panel = jnp.where(inblock, minus, panel)
            news[m] = jnp.dot(left, stack(panel), preferred_element_type=F32)
        for m in range(NODES):
            rows = slice(m * n, (m + 1) * n)
            left = spread(mats[tile, rows, :], inner)
            change = jnp.dot(left, stack(news[m]), preferred_element_type=F32)
            for c in range(2):
                half = slice(c * 128, (c + 1) * 128)
                old = mats[c, rows, :]
                if c == tile:
                    old = jnp.where(inblock[0:1, half], 0.0, old)
                mats[c, rows, :] = old - change[:, half]
        for m in range(NODES):
            here = pl.ds(pl.multiple_of(m * n + start, STEP), STEP)
            mats[0, here, :] = news[m, :, 0:128]
            mats[1, here, :] = news[m, :, 128:256]
        return carry

    for tile in range(2):
        lax.fori_loop(0, 4, functools.partial(step, tile), 0)
    for c in range(2):
        half = weight_ref[core * NODES] * mats[c, 0:n, :]
        for m in range(1, NODES):
            half = half + weight_ref[core * NODES + m] * mats[c, m * n : (m + 1) * n, :]
        out_ref[:, c * 128 : (c + 1) * 128] = half


def residual_kernel(cross_ref, b_ref, t_ref, high_ref, low_ref):
    z = t_ref[...] - dot3(halves(b_ref[...]), halves(cross_ref[...]))
    high_ref[...], low_ref[...] = halves(z)


def lift_kernel(scale, mine_ref, other_ref, cross_ref, high_ref, low_ref, out_hbm, out_ref, sems):
    rows = high_ref.shape[0] // CHUNKS
    total = (mine_ref[...] + other_ref[...]) * -scale
    right = halves(dot3(halves(total), halves(cross_ref[...].T)))
    copies = []
    for c in range(CHUNKS):
        part = pl.ds(c * rows, rows)
        out_ref[part, :] = dot3((high_ref[part, :], low_ref[part, :]), right)
        copies.append(pltpu.make_async_copy(out_ref.at[part], out_hbm.at[part], sems.at[c]))
        copies[-1].start()
    for copy in copies:
        copy.wait()


def swap_cores(x):
    return lax.ppermute(x, "gz", [(0, 1), (1, 0)])


def swap_bits(x, mesh, gx, gy):
    ny, nz = mesh.shape["gy"], mesh.shape["gz"]
    perm = []
    for i in range(mesh.size):
        x0, y0, z0 = i // (ny * nz), i // nz % ny, i % nz
        perm.append((i, ((x0 ^ gx) * ny + (y0 ^ gy)) * nz + z0))
    return lax.ppermute(x, ("gx", "gy", "gz"), perm)


def summed(x, mesh):
    nx, ny = mesh.shape["gx"], mesh.shape["gy"]
    low = [(a, b) for a in range(4) for b in range(2)]
    groups = [
        [(gx + a) * ny + gy + b for a, b in low] for gx in range(0, nx, 4) for gy in range(0, ny, 2)
    ]

    def cube(pieces):
        return lax.all_to_all(
            pieces, ("gx", "gy"), 0, 0, axis_index_groups=groups, tiled=True
        )

    x = jnp.sum(cube(x).reshape(CUBE, -1, x.shape[1]), axis=0)
    for bit in range(2, (nx - 1).bit_length()):
        x = x + swap_bits(x, mesh, 1 << bit, 0)
    for bit in range(1, (ny - 1).bit_length()):
        x = x + swap_bits(x, mesh, 0, 1 << bit)
    return cube(jnp.tile(x, (CUBE, 1)))


def on_device(basis, target, mesh):
    rows, n = basis.shape
    total_rows = rows * mesh.size
    pay_half = -(-(2 * n + 8) // (8 * CUBE)) * 8 * CUBE
    vmem = pl.BlockSpec(memory_space=pltpu.VMEM)
    smem = pl.BlockSpec(memory_space=pltpu.SMEM)
    hbm = pl.BlockSpec(memory_space=pltpu.HBM)
    limit = pltpu.CompilerParams(vmem_limit_bytes=48 * 1024 * 1024)
    core = lax.axis_index("gz")
    where = jnp.reshape(core, (1,)).astype(jnp.int32)
    half = jax.ShapeDtypeStruct((pay_half, 128), F32)
    keep, send = pl.pallas_call(
        gram_kernel,
        out_shape=(half, half),
        in_specs=[smem, hbm, hbm],
        out_specs=(vmem, vmem),
        scratch_shapes=[
            pltpu.VMEM((rows, n), F32),
            pltpu.VMEM((rows, n), F32),
            pltpu.VMEM((2 * pay_half, 128), F32),
            pltpu.SemaphoreType.DMA((2, CHUNKS)),
        ],
        compiler_params=pltpu.CompilerParams(vmem_limit_bytes=GRANT),
    )(where, basis, target)
    mine = summed(keep + swap_cores(send), mesh)
    other = swap_cores(mine)
    square = jax.ShapeDtypeStruct((n, n), F32)
    part, cross = pl.pallas_call(
        resolvent_kernel,
        out_shape=(square, square),
        in_specs=[smem, smem, smem, vmem, vmem],
        out_specs=(vmem, vmem),
        scratch_shapes=[
            pltpu.VMEM((2, NODES * n, 128), F32),
            pltpu.VMEM((2, 128, 128), F32),
            pltpu.VMEM((2 * 128, 128), F32),
            pltpu.VMEM((NODES, STEP, n), F32),
            pltpu.VMEM((2 * pay_half, 128), F32),
        ],
        compiler_params=limit,
        cost_estimate=pl.CostEstimate(flops=10**11, bytes_accessed=10**6, transcendentals=0),
    )(where, jnp.asarray(points**2, F32), jnp.asarray(weights, F32), mine, other)
    other = swap_cores(part)
    high, low = pl.pallas_call(
        residual_kernel,
        out_shape=(jax.ShapeDtypeStruct((rows, n), BF16),) * 2,
        in_specs=[vmem, vmem, vmem],
        out_specs=(vmem, vmem),
        compiler_params=limit,
        cost_estimate=pl.CostEstimate(flops=10**9, bytes_accessed=3 * 10**6, transcendentals=0),
    )(cross, basis, target)
    return pl.pallas_call(
        functools.partial(lift_kernel, float(np.sqrt(total_rows))),
        out_shape=jax.ShapeDtypeStruct((rows, n), F32),
        in_specs=[vmem] * 5,
        out_specs=hbm,
        scratch_shapes=[pltpu.VMEM((rows, n), F32), pltpu.SemaphoreType.DMA((CHUNKS,))],
        compiler_params=limit,
    )(part, other, cross, high, low)


def solution(mesh):
    return jax.shard_map(
        functools.partial(on_device, mesh=mesh),
        mesh=mesh,
        in_specs=(P(("gx", "gy", "gz"), None), P(("gx", "gy", "gz"), None)),
        out_specs=P(("gx", "gy", "gz"), None),
        check_vma=False,
    )
```

```python
import functools

import jax
import jax.numpy as jnp
import numpy as np
from jax import lax
from jax.experimental import pallas as pl
from jax.experimental.pallas import tpu as pltpu
from jax.sharding import PartitionSpec as P

half_points = [
    0.0950125098376374,
    0.2816035507792589,
    0.4580167776572274,
    0.6178762444026438,
    0.755404408355003,
    0.8656312023878318,
    0.9445750230732326,
    0.9894009349916499,
]
half_weights = [
    0.1894506104550685,
    0.1826034150449236,
    0.1691565193950025,
    0.1495959888165767,
    0.1246289712555339,
    0.0951585116824928,
    0.0622535239386479,
    0.0271524594117541,
]
points = (np.array([-v for v in half_points[::-1]] + half_points) + 1.0) / 2.0
weights = np.array(half_weights[::-1] + half_weights) / 2.0
NODES = 8
CHUNKS = 4
CUBE = 8
GRANT = 53 * 1024 * 1024
STEP = 32
F32 = jnp.float32
BF16 = jnp.bfloat16
highest = lax.Precision.HIGHEST


def iota(shape, dim):
    return lax.broadcasted_iota(jnp.int32, shape, dim)


def split(x):
    high = x.astype(BF16).astype(F32)
    rest = x - high
    mid = rest.astype(BF16).astype(F32)
    return high, mid, rest - mid


def dot(a, b):
    return jnp.dot(a, b, precision=highest, preferred_element_type=F32)


def halves(x):
    high = x.astype(BF16)
    return high, (x - high.astype(F32)).astype(BF16)


def dot3(a, b):
    (ah, al), (bh, bl) = a, b
    total = jnp.dot(ah, bl, preferred_element_type=F32) + jnp.dot(al, bh, preferred_element_type=F32)
    return total + jnp.dot(ah, bh, preferred_element_type=F32)


def gram_kernel(where_ref, b_hbm, t_hbm, keep_ref, send_ref, b_ref, t_ref, pay, sems):
    rows, n = b_ref.shape
    chunk = rows // CHUNKS
    copies = []
    for c in range(CHUNKS):
        part = pl.ds(c * chunk, chunk)
        for k, (source, dest) in enumerate(((b_hbm, b_ref), (t_hbm, t_ref))):
            copy = pltpu.make_async_copy(source.at[part], dest.at[part], sems.at[k, c])
            copy.start()
            copies.append(copy)
    cross = tgram = bgram = jnp.zeros((n, n), F32)
    for c in range(CHUNKS):
        part = slice(c * chunk, (c + 1) * chunk)
        copies[2 * c].wait()
        copies[2 * c + 1].wait()
        b, t = b_ref[part, :], t_ref[part, :]
        b, bt, t, tt = halves(b), halves(b.T), halves(t), halves(t.T)
        cross += dot3(bt, t)
        tgram += dot3(tt, t)
        bgram += dot3(bt, b)
    row, col = iota((n, n), 0), iota((n, n), 1)
    packed = jnp.where(row < col, tgram, bgram)
    diag = row == col
    tdiag = jnp.sum(jnp.where(diag, tgram, 0.0), axis=0, keepdims=True)
    bdiag = jnp.sum(jnp.where(diag, bgram, 0.0), axis=0, keepdims=True)
    for c in range(2):
        half = slice(c * 128, (c + 1) * 128)
        pay[c * n : (c + 1) * n, :] = cross[:, half]
        pay[(2 + c) * n : (3 + c) * n, :] = packed[:, half]
    pay[4 * n :, :] = jnp.zeros((pay.shape[0] - 4 * n, 128), F32)
    for c in range(2):
        half = slice(c * 128, (c + 1) * 128)
        pay[4 * n + c : 4 * n + c + 1, :] = tdiag[:, half]
        pay[4 * n + 2 + c : 4 * n + 3 + c, :] = bdiag[:, half]
    half, core = keep_ref.shape[0], where_ref[0]
    keep_ref[...] = pay[pl.ds(pl.multiple_of(core * half, 8), half), :]
    send_ref[...] = pay[pl.ds(pl.multiple_of((1 - core) * half, 8), half), :]


def invert_blocks(v):
    group = iota((8, 128), 1) // NODES
    node = iota((8, 128), 1) % NODES
    row = iota((8, 128), 0)
    for g in range(4):
        q, first = g // 2, g % 2 * 8
        pan = []
        for p in range(8):
            index = node + (first + p) * NODES
            pan.append([jnp.take_along_axis(x, index, axis=1) for x in v[q]])
        for p in range(8):
            recip = 1.0 / pan[p][g][p : p + 1, :]
            new = [x for x in pan[p]]
            new[g] = jnp.where(row == p, 1.0, new[g])
            new = [x * recip for x in new]
            pan[p] = new
            for o in range(8):
                if o != p:
                    factor = pan[o][g][p : p + 1, :]
                    old = [x for x in pan[o]]
                    old[g] = jnp.where(row == p, 0.0, old[g])
                    pan[o] = [x - factor * y for x, y in zip(old, new)]
        for o in range(2):
            acc = [x for x in v[o]]
            acc[g] = jnp.zeros((8, 128), F32)
            for p in range(8):
                factor = v[o][g][p : p + 1, :]
                acc = [x - factor * y for x, y in zip(acc, pan[p])]
            if o == q:
                for p in range(8):
                    acc = [jnp.where(group == first + p, y, x) for x, y in zip(acc, pan[p])]
            v[o] = acc
    return v


def resolvent_kernel(
    where_ref, shift_ref, weight_ref, mine_ref, other_ref, out_ref, cross_ref, mats, turned, inverses, news, pay
):
    n = out_ref.shape[1]
    half, core = mine_ref.shape[0], where_ref[0]
    pay[pl.ds(pl.multiple_of(core * half, 8), half), :] = mine_ref[...]
    pay[pl.ds(pl.multiple_of((1 - core) * half, 8), half), :] = other_ref[...]
    row, col = iota((n, n), 0), iota((n, n), 1)

    def wide(start, rows):
        return jnp.concatenate([pay[start : start + rows, :], pay[start + rows : start + 2 * rows, :]], 1)

    cross, packed = wide(0, n), wide(2 * n, n)
    cross_ref[...] = cross
    tdiag, bdiag = wide(4 * n, 1), wide(4 * n + 2, 1)
    upper = jnp.where(row < col, packed, 0.0)
    lower = jnp.where(row > col, packed, 0.0)
    tgram = upper + upper.T + jnp.where(row == col, tdiag, 0.0)
    bgram = lower + lower.T + jnp.where(row == col, bdiag, 0.0)
    crosst = cross.T
    square = dot(crosst, cross)
    normal = tgram - 2.0 * square + dot(crosst, dot(bgram, cross))
    for m in range(NODES):
        shifted = square + shift_ref[core * NODES + m] * normal
        mats[0, m * n : (m + 1) * n, :] = shifted[:, 0:128]
        mats[1, m * n : (m + 1) * n, :] = shifted[:, 128:256]

    def stack(x):
        h, m, l = split(x)
        return jnp.concatenate([h, m, h, l, h, m, l, m], 0).astype(BF16)

    def step(tile, part, carry):
        inner = pl.multiple_of(part * STEP, STEP)
        start = pl.multiple_of(tile * 128 + inner, STEP)
        v = []
        for q in range(2):
            rows = [mats[tile, pl.ds(start + 16 * q + i, NODES, stride=n), :] for i in range(16)]
            turned[q] = jnp.concatenate(rows, 0).T
            block = turned[q, pl.ds(inner, STEP), :]
            v.append([block[8 * g : 8 * g + 8] for g in range(4)])
        v = invert_blocks(v)
        for q in range(2):
            h, m, l = split(jnp.concatenate(v[q], 0))
            inverses[0, q * 128 : (q + 1) * 128, :] = jnp.concatenate([h, h, m, h], 0).T
            inverses[1, q * 128 : (q + 1) * 128, :] = jnp.concatenate([l, m, m, l], 0).T

        group = iota((n, 128), 1) // STEP
        index = iota((n, 128), 1) % STEP + inner
        local = iota((STEP, n), 1) - start
        inblock = (local >= 0) & (local < STEP)
        minus = jnp.where(local == iota((STEP, n), 0), -1.0, 0.0)
        for m in range(NODES):
            left = [inverses[c, pl.ds(m, STEP, stride=NODES), :] for c in range(2)]
            left = jnp.concatenate(left, 1).astype(BF16)
            here = pl.ds(pl.multiple_of(m * n + start, STEP), STEP)
            panel = jnp.concatenate([mats[0, here, :], mats[1, here, :]], 1)
            panel = jnp.where(inblock, minus, panel)
            news[m] = jnp.dot(left, stack(panel), preferred_element_type=F32)
        for m in range(NODES):
            rows = slice(m * n, (m + 1) * n)
            columns = jnp.take_along_axis(mats[tile, rows, :], index, axis=1)
            h, d, l = split(columns)
            one = jnp.where(group == 2, d, h)
            two = jnp.where((group == 0) | (group == 3), l, d)
            lhs = jnp.concatenate([one, two], 1).astype(BF16)
            change = jnp.dot(lhs, stack(news[m]), preferred_element_type=F32)
            for c in range(2):
                half = slice(c * 128, (c + 1) * 128)
                old = mats[c, rows, :]
                if c == tile:
                    old = jnp.where(inblock[0:1, half], 0.0, old)
                mats[c, rows, :] = old - change[:, half]
        for m in range(NODES):
            here = pl.ds(pl.multiple_of(m * n + start, STEP), STEP)
            mats[0, here, :] = news[m, :, 0:128]
            mats[1, here, :] = news[m, :, 128:256]
        return carry

    for tile in range(2):
        lax.fori_loop(0, 4, functools.partial(step, tile), 0)
    for c in range(2):
        half = weight_ref[core * NODES] * mats[c, 0:n, :]
        for m in range(1, NODES):
            half = half + weight_ref[core * NODES + m] * mats[c, m * n : (m + 1) * n, :]
        out_ref[:, c * 128 : (c + 1) * 128] = half


def residual_kernel(cross_ref, b_ref, t_ref, high_ref, low_ref):
    z = t_ref[...] - dot3(halves(b_ref[...]), halves(cross_ref[...]))
    high_ref[...], low_ref[...] = halves(z)


def lift_kernel(scale, mine_ref, other_ref, cross_ref, high_ref, low_ref, out_hbm, out_ref, sems):
    rows = high_ref.shape[0] // CHUNKS
    total = (mine_ref[...] + other_ref[...]) * -scale
    right = halves(dot3(halves(total), halves(cross_ref[...].T)))
    copies = []
    for c in range(CHUNKS):
        part = pl.ds(c * rows, rows)
        out_ref[part, :] = dot3((high_ref[part, :], low_ref[part, :]), right)
        copies.append(pltpu.make_async_copy(out_ref.at[part], out_hbm.at[part], sems.at[c]))
        copies[-1].start()
    for copy in copies:
        copy.wait()


def swap_cores(x):
    return lax.ppermute(x, "gz", [(0, 1), (1, 0)])


def swap_bits(x, mesh, gx, gy):
    ny, nz = mesh.shape["gy"], mesh.shape["gz"]
    perm = []
    for i in range(mesh.size):
        x0, y0, z0 = i // (ny * nz), i // nz % ny, i % nz
        perm.append((i, ((x0 ^ gx) * ny + (y0 ^ gy)) * nz + z0))
    return lax.ppermute(x, ("gx", "gy", "gz"), perm)


def summed(x, mesh):
    nx, ny = mesh.shape["gx"], mesh.shape["gy"]
    low = [(a, b) for a in range(4) for b in range(2)]
    groups = [
        [(gx + a) * ny + gy + b for a, b in low] for gx in range(0, nx, 4) for gy in range(0, ny, 2)
    ]

    def cube(pieces):
        return lax.all_to_all(
            pieces, ("gx", "gy"), 0, 0, axis_index_groups=groups, tiled=True
        )

    x = jnp.sum(cube(x).reshape(CUBE, -1, x.shape[1]), axis=0)
    for bit in range(2, (nx - 1).bit_length()):
        x = x + swap_bits(x, mesh, 1 << bit, 0)
    for bit in range(1, (ny - 1).bit_length()):
        x = x + swap_bits(x, mesh, 0, 1 << bit)
    return cube(jnp.tile(x, (CUBE, 1)))


def on_device(basis, target, mesh):
    rows, n = basis.shape
    total_rows = rows * mesh.size
    pay_half = -(-(2 * n + 8) // (8 * CUBE)) * 8 * CUBE
    vmem = pl.BlockSpec(memory_space=pltpu.VMEM)
    smem = pl.BlockSpec(memory_space=pltpu.SMEM)
    hbm = pl.BlockSpec(memory_space=pltpu.HBM)
    limit = pltpu.CompilerParams(vmem_limit_bytes=48 * 1024 * 1024)
    core = lax.axis_index("gz")
    where = jnp.reshape(core, (1,)).astype(jnp.int32)
    half = jax.ShapeDtypeStruct((pay_half, 128), F32)
    keep, send = pl.pallas_call(
        gram_kernel,
        out_shape=(half, half),
        in_specs=[smem, hbm, hbm],
        out_specs=(vmem, vmem),
        scratch_shapes=[
            pltpu.VMEM((rows, n), F32),
            pltpu.VMEM((rows, n), F32),
            pltpu.VMEM((2 * pay_half, 128), F32),
            pltpu.SemaphoreType.DMA((2, CHUNKS)),
        ],
        compiler_params=pltpu.CompilerParams(vmem_limit_bytes=GRANT),
    )(where, basis, target)
    mine = summed(keep + swap_cores(send), mesh)
    other = swap_cores(mine)
    square = jax.ShapeDtypeStruct((n, n), F32)
    part, cross = pl.pallas_call(
        resolvent_kernel,
        out_shape=(square, square),
        in_specs=[smem, smem, smem, vmem, vmem],
        out_specs=(vmem, vmem),
        scratch_shapes=[
            pltpu.VMEM((2, NODES * n, 128), F32),
            pltpu.VMEM((2, 128, 128), F32),
            pltpu.VMEM((2, 2 * 128, 128), F32),
            pltpu.VMEM((NODES, STEP, n), F32),
            pltpu.VMEM((2 * pay_half, 128), F32),
        ],
        compiler_params=limit,
        cost_estimate=pl.CostEstimate(flops=10**11, bytes_accessed=10**6, transcendentals=0),
    )(where, jnp.asarray(points**2, F32), jnp.asarray(weights, F32), mine, other)
    other = swap_cores(part)
    high, low = pl.pallas_call(
        residual_kernel,
        out_shape=(jax.ShapeDtypeStruct((rows, n), BF16),) * 2,
        in_specs=[vmem, vmem, vmem],
        out_specs=(vmem, vmem),
        compiler_params=limit,
        cost_estimate=pl.CostEstimate(flops=10**9, bytes_accessed=3 * 10**6, transcendentals=0),
    )(cross, basis, target)
    return pl.pallas_call(
        functools.partial(lift_kernel, float(np.sqrt(total_rows))),
        out_shape=jax.ShapeDtypeStruct((rows, n), F32),
        in_specs=[vmem] * 5,
        out_specs=hbm,
        scratch_shapes=[pltpu.VMEM((rows, n), F32), pltpu.SemaphoreType.DMA((CHUNKS,))],
        compiler_params=limit,
    )(part, other, cross, high, low)


def solution(mesh):
    return jax.shard_map(
        functools.partial(on_device, mesh=mesh),
        mesh=mesh,
        in_specs=(P(("gx", "gy", "gz"), None), P(("gx", "gy", "gz"), None)),
        out_specs=P(("gx", "gy", "gz"), None),
        check_vma=False,
    )
```

```python
import functools

import jax
import jax.numpy as jnp
import numpy as np
from jax import lax
from jax.experimental import pallas as pl
from jax.experimental.pallas import tpu as pltpu
from jax.sharding import PartitionSpec as P

half_points = [
    0.0950125098376374,
    0.2816035507792589,
    0.4580167776572274,
    0.6178762444026438,
    0.755404408355003,
    0.8656312023878318,
    0.9445750230732326,
    0.9894009349916499,
]
half_weights = [
    0.1894506104550685,
    0.1826034150449236,
    0.1691565193950025,
    0.1495959888165767,
    0.1246289712555339,
    0.0951585116824928,
    0.0622535239386479,
    0.0271524594117541,
]
points = (np.array([-v for v in half_points[::-1]] + half_points) + 1.0) / 2.0
weights = np.array(half_weights[::-1] + half_weights) / 2.0
NODES = 8
CHUNKS = 4
CUBE = 8
GRANT = 53 * 1024 * 1024
STEP = 32
F32 = jnp.float32
BF16 = jnp.bfloat16
highest = lax.Precision.HIGHEST


def iota(shape, dim):
    return lax.broadcasted_iota(jnp.int32, shape, dim)


def split(x):
    high = x.astype(BF16).astype(F32)
    rest = x - high
    mid = rest.astype(BF16).astype(F32)
    return high, mid, rest - mid


def dot(a, b):
    return jnp.dot(a, b, precision=highest, preferred_element_type=F32)


def halves(x):
    high = x.astype(BF16)
    return high, (x - high.astype(F32)).astype(BF16)


def dot3(a, b):
    (ah, al), (bh, bl) = a, b
    total = jnp.dot(ah, bl, preferred_element_type=F32) + jnp.dot(al, bh, preferred_element_type=F32)
    return total + jnp.dot(ah, bh, preferred_element_type=F32)


def gram_kernel(where_ref, b_hbm, t_hbm, keep_ref, send_ref, b_ref, t_ref, pay, sems):
    rows, n = b_ref.shape
    chunk = rows // CHUNKS
    copies = []
    for c in range(CHUNKS):
        part = pl.ds(c * chunk, chunk)
        for k, (source, dest) in enumerate(((b_hbm, b_ref), (t_hbm, t_ref))):
            copy = pltpu.make_async_copy(source.at[part], dest.at[part], sems.at[k, c])
            copy.start()
            copies.append(copy)
    cross = tgram = bgram = jnp.zeros((n, n), F32)
    for c in range(CHUNKS):
        part = slice(c * chunk, (c + 1) * chunk)
        copies[2 * c].wait()
        copies[2 * c + 1].wait()
        b, t = b_ref[part, :], t_ref[part, :]
        b, bt, t, tt = halves(b), halves(b.T), halves(t), halves(t.T)
        cross += dot3(bt, t)
        tgram += dot3(tt, t)
        bgram += dot3(bt, b)
    row, col = iota((n, n), 0), iota((n, n), 1)
    packed = jnp.where(row < col, tgram, bgram)
    diag = row == col
    tdiag = jnp.sum(jnp.where(diag, tgram, 0.0), axis=0, keepdims=True)
    bdiag = jnp.sum(jnp.where(diag, bgram, 0.0), axis=0, keepdims=True)
    for c in range(2):
        half = slice(c * 128, (c + 1) * 128)
        pay[c * n : (c + 1) * n, :] = cross[:, half]
        pay[(2 + c) * n : (3 + c) * n, :] = packed[:, half]
    pay[4 * n :, :] = jnp.zeros((pay.shape[0] - 4 * n, 128), F32)
    for c in range(2):
        half = slice(c * 128, (c + 1) * 128)
        pay[4 * n + c : 4 * n + c + 1, :] = tdiag[:, half]
        pay[4 * n + 2 + c : 4 * n + 3 + c, :] = bdiag[:, half]
    half, core = keep_ref.shape[0], where_ref[0]
    keep_ref[...] = pay[pl.ds(pl.multiple_of(core * half, 8), half), :]
    send_ref[...] = pay[pl.ds(pl.multiple_of((1 - core) * half, 8), half), :]


def invert_blocks(v):
    group = iota((8, 128), 1) // NODES
    node = iota((8, 128), 1) % NODES
    row = iota((8, 128), 0)
    for g in range(4):
        q, first = g // 2, g % 2 * 8
        pan = []
        for p in range(8):
            index = node + (first + p) * NODES
            pan.append([jnp.take_along_axis(x, index, axis=1) for x in v[q]])
        for p in range(8):
            pivot = pan[p][g][p : p + 1, :]
            recip = pl.reciprocal(pivot, approx=True)
            recip = recip * (2.0 - pivot * recip)
            new = [x for x in pan[p]]
            new[g] = jnp.where(row == p, 1.0, new[g])
            new = [x * recip for x in new]
            pan[p] = new
            for o in range(8):
                if o != p:
                    factor = pan[o][g][p : p + 1, :]
                    old = [x for x in pan[o]]
                    old[g] = jnp.where(row == p, 0.0, old[g])
                    pan[o] = [x - factor * y for x, y in zip(old, new)]
        for o in range(2):
            acc = [x for x in v[o]]
            acc[g] = jnp.zeros((8, 128), F32)
            for p in range(8):
                factor = v[o][g][p : p + 1, :]
                acc = [x - factor * y for x, y in zip(acc, pan[p])]
            if o == q:
                for p in range(8):
                    acc = [jnp.where(group == first + p, y, x) for x, y in zip(acc, pan[p])]
            v[o] = acc
    return v


def resolvent_kernel(
    where_ref, shift_ref, weight_ref, mine_ref, other_ref, out_ref, cross_ref, mats, turned, inverses, news, pay
):
    n = out_ref.shape[1]
    half, core = mine_ref.shape[0], where_ref[0]
    pay[pl.ds(pl.multiple_of(core * half, 8), half), :] = mine_ref[...]
    pay[pl.ds(pl.multiple_of((1 - core) * half, 8), half), :] = other_ref[...]
    row, col = iota((n, n), 0), iota((n, n), 1)

    def wide(start, rows):
        return jnp.concatenate([pay[start : start + rows, :], pay[start + rows : start + 2 * rows, :]], 1)

    cross, packed = wide(0, n), wide(2 * n, n)
    cross_ref[...] = cross
    tdiag, bdiag = wide(4 * n, 1), wide(4 * n + 2, 1)
    upper = jnp.where(row < col, packed, 0.0)
    lower = jnp.where(row > col, packed, 0.0)
    tgram = upper + upper.T + jnp.where(row == col, tdiag, 0.0)
    bgram = lower + lower.T + jnp.where(row == col, bdiag, 0.0)
    crosst = cross.T
    square = dot(crosst, cross)
    normal = tgram - 2.0 * square + dot(crosst, dot(bgram, cross))
    for m in range(NODES):
        shifted = square + shift_ref[core * NODES + m] * normal
        mats[0, m * n : (m + 1) * n, :] = shifted[:, 0:128]
        mats[1, m * n : (m + 1) * n, :] = shifted[:, 128:256]

    def stack(x):
        h, m, l = split(x)
        return jnp.concatenate([h, m, h, l, h, m, l, m], 0).astype(BF16)

    def step(tile, part, carry):
        inner = pl.multiple_of(part * STEP, STEP)
        start = pl.multiple_of(tile * 128 + inner, STEP)
        v = []
        for q in range(2):
            rows = [mats[tile, pl.ds(start + 16 * q + i, NODES, stride=n), :] for i in range(16)]
            turned[q] = jnp.concatenate(rows, 0).T
            block = turned[q, pl.ds(inner, STEP), :]
            v.append([block[8 * g : 8 * g + 8] for g in range(4)])
        v = invert_blocks(v)
        for q in range(2):
            h, m, l = split(jnp.concatenate(v[q], 0))
            inverses[0, q * 128 : (q + 1) * 128, :] = jnp.concatenate([h, h, m, h], 0).T
            inverses[1, q * 128 : (q + 1) * 128, :] = jnp.concatenate([l, m, m, l], 0).T

        group = iota((n, 128), 1) // STEP
        index = iota((n, 128), 1) % STEP + inner
        local = iota((STEP, n), 1) - start
        inblock = (local >= 0) & (local < STEP)
        minus = jnp.where(local == iota((STEP, n), 0), -1.0, 0.0)
        for m in range(NODES):
            left = [inverses[c, pl.ds(m, STEP, stride=NODES), :] for c in range(2)]
            left = jnp.concatenate(left, 1).astype(BF16)
            here = pl.ds(pl.multiple_of(m * n + start, STEP), STEP)
            panel = jnp.concatenate([mats[0, here, :], mats[1, here, :]], 1)
            panel = jnp.where(inblock, minus, panel)
            news[m] = jnp.dot(left, stack(panel), preferred_element_type=F32)
        for m in range(NODES):
            rows = slice(m * n, (m + 1) * n)
            columns = jnp.take_along_axis(mats[tile, rows, :], index, axis=1)
            h, d, l = split(columns)
            one = jnp.where(group == 2, d, h)
            two = jnp.where((group == 0) | (group == 3), l, d)
            lhs = jnp.concatenate([one, two], 1).astype(BF16)
            change = jnp.dot(lhs, stack(news[m]), preferred_element_type=F32)
            for c in range(2):
                half = slice(c * 128, (c + 1) * 128)
                old = mats[c, rows, :]
                if c == tile:
                    old = jnp.where(inblock[0:1, half], 0.0, old)
                mats[c, rows, :] = old - change[:, half]
        for m in range(NODES):
            here = pl.ds(pl.multiple_of(m * n + start, STEP), STEP)
            mats[0, here, :] = news[m, :, 0:128]
            mats[1, here, :] = news[m, :, 128:256]
        return carry

    for tile in range(2):
        lax.fori_loop(0, 4, functools.partial(step, tile), 0)
    for c in range(2):
        half = weight_ref[core * NODES] * mats[c, 0:n, :]
        for m in range(1, NODES):
            half = half + weight_ref[core * NODES + m] * mats[c, m * n : (m + 1) * n, :]
        out_ref[:, c * 128 : (c + 1) * 128] = half


def residual_kernel(cross_ref, b_ref, t_ref, high_ref, low_ref):
    z = t_ref[...] - dot3(halves(b_ref[...]), halves(cross_ref[...]))
    high_ref[...], low_ref[...] = halves(z)


def lift_kernel(scale, mine_ref, other_ref, cross_ref, high_ref, low_ref, out_hbm, out_ref, sems):
    rows = high_ref.shape[0] // CHUNKS
    total = (mine_ref[...] + other_ref[...]) * -scale
    right = halves(dot3(halves(total), halves(cross_ref[...].T)))
    copies = []
    for c in range(CHUNKS):
        part = pl.ds(c * rows, rows)
        out_ref[part, :] = dot3((high_ref[part, :], low_ref[part, :]), right)
        copies.append(pltpu.make_async_copy(out_ref.at[part], out_hbm.at[part], sems.at[c]))
        copies[-1].start()
    for copy in copies:
        copy.wait()


def swap_cores(x):
    return lax.ppermute(x, "gz", [(0, 1), (1, 0)])


def swap_bits(x, mesh, gx, gy):
    ny, nz = mesh.shape["gy"], mesh.shape["gz"]
    perm = []
    for i in range(mesh.size):
        x0, y0, z0 = i // (ny * nz), i // nz % ny, i % nz
        perm.append((i, ((x0 ^ gx) * ny + (y0 ^ gy)) * nz + z0))
    return lax.ppermute(x, ("gx", "gy", "gz"), perm)


def summed(x, mesh):
    nx, ny = mesh.shape["gx"], mesh.shape["gy"]
    low = [(a, b) for a in range(4) for b in range(2)]
    groups = [
        [(gx + a) * ny + gy + b for a, b in low] for gx in range(0, nx, 4) for gy in range(0, ny, 2)
    ]

    def cube(pieces):
        return lax.all_to_all(
            pieces, ("gx", "gy"), 0, 0, axis_index_groups=groups, tiled=True
        )

    x = jnp.sum(cube(x).reshape(CUBE, -1, x.shape[1]), axis=0)
    for bit in range(2, (nx - 1).bit_length()):
        x = x + swap_bits(x, mesh, 1 << bit, 0)
    for bit in range(1, (ny - 1).bit_length()):
        x = x + swap_bits(x, mesh, 0, 1 << bit)
    return cube(jnp.tile(x, (CUBE, 1)))


def on_device(basis, target, mesh):
    rows, n = basis.shape
    total_rows = rows * mesh.size
    pay_half = -(-(2 * n + 8) // (8 * CUBE)) * 8 * CUBE
    vmem = pl.BlockSpec(memory_space=pltpu.VMEM)
    smem = pl.BlockSpec(memory_space=pltpu.SMEM)
    hbm = pl.BlockSpec(memory_space=pltpu.HBM)
    limit = pltpu.CompilerParams(vmem_limit_bytes=48 * 1024 * 1024)
    core = lax.axis_index("gz")
    where = jnp.reshape(core, (1,)).astype(jnp.int32)
    half = jax.ShapeDtypeStruct((pay_half, 128), F32)
    keep, send = pl.pallas_call(
        gram_kernel,
        out_shape=(half, half),
        in_specs=[smem, hbm, hbm],
        out_specs=(vmem, vmem),
        scratch_shapes=[
            pltpu.VMEM((rows, n), F32),
            pltpu.VMEM((rows, n), F32),
            pltpu.VMEM((2 * pay_half, 128), F32),
            pltpu.SemaphoreType.DMA((2, CHUNKS)),
        ],
        compiler_params=pltpu.CompilerParams(vmem_limit_bytes=GRANT),
    )(where, basis, target)
    mine = summed(keep + swap_cores(send), mesh)
    other = swap_cores(mine)
    square = jax.ShapeDtypeStruct((n, n), F32)
    part, cross = pl.pallas_call(
        resolvent_kernel,
        out_shape=(square, square),
        in_specs=[smem, smem, smem, vmem, vmem],
        out_specs=(vmem, vmem),
        scratch_shapes=[
            pltpu.VMEM((2, NODES * n, 128), F32),
            pltpu.VMEM((2, 128, 128), F32),
            pltpu.VMEM((2, 2 * 128, 128), F32),
            pltpu.VMEM((NODES, STEP, n), F32),
            pltpu.VMEM((2 * pay_half, 128), F32),
        ],
        compiler_params=limit,
        cost_estimate=pl.CostEstimate(flops=10**11, bytes_accessed=10**6, transcendentals=0),
    )(where, jnp.asarray(points**2, F32), jnp.asarray(weights, F32), mine, other)
    other = swap_cores(part)
    high, low = pl.pallas_call(
        residual_kernel,
        out_shape=(jax.ShapeDtypeStruct((rows, n), BF16),) * 2,
        in_specs=[vmem, vmem, vmem],
        out_specs=(vmem, vmem),
        compiler_params=limit,
        cost_estimate=pl.CostEstimate(flops=10**9, bytes_accessed=3 * 10**6, transcendentals=0),
    )(cross, basis, target)
    return pl.pallas_call(
        functools.partial(lift_kernel, float(np.sqrt(total_rows))),
        out_shape=jax.ShapeDtypeStruct((rows, n), F32),
        in_specs=[vmem] * 5,
        out_specs=hbm,
        scratch_shapes=[pltpu.VMEM((rows, n), F32), pltpu.SemaphoreType.DMA((CHUNKS,))],
        compiler_params=limit,
    )(part, other, cross, high, low)


def solution(mesh):
    return jax.shard_map(
        functools.partial(on_device, mesh=mesh),
        mesh=mesh,
        in_specs=(P(("gx", "gy", "gz"), None), P(("gx", "gy", "gz"), None)),
        out_specs=P(("gx", "gy", "gz"), None),
        check_vma=False,
    )
```

```python
import functools

import jax
import jax.numpy as jnp
import numpy as np
from jax import lax
from jax.experimental import pallas as pl
from jax.experimental.pallas import tpu as pltpu
from jax.sharding import PartitionSpec as P

half_points = [
    0.0950125098376374,
    0.2816035507792589,
    0.4580167776572274,
    0.6178762444026438,
    0.755404408355003,
    0.8656312023878318,
    0.9445750230732326,
    0.9894009349916499,
]
half_weights = [
    0.1894506104550685,
    0.1826034150449236,
    0.1691565193950025,
    0.1495959888165767,
    0.1246289712555339,
    0.0951585116824928,
    0.0622535239386479,
    0.0271524594117541,
]
points = (np.array([-v for v in half_points[::-1]] + half_points) + 1.0) / 2.0
weights = np.array(half_weights[::-1] + half_weights) / 2.0
NODES = 8
CHUNKS = 4
CUBE = 8
GRANT = 53 * 1024 * 1024
STEP = 32
F32 = jnp.float32
BF16 = jnp.bfloat16
highest = lax.Precision.HIGHEST


def iota(shape, dim):
    return lax.broadcasted_iota(jnp.int32, shape, dim)


def split(x):
    high = x.astype(BF16).astype(F32)
    rest = x - high
    mid = rest.astype(BF16).astype(F32)
    return high, mid, rest - mid


def dot(a, b):
    return jnp.dot(a, b, precision=highest, preferred_element_type=F32)


def halves(x):
    high = x.astype(BF16)
    return high, (x - high.astype(F32)).astype(BF16)


def dot3(a, b):
    (ah, al), (bh, bl) = a, b
    total = jnp.dot(ah, bl, preferred_element_type=F32) + jnp.dot(al, bh, preferred_element_type=F32)
    return total + jnp.dot(ah, bh, preferred_element_type=F32)


def gram_kernel(where_ref, b_hbm, t_hbm, keep_ref, send_ref, b_ref, t_ref, pay, sems):
    rows, n = b_ref.shape
    chunk = rows // CHUNKS
    copies = []
    for c in range(CHUNKS):
        part = pl.ds(c * chunk, chunk)
        for k, (source, dest) in enumerate(((b_hbm, b_ref), (t_hbm, t_ref))):
            copy = pltpu.make_async_copy(source.at[part], dest.at[part], sems.at[k, c])
            copy.start()
            copies.append(copy)
    cross = tgram = bgram = jnp.zeros((n, n), F32)
    for c in range(CHUNKS):
        part = slice(c * chunk, (c + 1) * chunk)
        copies[2 * c].wait()
        copies[2 * c + 1].wait()
        b, t = b_ref[part, :], t_ref[part, :]
        b, bt, t, tt = halves(b), halves(b.T), halves(t), halves(t.T)
        cross += dot3(bt, t)
        tgram += dot3(tt, t)
        bgram += dot3(bt, b)
    row, col = iota((n, n), 0), iota((n, n), 1)
    packed = jnp.where(row < col, tgram, bgram)
    diag = row == col
    tdiag = jnp.sum(jnp.where(diag, tgram, 0.0), axis=0, keepdims=True)
    bdiag = jnp.sum(jnp.where(diag, bgram, 0.0), axis=0, keepdims=True)
    for c in range(2):
        half = slice(c * 128, (c + 1) * 128)
        pay[c * n : (c + 1) * n, :] = cross[:, half]
        pay[(2 + c) * n : (3 + c) * n, :] = packed[:, half]
    pay[4 * n :, :] = jnp.zeros((pay.shape[0] - 4 * n, 128), F32)
    for c in range(2):
        half = slice(c * 128, (c + 1) * 128)
        pay[4 * n + c : 4 * n + c + 1, :] = tdiag[:, half]
        pay[4 * n + 2 + c : 4 * n + 3 + c, :] = bdiag[:, half]
    half, core = keep_ref.shape[0], where_ref[0]
    keep_ref[...] = pay[pl.ds(pl.multiple_of(core * half, 8), half), :]
    send_ref[...] = pay[pl.ds(pl.multiple_of((1 - core) * half, 8), half), :]


def invert_blocks(v, between):
    group = iota((8, 128), 1) // NODES
    node = iota((8, 128), 1) % NODES
    row = iota((8, 128), 0)
    for g in range(4):
        q, first = g // 2, g % 2 * 8
        pan = []
        for p in range(8):
            index = node + (first + p) * NODES
            pan.append([jnp.take_along_axis(x, index, axis=1) for x in v[q]])
        for p in range(8):
            recip = 1.0 / pan[p][g][p : p + 1, :]
            new = [x for x in pan[p]]
            new[g] = jnp.where(row == p, 1.0, new[g])
            new = [x * recip for x in new]
            pan[p] = new
            for o in range(8):
                if o != p:
                    factor = pan[o][g][p : p + 1, :]
                    old = [x for x in pan[o]]
                    old[g] = jnp.where(row == p, 0.0, old[g])
                    pan[o] = [x - factor * y for x, y in zip(old, new)]
            if p % 2:
                between[(8 * g + p) // 2]()
        for o in range(2):
            acc = [x for x in v[o]]
            acc[g] = jnp.zeros((8, 128), F32)
            for p in range(8):
                factor = v[o][g][p : p + 1, :]
                acc = [x - factor * y for x, y in zip(acc, pan[p])]
            if o == q:
                for p in range(8):
                    acc = [jnp.where(group == first + p, y, x) for x, y in zip(acc, pan[p])]
            v[o] = acc
    return v


def resolvent_kernel(
    where_ref, shift_ref, weight_ref, mine_ref, other_ref, out_ref, cross_ref, pay, blocks, turned, inverses, news, stacks, *mats
):
    n = out_ref.shape[1]
    last = n // STEP - 1
    half, core = mine_ref.shape[0], where_ref[0]
    pay[pl.ds(pl.multiple_of(core * half, 8), half), :] = mine_ref[...]
    pay[pl.ds(pl.multiple_of((1 - core) * half, 8), half), :] = other_ref[...]
    row, col = iota((n, n), 0), iota((n, n), 1)

    def wide(start, rows):
        return jnp.concatenate([pay[start : start + rows, :], pay[start + rows : start + 2 * rows, :]], 1)

    cross, packed = wide(0, n), wide(2 * n, n)
    cross_ref[...] = cross
    tdiag, bdiag = wide(4 * n, 1), wide(4 * n + 2, 1)
    upper = jnp.where(row < col, packed, 0.0)
    lower = jnp.where(row > col, packed, 0.0)
    tgram = upper + upper.T + jnp.where(row == col, tdiag, 0.0)
    bgram = lower + lower.T + jnp.where(row == col, bdiag, 0.0)
    crosst = cross.T
    square = dot(crosst, cross)
    normal = tgram - 2.0 * square + dot(crosst, dot(bgram, cross))
    for m in range(NODES):
        shifted = square + shift_ref[core * NODES + m] * normal
        mats[m][0] = shifted[:, 0:128]
        mats[m][1] = shifted[:, 128:256]
        blocks[m * STEP : (m + 1) * STEP, :] = shifted[0:STEP, 0:128]

    def stack(x):
        h, m, l = split(x)
        return jnp.concatenate([h, m, h, l, h, m, l, m], 0).astype(BF16)

    def spread(x, first):
        lane = iota(x.shape, 1)
        group = lane // STEP
        h, d, l = split(jnp.take_along_axis(x, lane % STEP + first, axis=1))
        one = jnp.where(group == 2, d, h)
        two = jnp.where((group == 0) | (group == 3), l, d)
        return jnp.concatenate([one, two], 1).astype(BF16)

    def place(kb):
        return kb // 4, pl.multiple_of(kb % 4 * STEP, STEP), pl.ds(pl.multiple_of(kb * STEP, STEP), STEP)

    def columns_of(kb):
        local = iota((STEP, n), 1) - kb * STEP
        return local, (local >= 0) & (local < STEP)

    def update(kb, m, side):
        tile, first, here = place(kb)
        local, inblock = columns_of(kb)
        rows = slice(side * 128, (side + 1) * 128)
        right = jnp.concatenate([stacks[m, 0], stacks[m, 1]], 1)
        change = jnp.dot(spread(mats[m][tile, rows, :], first), right, preferred_element_type=F32)
        for c in range(2):
            part = slice(c * 128, (c + 1) * 128)
            old = jnp.where(inblock[0:1, part], 0.0, mats[m][c, rows, :])
            mats[m][c, rows, :] = old - change[:, part]
        if side == 1:
            for c in range(2):
                mats[m][c, here, :] = news[m, c]

    def pivots(kb, work):
        tile, first, here = place(kb)
        v = []
        for q in range(2):
            rows = [blocks[pl.ds(16 * q + i, NODES, stride=STEP), :] for i in range(16)]
            turned[q] = jnp.concatenate(rows, 0).T
            block = turned[q, pl.ds(first, STEP), :]
            v.append([block[8 * g : 8 * g + 8] for g in range(4)])
        v = invert_blocks(v, work)
        for q in range(2):
            inverses[q * 128 : (q + 1) * 128, 0:STEP] = jnp.concatenate(v[q], 0).T
        local, inblock = columns_of(kb)
        minus = jnp.where(local == iota((STEP, n), 0), -1.0, 0.0)
        for m in range(NODES):
            left = spread(inverses[pl.ds(m, STEP, stride=NODES), :], 0)
            panel = jnp.concatenate([mats[m][0, here, :], mats[m][1, here, :]], 1)
            panel = jnp.where(inblock, minus, panel)
            new = jnp.dot(left, stack(panel), preferred_element_type=F32)
            for c in range(2):
                part = new[:, c * 128 : (c + 1) * 128]
                news[m, c] = part
                stacks[m, c] = stack(part)
        tile1, _, here1 = place(jnp.minimum(kb + 1, last))
        for m in range(NODES):
            left = spread(mats[m][tile, here1, :], first)
            change = jnp.dot(left, stacks[m, tile1], preferred_element_type=F32)
            blocks[m * STEP : (m + 1) * STEP, :] = mats[m][tile1, here1, :] - change

    def step(kb, carry):
        work = [functools.partial(update, kb - 1, m, side) for m in range(NODES) for side in range(2)]
        pivots(kb, work)
        return carry

    pivots(jnp.int32(0), [lambda: None] * 16)
    lax.fori_loop(1, last + 1, step, 0)
    for m in range(NODES):
        for side in range(2):
            update(jnp.int32(last), m, side)
    for c in range(2):
        total = weight_ref[core * NODES] * mats[0][c]
        for m in range(1, NODES):
            total = total + weight_ref[core * NODES + m] * mats[m][c]
        out_ref[:, c * 128 : (c + 1) * 128] = total


def residual_kernel(cross_ref, b_ref, t_ref, high_ref, low_ref):
    z = t_ref[...] - dot3(halves(b_ref[...]), halves(cross_ref[...]))
    high_ref[...], low_ref[...] = halves(z)


def lift_kernel(scale, mine_ref, other_ref, cross_ref, high_ref, low_ref, out_hbm, out_ref, sems):
    rows = high_ref.shape[0] // CHUNKS
    total = (mine_ref[...] + other_ref[...]) * -scale
    right = halves(dot3(halves(total), halves(cross_ref[...].T)))
    copies = []
    for c in range(CHUNKS):
        part = pl.ds(c * rows, rows)
        out_ref[part, :] = dot3((high_ref[part, :], low_ref[part, :]), right)
        copies.append(pltpu.make_async_copy(out_ref.at[part], out_hbm.at[part], sems.at[c]))
        copies[-1].start()
    for copy in copies:
        copy.wait()


def swap_cores(x):
    return lax.ppermute(x, "gz", [(0, 1), (1, 0)])


def swap_bits(x, mesh, gx, gy):
    ny, nz = mesh.shape["gy"], mesh.shape["gz"]
    perm = []
    for i in range(mesh.size):
        x0, y0, z0 = i // (ny * nz), i // nz % ny, i % nz
        perm.append((i, ((x0 ^ gx) * ny + (y0 ^ gy)) * nz + z0))
    return lax.ppermute(x, ("gx", "gy", "gz"), perm)


def summed(x, mesh):
    nx, ny = mesh.shape["gx"], mesh.shape["gy"]
    low = [(a, b) for a in range(4) for b in range(2)]
    groups = [
        [(gx + a) * ny + gy + b for a, b in low] for gx in range(0, nx, 4) for gy in range(0, ny, 2)
    ]

    def cube(pieces):
        return lax.all_to_all(
            pieces, ("gx", "gy"), 0, 0, axis_index_groups=groups, tiled=True
        )

    x = jnp.sum(cube(x).reshape(CUBE, -1, x.shape[1]), axis=0)
    for bit in range(2, (nx - 1).bit_length()):
        x = x + swap_bits(x, mesh, 1 << bit, 0)
    for bit in range(1, (ny - 1).bit_length()):
        x = x + swap_bits(x, mesh, 0, 1 << bit)
    return cube(jnp.tile(x, (CUBE, 1)))


def on_device(basis, target, mesh):
    rows, n = basis.shape
    total_rows = rows * mesh.size
    pay_half = -(-(2 * n + 8) // (8 * CUBE)) * 8 * CUBE
    vmem = pl.BlockSpec(memory_space=pltpu.VMEM)
    smem = pl.BlockSpec(memory_space=pltpu.SMEM)
    hbm = pl.BlockSpec(memory_space=pltpu.HBM)
    limit = pltpu.CompilerParams(vmem_limit_bytes=48 * 1024 * 1024)
    core = lax.axis_index("gz")
    where = jnp.reshape(core, (1,)).astype(jnp.int32)
    half = jax.ShapeDtypeStruct((pay_half, 128), F32)
    keep, send = pl.pallas_call(
        gram_kernel,
        out_shape=(half, half),
        in_specs=[smem, hbm, hbm],
        out_specs=(vmem, vmem),
        scratch_shapes=[
            pltpu.VMEM((rows, n), F32),
            pltpu.VMEM((rows, n), F32),
            pltpu.VMEM((2 * pay_half, 128), F32),
            pltpu.SemaphoreType.DMA((2, CHUNKS)),
        ],
        compiler_params=pltpu.CompilerParams(vmem_limit_bytes=GRANT),
    )(where, basis, target)
    mine = summed(keep + swap_cores(send), mesh)
    other = swap_cores(mine)
    square = jax.ShapeDtypeStruct((n, n), F32)
    part, cross = pl.pallas_call(
        resolvent_kernel,
        out_shape=(square, square),
        in_specs=[smem, smem, smem, vmem, vmem],
        out_specs=(vmem, vmem),
        scratch_shapes=[
            pltpu.VMEM((2 * pay_half, 128), F32),
            pltpu.VMEM((NODES * STEP, 128), F32),
            pltpu.VMEM((2, 128, 128), F32),
            pltpu.VMEM((2 * 128, 128), F32),
            pltpu.VMEM((NODES, 2, STEP, 128), F32),
            pltpu.VMEM((NODES, 2, 8 * STEP, 128), BF16),
        ]
        + [pltpu.VMEM((2, n, 128), F32)] * NODES,
        compiler_params=limit,
        cost_estimate=pl.CostEstimate(flops=10**11, bytes_accessed=10**6, transcendentals=0),
    )(where, jnp.asarray(points**2, F32), jnp.asarray(weights, F32), mine, other)
    other = swap_cores(part)
    high, low = pl.pallas_call(
        residual_kernel,
        out_shape=(jax.ShapeDtypeStruct((rows, n), BF16),) * 2,
        in_specs=[vmem, vmem, vmem],
        out_specs=(vmem, vmem),
        compiler_params=limit,
        cost_estimate=pl.CostEstimate(flops=10**9, bytes_accessed=3 * 10**6, transcendentals=0),
    )(cross, basis, target)
    return pl.pallas_call(
        functools.partial(lift_kernel, float(np.sqrt(total_rows))),
        out_shape=jax.ShapeDtypeStruct((rows, n), F32),
        in_specs=[vmem] * 5,
        out_specs=hbm,
        scratch_shapes=[pltpu.VMEM((rows, n), F32), pltpu.SemaphoreType.DMA((CHUNKS,))],
        compiler_params=limit,
    )(part, other, cross, high, low)


def solution(mesh):
    return jax.shard_map(
        functools.partial(on_device, mesh=mesh),
        mesh=mesh,
        in_specs=(P(("gx", "gy", "gz"), None), P(("gx", "gy", "gz"), None)),
        out_specs=P(("gx", "gy", "gz"), None),
        check_vma=False,
    )
```

```python
import functools

import jax
import jax.numpy as jnp
import numpy as np
from jax import lax
from jax.experimental import pallas as pl
from jax.experimental.pallas import tpu as pltpu
from jax.sharding import PartitionSpec as P

half_points = [
    0.0950125098376374,
    0.2816035507792589,
    0.4580167776572274,
    0.6178762444026438,
    0.755404408355003,
    0.8656312023878318,
    0.9445750230732326,
    0.9894009349916499,
]
half_weights = [
    0.1894506104550685,
    0.1826034150449236,
    0.1691565193950025,
    0.1495959888165767,
    0.1246289712555339,
    0.0951585116824928,
    0.0622535239386479,
    0.0271524594117541,
]
points = (np.array([-v for v in half_points[::-1]] + half_points) + 1.0) / 2.0
weights = np.array(half_weights[::-1] + half_weights) / 2.0
NODES = 8
CHUNKS = 4
CUBE = 8
GRANT = 53 * 1024 * 1024
STEP = 32
F32 = jnp.float32
BF16 = jnp.bfloat16
highest = lax.Precision.HIGHEST


def iota(shape, dim):
    return lax.broadcasted_iota(jnp.int32, shape, dim)


def split(x):
    high = x.astype(BF16).astype(F32)
    rest = x - high
    mid = rest.astype(BF16).astype(F32)
    return high, mid, rest - mid


def dot(a, b):
    return jnp.dot(a, b, precision=highest, preferred_element_type=F32)


def halves(x):
    high = x.astype(BF16)
    return high, (x - high.astype(F32)).astype(BF16)


def dot3(a, b):
    (ah, al), (bh, bl) = a, b
    total = jnp.dot(ah, bl, preferred_element_type=F32) + jnp.dot(al, bh, preferred_element_type=F32)
    return total + jnp.dot(ah, bh, preferred_element_type=F32)


def gram_kernel(where_ref, b_hbm, t_hbm, keep_ref, send_ref, b_ref, t_ref, pay, sems):
    rows, n = b_ref.shape
    chunk = rows // CHUNKS
    copies = []
    for c in range(CHUNKS):
        part = pl.ds(c * chunk, chunk)
        for k, (source, dest) in enumerate(((b_hbm, b_ref), (t_hbm, t_ref))):
            copy = pltpu.make_async_copy(source.at[part], dest.at[part], sems.at[k, c])
            copy.start()
            copies.append(copy)
    cross = tgram = bgram = jnp.zeros((n, n), F32)
    for c in range(CHUNKS):
        part = slice(c * chunk, (c + 1) * chunk)
        copies[2 * c].wait()
        copies[2 * c + 1].wait()
        b, t = b_ref[part, :], t_ref[part, :]
        b, bt, t, tt = halves(b), halves(b.T), halves(t), halves(t.T)
        cross += dot3(bt, t)
        tgram += dot3(tt, t)
        bgram += dot3(bt, b)
    row, col = iota((n, n), 0), iota((n, n), 1)
    packed = jnp.where(row < col, tgram, bgram)
    diag = row == col
    tdiag = jnp.sum(jnp.where(diag, tgram, 0.0), axis=0, keepdims=True)
    bdiag = jnp.sum(jnp.where(diag, bgram, 0.0), axis=0, keepdims=True)
    for c in range(2):
        half = slice(c * 128, (c + 1) * 128)
        pay[c * n : (c + 1) * n, :] = cross[:, half]
        pay[(2 + c) * n : (3 + c) * n, :] = packed[:, half]
    pay[4 * n :, :] = jnp.zeros((pay.shape[0] - 4 * n, 128), F32)
    for c in range(2):
        half = slice(c * 128, (c + 1) * 128)
        pay[4 * n + c : 4 * n + c + 1, :] = tdiag[:, half]
        pay[4 * n + 2 + c : 4 * n + 3 + c, :] = bdiag[:, half]
    half, core = keep_ref.shape[0], where_ref[0]
    keep_ref[...] = pay[pl.ds(pl.multiple_of(core * half, 8), half), :]
    send_ref[...] = pay[pl.ds(pl.multiple_of((1 - core) * half, 8), half), :]


def invert_blocks(v):
    group = iota((8, 128), 1) // NODES
    node = iota((8, 128), 1) % NODES
    row = iota((8, 128), 0)
    for g in range(4):
        q, first = g // 2, g % 2 * 8
        pan = []
        for p in range(8):
            index = node + (first + p) * NODES
            pan.append([jnp.take_along_axis(x, index, axis=1) for x in v[q]])
        for p in range(8):
            recip = 1.0 / pan[p][g][p : p + 1, :]
            new = [x for x in pan[p]]
            new[g] = jnp.where(row == p, 1.0, new[g])
            new = [x * recip for x in new]
            pan[p] = new
            for o in range(8):
                if o != p:
                    factor = pan[o][g][p : p + 1, :]
                    old = [x for x in pan[o]]
                    old[g] = jnp.where(row == p, 0.0, old[g])
                    pan[o] = [x - factor * y for x, y in zip(old, new)]
        for o in range(2):
            acc = [x for x in v[o]]
            acc[g] = jnp.zeros((8, 128), F32)
            for p in range(8):
                factor = v[o][g][p : p + 1, :]
                acc = [x - factor * y for x, y in zip(acc, pan[p])]
            if o == q:
                for p in range(8):
                    acc = [jnp.where(group == first + p, y, x) for x, y in zip(acc, pan[p])]
            v[o] = acc
    return v


def resolvent_kernel(
    where_ref, shift_ref, weight_ref, mine_ref, other_ref, out_ref, cross_ref, mats, turned, inverses, news, pay
):
    n = out_ref.shape[1]
    half, core = mine_ref.shape[0], where_ref[0]
    pay[pl.ds(pl.multiple_of(core * half, 8), half), :] = mine_ref[...]
    pay[pl.ds(pl.multiple_of((1 - core) * half, 8), half), :] = other_ref[...]
    row, col = iota((n, n), 0), iota((n, n), 1)

    def wide(start, rows):
        return jnp.concatenate([pay[start : start + rows, :], pay[start + rows : start + 2 * rows, :]], 1)

    cross, packed = wide(0, n), wide(2 * n, n)
    cross_ref[...] = cross
    tdiag, bdiag = wide(4 * n, 1), wide(4 * n + 2, 1)
    upper = jnp.where(row < col, packed, 0.0)
    lower = jnp.where(row > col, packed, 0.0)
    tgram = upper + upper.T + jnp.where(row == col, tdiag, 0.0)
    bgram = lower + lower.T + jnp.where(row == col, bdiag, 0.0)
    crosst = cross.T
    left, right = halves(crosst), halves(cross)
    square = dot3(left, right)
    normal = tgram - 2.0 * square + dot3(left, halves(dot3(halves(bgram), right)))
    for m in range(NODES):
        shifted = square + shift_ref[core * NODES + m] * normal
        mats[0, m * n : (m + 1) * n, :] = shifted[:, 0:128]
        mats[1, m * n : (m + 1) * n, :] = shifted[:, 128:256]

    def stack(x):
        h, m, l = split(x)
        return jnp.concatenate([h, m, h, l, h, m, l, m], 0).astype(BF16)

    def step(tile, part, carry):
        inner = pl.multiple_of(part * STEP, STEP)
        start = pl.multiple_of(tile * 128 + inner, STEP)
        v = []
        for q in range(2):
            rows = [mats[tile, pl.ds(start + 16 * q + i, NODES, stride=n), :] for i in range(16)]
            turned[q] = jnp.concatenate(rows, 0).T
            block = turned[q, pl.ds(inner, STEP), :]
            v.append([block[8 * g : 8 * g + 8] for g in range(4)])
        v = invert_blocks(v)
        for q in range(2):
            h, m, l = split(jnp.concatenate(v[q], 0))
            inverses[0, q * 128 : (q + 1) * 128, :] = jnp.concatenate([h, h, m, h], 0).T
            inverses[1, q * 128 : (q + 1) * 128, :] = jnp.concatenate([l, m, m, l], 0).T

        group = iota((n, 128), 1) // STEP
        index = iota((n, 128), 1) % STEP + inner
        local = iota((STEP, n), 1) - start
        inblock = (local >= 0) & (local < STEP)
        minus = jnp.where(local == iota((STEP, n), 0), -1.0, 0.0)
        for m in range(NODES):
            left = [inverses[c, pl.ds(m, STEP, stride=NODES), :] for c in range(2)]
            left = jnp.concatenate(left, 1).astype(BF16)
            here = pl.ds(pl.multiple_of(m * n + start, STEP), STEP)
            panel = jnp.concatenate([mats[0, here, :], mats[1, here, :]], 1)
            panel = jnp.where(inblock, minus, panel)
            news[m] = jnp.dot(left, stack(panel), preferred_element_type=F32)
        for m in range(NODES):
            rows = slice(m * n, (m + 1) * n)
            columns = jnp.take_along_axis(mats[tile, rows, :], index, axis=1)
            h, d, l = split(columns)
            one = jnp.where(group == 2, d, h)
            two = jnp.where((group == 0) | (group == 3), l, d)
            lhs = jnp.concatenate([one, two], 1).astype(BF16)
            change = jnp.dot(lhs, stack(news[m]), preferred_element_type=F32)
            for c in range(2):
                half = slice(c * 128, (c + 1) * 128)
                old = mats[c, rows, :]
                if c == tile:
                    old = jnp.where(inblock[0:1, half], 0.0, old)
                mats[c, rows, :] = old - change[:, half]
        for m in range(NODES):
            here = pl.ds(pl.multiple_of(m * n + start, STEP), STEP)
            mats[0, here, :] = news[m, :, 0:128]
            mats[1, here, :] = news[m, :, 128:256]
        return carry

    for tile in range(2):
        lax.fori_loop(0, 4, functools.partial(step, tile), 0)
    for c in range(2):
        half = weight_ref[core * NODES] * mats[c, 0:n, :]
        for m in range(1, NODES):
            half = half + weight_ref[core * NODES + m] * mats[c, m * n : (m + 1) * n, :]
        out_ref[:, c * 128 : (c + 1) * 128] = half


def residual_kernel(cross_ref, b_ref, t_ref, high_ref, low_ref):
    z = t_ref[...] - dot3(halves(b_ref[...]), halves(cross_ref[...]))
    high_ref[...], low_ref[...] = halves(z)


def lift_kernel(scale, mine_ref, other_ref, cross_ref, high_ref, low_ref, out_hbm, out_ref, sems):
    rows = high_ref.shape[0] // CHUNKS
    total = (mine_ref[...] + other_ref[...]) * -scale
    right = halves(dot3(halves(total), halves(cross_ref[...].T)))
    copies = []
    for c in range(CHUNKS):
        part = pl.ds(c * rows, rows)
        out_ref[part, :] = dot3((high_ref[part, :], low_ref[part, :]), right)
        copies.append(pltpu.make_async_copy(out_ref.at[part], out_hbm.at[part], sems.at[c]))
        copies[-1].start()
    for copy in copies:
        copy.wait()


def swap_cores(x):
    return lax.ppermute(x, "gz", [(0, 1), (1, 0)])


def swap_bits(x, mesh, gx, gy):
    ny, nz = mesh.shape["gy"], mesh.shape["gz"]
    perm = []
    for i in range(mesh.size):
        x0, y0, z0 = i // (ny * nz), i // nz % ny, i % nz
        perm.append((i, ((x0 ^ gx) * ny + (y0 ^ gy)) * nz + z0))
    return lax.ppermute(x, ("gx", "gy", "gz"), perm)


def summed(x, mesh):
    nx, ny = mesh.shape["gx"], mesh.shape["gy"]
    low = [(a, b) for a in range(4) for b in range(2)]
    groups = [
        [(gx + a) * ny + gy + b for a, b in low] for gx in range(0, nx, 4) for gy in range(0, ny, 2)
    ]

    def cube(pieces):
        return lax.all_to_all(
            pieces, ("gx", "gy"), 0, 0, axis_index_groups=groups, tiled=True
        )

    x = jnp.sum(cube(x).reshape(CUBE, -1, x.shape[1]), axis=0)
    for bit in range(2, (nx - 1).bit_length()):
        x = x + swap_bits(x, mesh, 1 << bit, 0)
    for bit in range(1, (ny - 1).bit_length()):
        x = x + swap_bits(x, mesh, 0, 1 << bit)
    return cube(jnp.tile(x, (CUBE, 1)))


def on_device(basis, target, mesh):
    rows, n = basis.shape
    total_rows = rows * mesh.size
    pay_half = -(-(2 * n + 8) // (8 * CUBE)) * 8 * CUBE
    vmem = pl.BlockSpec(memory_space=pltpu.VMEM)
    smem = pl.BlockSpec(memory_space=pltpu.SMEM)
    hbm = pl.BlockSpec(memory_space=pltpu.HBM)
    limit = pltpu.CompilerParams(vmem_limit_bytes=48 * 1024 * 1024)
    core = lax.axis_index("gz")
    where = jnp.reshape(core, (1,)).astype(jnp.int32)
    half = jax.ShapeDtypeStruct((pay_half, 128), F32)
    keep, send = pl.pallas_call(
        gram_kernel,
        out_shape=(half, half),
        in_specs=[smem, hbm, hbm],
        out_specs=(vmem, vmem),
        scratch_shapes=[
            pltpu.VMEM((rows, n), F32),
            pltpu.VMEM((rows, n), F32),
            pltpu.VMEM((2 * pay_half, 128), F32),
            pltpu.SemaphoreType.DMA((2, CHUNKS)),
        ],
        compiler_params=pltpu.CompilerParams(vmem_limit_bytes=GRANT),
    )(where, basis, target)
    mine = summed(keep + swap_cores(send), mesh)
    other = swap_cores(mine)
    square = jax.ShapeDtypeStruct((n, n), F32)
    part, cross = pl.pallas_call(
        resolvent_kernel,
        out_shape=(square, square),
        in_specs=[smem, smem, smem, vmem, vmem],
        out_specs=(vmem, vmem),
        scratch_shapes=[
            pltpu.VMEM((2, NODES * n, 128), F32),
            pltpu.VMEM((2, 128, 128), F32),
            pltpu.VMEM((2, 2 * 128, 128), F32),
            pltpu.VMEM((NODES, STEP, n), F32),
            pltpu.VMEM((2 * pay_half, 128), F32),
        ],
        compiler_params=limit,
        cost_estimate=pl.CostEstimate(flops=10**11, bytes_accessed=10**6, transcendentals=0),
    )(where, jnp.asarray(points**2, F32), jnp.asarray(weights, F32), mine, other)
    other = swap_cores(part)
    high, low = pl.pallas_call(
        residual_kernel,
        out_shape=(jax.ShapeDtypeStruct((rows, n), BF16),) * 2,
        in_specs=[vmem, vmem, vmem],
        out_specs=(vmem, vmem),
        compiler_params=limit,
        cost_estimate=pl.CostEstimate(flops=10**9, bytes_accessed=3 * 10**6, transcendentals=0),
    )(cross, basis, target)
    return pl.pallas_call(
        functools.partial(lift_kernel, float(np.sqrt(total_rows))),
        out_shape=jax.ShapeDtypeStruct((rows, n), F32),
        in_specs=[vmem] * 5,
        out_specs=hbm,
        scratch_shapes=[pltpu.VMEM((rows, n), F32), pltpu.SemaphoreType.DMA((CHUNKS,))],
        compiler_params=limit,
    )(part, other, cross, high, low)


def solution(mesh):
    return jax.shard_map(
        functools.partial(on_device, mesh=mesh),
        mesh=mesh,
        in_specs=(P(("gx", "gy", "gz"), None), P(("gx", "gy", "gz"), None)),
        out_specs=P(("gx", "gy", "gz"), None),
        check_vma=False,
    )
```

```python
import functools

import jax
import jax.numpy as jnp
import numpy as np
from jax import lax
from jax.experimental import pallas as pl
from jax.experimental.pallas import tpu as pltpu
from jax.sharding import PartitionSpec as P

half_points = [
    0.0950125098376374,
    0.2816035507792589,
    0.4580167776572274,
    0.6178762444026438,
    0.755404408355003,
    0.8656312023878318,
    0.9445750230732326,
    0.9894009349916499,
]
half_weights = [
    0.1894506104550685,
    0.1826034150449236,
    0.1691565193950025,
    0.1495959888165767,
    0.1246289712555339,
    0.0951585116824928,
    0.0622535239386479,
    0.0271524594117541,
]
points = (np.array([-v for v in half_points[::-1]] + half_points) + 1.0) / 2.0
weights = np.array(half_weights[::-1] + half_weights) / 2.0
NODES = 8
CHUNKS = 4
CUBE = 8
GRANT = 53 * 1024 * 1024
STEP = 32
F32 = jnp.float32
BF16 = jnp.bfloat16
highest = lax.Precision.HIGHEST


def iota(shape, dim):
    return lax.broadcasted_iota(jnp.int32, shape, dim)


def split(x):
    high = x.astype(BF16).astype(F32)
    rest = x - high
    mid = rest.astype(BF16).astype(F32)
    return high, mid, rest - mid


def dot(a, b):
    return jnp.dot(a, b, precision=highest, preferred_element_type=F32)


def halves(x):
    high = x.astype(BF16)
    return high, (x - high.astype(F32)).astype(BF16)


def dot3(a, b):
    (ah, al), (bh, bl) = a, b
    total = jnp.dot(ah, bl, preferred_element_type=F32) + jnp.dot(al, bh, preferred_element_type=F32)
    return total + jnp.dot(ah, bh, preferred_element_type=F32)


def gram_kernel(where_ref, b_hbm, t_hbm, keep_ref, send_ref, b_ref, t_ref, pay, sems):
    rows, n = b_ref.shape
    chunk = rows // CHUNKS
    copies = []
    for c in range(CHUNKS):
        part = pl.ds(c * chunk, chunk)
        for k, (source, dest) in enumerate(((b_hbm, b_ref), (t_hbm, t_ref))):
            copy = pltpu.make_async_copy(source.at[part], dest.at[part], sems.at[k, c])
            copy.start()
            copies.append(copy)
    cross = tgram = bgram = jnp.zeros((n, n), F32)
    for c in range(CHUNKS):
        part = slice(c * chunk, (c + 1) * chunk)
        copies[2 * c].wait()
        copies[2 * c + 1].wait()
        b, t = b_ref[part, :], t_ref[part, :]
        b, bt, t, tt = halves(b), halves(b.T), halves(t), halves(t.T)
        cross += dot3(bt, t)
        tgram += dot3(tt, t)
        bgram += dot3(bt, b)
    row, col = iota((n, n), 0), iota((n, n), 1)
    packed = jnp.where(row < col, tgram, bgram)
    diag = row == col
    tdiag = jnp.sum(jnp.where(diag, tgram, 0.0), axis=0, keepdims=True)
    bdiag = jnp.sum(jnp.where(diag, bgram, 0.0), axis=0, keepdims=True)
    for c in range(2):
        half = slice(c * 128, (c + 1) * 128)
        pay[c * n : (c + 1) * n, :] = cross[:, half]
        pay[(2 + c) * n : (3 + c) * n, :] = packed[:, half]
    pay[4 * n :, :] = jnp.zeros((pay.shape[0] - 4 * n, 128), F32)
    for c in range(2):
        half = slice(c * 128, (c + 1) * 128)
        pay[4 * n + c : 4 * n + c + 1, :] = tdiag[:, half]
        pay[4 * n + 2 + c : 4 * n + 3 + c, :] = bdiag[:, half]
    half, core = keep_ref.shape[0], where_ref[0]
    keep_ref[...] = pay[pl.ds(pl.multiple_of(core * half, 8), half), :]
    send_ref[...] = pay[pl.ds(pl.multiple_of((1 - core) * half, 8), half), :]


def invert_blocks(v):
    group = iota((8, 128), 1) // NODES
    node = iota((8, 128), 1) % NODES
    row = iota((8, 128), 0)
    for g in range(4):
        q, first = g // 2, g % 2 * 8
        pan = []
        for p in range(8):
            index = node + (first + p) * NODES
            pan.append([jnp.take_along_axis(x, index, axis=1) for x in v[q]])
        for p in range(8):
            recip = 1.0 / pan[p][g][p : p + 1, :]
            new = [x for x in pan[p]]
            new[g] = jnp.where(row == p, 1.0, new[g])
            new = [x * recip for x in new]
            pan[p] = new
            for o in range(8):
                if o != p:
                    factor = pan[o][g][p : p + 1, :]
                    old = [x for x in pan[o]]
                    old[g] = jnp.where(row == p, 0.0, old[g])
                    pan[o] = [x - factor * y for x, y in zip(old, new)]
        for o in range(2):
            acc = [x for x in v[o]]
            acc[g] = jnp.zeros((8, 128), F32)
            for p in range(8):
                factor = v[o][g][p : p + 1, :]
                acc = [x - factor * y for x, y in zip(acc, pan[p])]
            if o == q:
                for p in range(8):
                    acc = [jnp.where(group == first + p, y, x) for x, y in zip(acc, pan[p])]
            v[o] = acc
    return v


def resolvent_kernel(
    where_ref, shift_ref, weight_ref, mine_ref, other_ref, out_ref, cross_ref, mats, turned, inverses, news, stacks, pay
):
    n = out_ref.shape[1]
    half, core = mine_ref.shape[0], where_ref[0]
    pay[pl.ds(pl.multiple_of(core * half, 8), half), :] = mine_ref[...]
    pay[pl.ds(pl.multiple_of((1 - core) * half, 8), half), :] = other_ref[...]
    row, col = iota((n, n), 0), iota((n, n), 1)

    def wide(start, rows):
        return jnp.concatenate([pay[start : start + rows, :], pay[start + rows : start + 2 * rows, :]], 1)

    cross, packed = wide(0, n), wide(2 * n, n)
    cross_ref[...] = cross
    tdiag, bdiag = wide(4 * n, 1), wide(4 * n + 2, 1)
    upper = jnp.where(row < col, packed, 0.0)
    lower = jnp.where(row > col, packed, 0.0)
    tgram = upper + upper.T + jnp.where(row == col, tdiag, 0.0)
    bgram = lower + lower.T + jnp.where(row == col, bdiag, 0.0)
    crosst = cross.T
    left, right = halves(crosst), halves(cross)
    square = dot3(left, right)
    normal = tgram - 2.0 * square + dot3(left, halves(dot3(halves(bgram), right)))
    for m in range(NODES):
        shifted = square + shift_ref[core * NODES + m] * normal
        mats[0, m * n : (m + 1) * n, :] = shifted[:, 0:128]
        mats[1, m * n : (m + 1) * n, :] = shifted[:, 128:256]

    def stack(x):
        h, m, l = split(x)
        return jnp.concatenate([h, m, h, l, h, m, l, m], 0).astype(BF16)

    def step(tile, part, carry):
        inner = pl.multiple_of(part * STEP, STEP)
        start = pl.multiple_of(tile * 128 + inner, STEP)
        v = []
        for q in range(2):
            rows = [mats[tile, pl.ds(start + 16 * q + i, NODES, stride=n), :] for i in range(16)]
            turned[q] = jnp.concatenate(rows, 0).T
            block = turned[q, pl.ds(inner, STEP), :]
            v.append([block[8 * g : 8 * g + 8] for g in range(4)])
        v = invert_blocks(v)
        for q in range(2):
            h, m, l = split(jnp.concatenate(v[q], 0))
            inverses[0, q * 128 : (q + 1) * 128, :] = jnp.concatenate([h, h, m, h], 0).T
            inverses[1, q * 128 : (q + 1) * 128, :] = jnp.concatenate([l, m, m, l], 0).T

        group = iota((n, 128), 1) // STEP
        index = iota((n, 128), 1) % STEP + inner
        local = iota((STEP, n), 1) - start
        inblock = (local >= 0) & (local < STEP)
        minus = jnp.where(local == iota((STEP, n), 0), -1.0, 0.0)
        for m in range(NODES):
            left = [inverses[c, pl.ds(m, STEP, stride=NODES), :] for c in range(2)]
            left = jnp.concatenate(left, 1).astype(BF16)
            here = pl.ds(pl.multiple_of(m * n + start, STEP), STEP)
            panel = jnp.concatenate([mats[0, here, :], mats[1, here, :]], 1)
            panel = jnp.where(inblock, minus, panel)
            new = jnp.dot(left, stack(panel), preferred_element_type=F32)
            news[m] = new
            stacks[m] = stack(new)
        for m in range(NODES):
            rows = slice(m * n, (m + 1) * n)
            columns = jnp.take_along_axis(mats[tile, rows, :], index, axis=1)
            h, d, l = split(columns)
            one = jnp.where(group == 2, d, h)
            two = jnp.where((group == 0) | (group == 3), l, d)
            lhs = jnp.concatenate([one, two], 1).astype(BF16)
            change = jnp.dot(lhs, stacks[m], preferred_element_type=F32)
            for c in range(2):
                half = slice(c * 128, (c + 1) * 128)
                old = mats[c, rows, :]
                if c == tile:
                    old = jnp.where(inblock[0:1, half], 0.0, old)
                mats[c, rows, :] = old - change[:, half]
        for m in range(NODES):
            here = pl.ds(pl.multiple_of(m * n + start, STEP), STEP)
            mats[0, here, :] = news[m, :, 0:128]
            mats[1, here, :] = news[m, :, 128:256]
        return carry

    for tile in range(2):
        lax.fori_loop(0, 4, functools.partial(step, tile), 0)
    for c in range(2):
        half = weight_ref[core * NODES] * mats[c, 0:n, :]
        for m in range(1, NODES):
            half = half + weight_ref[core * NODES + m] * mats[c, m * n : (m + 1) * n, :]
        out_ref[:, c * 128 : (c + 1) * 128] = half


def residual_kernel(cross_ref, b_ref, t_ref, high_ref, low_ref):
    z = t_ref[...] - dot3(halves(b_ref[...]), halves(cross_ref[...]))
    high_ref[...], low_ref[...] = halves(z)


def lift_kernel(scale, mine_ref, other_ref, cross_ref, high_ref, low_ref, out_hbm, out_ref, sems):
    rows = high_ref.shape[0] // CHUNKS
    total = (mine_ref[...] + other_ref[...]) * -scale
    right = halves(dot3(halves(total), halves(cross_ref[...].T)))
    copies = []
    for c in range(CHUNKS):
        part = pl.ds(c * rows, rows)
        out_ref[part, :] = dot3((high_ref[part, :], low_ref[part, :]), right)
        copies.append(pltpu.make_async_copy(out_ref.at[part], out_hbm.at[part], sems.at[c]))
        copies[-1].start()
    for copy in copies:
        copy.wait()


def swap_cores(x):
    return lax.ppermute(x, "gz", [(0, 1), (1, 0)])


def swap_bits(x, mesh, gx, gy):
    ny, nz = mesh.shape["gy"], mesh.shape["gz"]
    perm = []
    for i in range(mesh.size):
        x0, y0, z0 = i // (ny * nz), i // nz % ny, i % nz
        perm.append((i, ((x0 ^ gx) * ny + (y0 ^ gy)) * nz + z0))
    return lax.ppermute(x, ("gx", "gy", "gz"), perm)


def summed(x, mesh):
    nx, ny = mesh.shape["gx"], mesh.shape["gy"]
    low = [(a, b) for a in range(4) for b in range(2)]
    groups = [
        [(gx + a) * ny + gy + b for a, b in low] for gx in range(0, nx, 4) for gy in range(0, ny, 2)
    ]

    def cube(pieces):
        return lax.all_to_all(
            pieces, ("gx", "gy"), 0, 0, axis_index_groups=groups, tiled=True
        )

    x = jnp.sum(cube(x).reshape(CUBE, -1, x.shape[1]), axis=0)
    for bit in range(2, (nx - 1).bit_length()):
        x = x + swap_bits(x, mesh, 1 << bit, 0)
    for bit in range(1, (ny - 1).bit_length()):
        x = x + swap_bits(x, mesh, 0, 1 << bit)
    return cube(jnp.tile(x, (CUBE, 1)))


def on_device(basis, target, mesh):
    rows, n = basis.shape
    total_rows = rows * mesh.size
    pay_half = -(-(2 * n + 8) // (8 * CUBE)) * 8 * CUBE
    vmem = pl.BlockSpec(memory_space=pltpu.VMEM)
    smem = pl.BlockSpec(memory_space=pltpu.SMEM)
    hbm = pl.BlockSpec(memory_space=pltpu.HBM)
    limit = pltpu.CompilerParams(vmem_limit_bytes=48 * 1024 * 1024)
    core = lax.axis_index("gz")
    where = jnp.reshape(core, (1,)).astype(jnp.int32)
    half = jax.ShapeDtypeStruct((pay_half, 128), F32)
    keep, send = pl.pallas_call(
        gram_kernel,
        out_shape=(half, half),
        in_specs=[smem, hbm, hbm],
        out_specs=(vmem, vmem),
        scratch_shapes=[
            pltpu.VMEM((rows, n), F32),
            pltpu.VMEM((rows, n), F32),
            pltpu.VMEM((2 * pay_half, 128), F32),
            pltpu.SemaphoreType.DMA((2, CHUNKS)),
        ],
        compiler_params=pltpu.CompilerParams(vmem_limit_bytes=GRANT),
    )(where, basis, target)
    mine = summed(keep + swap_cores(send), mesh)
    other = swap_cores(mine)
    square = jax.ShapeDtypeStruct((n, n), F32)
    part, cross = pl.pallas_call(
        resolvent_kernel,
        out_shape=(square, square),
        in_specs=[smem, smem, smem, vmem, vmem],
        out_specs=(vmem, vmem),
        scratch_shapes=[
            pltpu.VMEM((2, NODES * n, 128), F32),
            pltpu.VMEM((2, 128, 128), F32),
            pltpu.VMEM((2, 2 * 128, 128), F32),
            pltpu.VMEM((NODES, STEP, n), F32),
            pltpu.VMEM((NODES, 8 * STEP, n), BF16),
            pltpu.VMEM((2 * pay_half, 128), F32),
        ],
        compiler_params=limit,
        cost_estimate=pl.CostEstimate(flops=10**11, bytes_accessed=10**6, transcendentals=0),
    )(where, jnp.asarray(points**2, F32), jnp.asarray(weights, F32), mine, other)
    other = swap_cores(part)
    high, low = pl.pallas_call(
        residual_kernel,
        out_shape=(jax.ShapeDtypeStruct((rows, n), BF16),) * 2,
        in_specs=[vmem, vmem, vmem],
        out_specs=(vmem, vmem),
        compiler_params=limit,
        cost_estimate=pl.CostEstimate(flops=10**9, bytes_accessed=3 * 10**6, transcendentals=0),
    )(cross, basis, target)
    return pl.pallas_call(
        functools.partial(lift_kernel, float(np.sqrt(total_rows))),
        out_shape=jax.ShapeDtypeStruct((rows, n), F32),
        in_specs=[vmem] * 5,
        out_specs=hbm,
        scratch_shapes=[pltpu.VMEM((rows, n), F32), pltpu.SemaphoreType.DMA((CHUNKS,))],
        compiler_params=limit,
    )(part, other, cross, high, low)


def solution(mesh):
    return jax.shard_map(
        functools.partial(on_device, mesh=mesh),
        mesh=mesh,
        in_specs=(P(("gx", "gy", "gz"), None), P(("gx", "gy", "gz"), None)),
        out_specs=P(("gx", "gy", "gz"), None),
        check_vma=False,
    )
```
